32 devices in a mesh: dp: 8 (over z, y), tensor: 4 (over x, core).
Axes of the slice: x: 2, y: 2, z: 4, core: 2. Of those that a mesh axis runs over, the one named last changes fastest.
Arguments:
- tokens: bfloat16 [8192, 768], P(('dp', 'tensor')), may hold values from -6 to 6
- gain_one: float32 [768], replicated, may hold values from 0.25 to 1.75
- w_qkv: bfloat16 [3, 768, 768], P(None, 'dp', 'tensor'), may hold values from -0.21875 to 0.21875
- rel_table: float32 [12, 32], replicated, may hold values from -4 to 4
- w_mix: bfloat16 [768, 768], P('tensor', 'dp'), may hold values from -1.75 to 1.75
- gain_two: float32 [768], replicated, may hold values from 0.25 to 1.75
- w_router: bfloat16 [768, 64], replicated, may hold values from -0.15625 to 0.15625
- w_in: bfloat16 [64, 768, 3072], P('dp', None, 'tensor'), may hold values from -0.21875 to 0.21875
- w_out: bfloat16 [64, 3072, 768], P('dp', 'tensor'), may hold values from -0.109375 to 0.109375
- routes: int32 [8192, 2], P('dp'), may hold values from 0 to 63, as said below
- buffer_row_index: int32 [8192, 2], P('dp'), may hold values from 0 to 39, as said below
- image_starts: int32 [8, 2], P('dp'), may hold values from 0 to 768, as said below
- d_output: bfloat16 [8192, 768], P(('dp', 'tensor')), may hold values from -6 to 6
Outputs:
- output: bfloat16 [8192, 768], P(('dp', 'tensor'))
- grad_input: float32 [8192, 768], P(('dp', 'tensor'))
- grad_gain_one: float32 [768], replicated
- grad_qkv: float32 [3, 768, 768], P(None, 'dp', 'tensor')
- grad_table: float32 [12, 32], replicated
- grad_mix: float32 [768, 768], P('tensor', 'dp')
- grad_gain_two: float32 [768], replicated
- grad_router: float32 [768, 64], replicated
- grad_in: float32 [64, 768, 3072], P('dp', None, 'tensor')
- grad_out: float32 [64, 3072, 768], P('dp', 'tensor')
The draws below stay inside these ranges and needn't reach their ends.
Inputs may be any that keep to these rules, and one draw needn't show every extreme that they name: `routes`: A token's two experts differ. Among the 1024 tokens of one sequence each expert is named at most 40 times, and one expert, drawn from the seed, is named exactly 40 times in every sequence. Among the tokens of one sequence, the pairs (routes, buffer_row_index) of all choices are distinct. `image_starts`: row s belongs to sequence s; its starts rise, and its pieces of 256 tokens do not intersect and do not leave the sequence. Some sequence has a piece starting at 0 and some sequence has one ending at its last position.
All inputs are finite; a program needn't handle non-finite values.
Results may differ from the reference program's by a relative error of at most 0.015.
Values may be sent and summed in bfloat16 or wider, within the bound.
No kernel may reach another device: no remote copies, remote signals or barrier semaphores. Data moves between devices by JAX's collectives and lax.ppermute only.
A program may use at most 256 MiB of HBM per device.

```python
import math
import jax
import jax.numpy as jnp
from jax import lax

D = 768
HEADS = 12
HEAD_DIM = 64
FF = 3072
EXPERTS = 64
TOK_DP = 1024
SPAN = 256
IMAGES = 2
BUCKETS = 32
CAP = 40
TOKENS = 8192
N_DP = 8


def assignment_pairs(key):
    blocks = TOKENS // TOK_DP
    slot_count = EXPERTS * CAP
    full_key, rest_key = jax.random.split(jax.random.fold_in(key, 17))
    full_expert = jax.random.randint(full_key, (), 0, EXPERTS)

    def one_block(block_key):
        rank_key, flip_key, order_key = jax.random.split(block_key, 3)
        indices = jnp.arange(slot_count, dtype=jnp.int32)
        rank_values = jax.random.permutation(rank_key, slot_count).astype(jnp.int32)
        attention_scores = jnp.where(indices // CAP == full_expert, indices - slot_count, rank_values)
        picked = jnp.sort(jnp.argsort(attention_scores, stable=True)[:2 * TOK_DP].astype(jnp.int32))
        first_half = picked[:TOK_DP]
        second = picked[TOK_DP:]
        flipped = jax.random.randint(flip_key, (TOK_DP,), 0, 2) == 1
        paired = jnp.stack([jnp.where(flipped, second, first_half), jnp.where(flipped, first_half, second)], axis=1)
        return paired[jax.random.permutation(order_key, TOK_DP)]
    return jax.vmap(one_block)(jax.random.split(rest_key, blocks)).reshape(TOKENS, 2)


def draw_routes(key, part):
    return (assignment_pairs(key) // CAP).astype(jnp.int32)


def draw_buffer_row_index(key, part):
    return (assignment_pairs(key) % CAP).astype(jnp.int32)


def draw_image_starts(key, part):
    key = jax.random.fold_in(key, 5)
    offset_key, first_key, last_key = jax.random.split(key, 3)
    sequences = TOKENS // TOK_DP
    region = TOK_DP // IMAGES
    offsets = jax.random.randint(offset_key, (sequences, IMAGES), 0, region - SPAN + 1)
    starts = jnp.arange(IMAGES, dtype=jnp.int32)[None, :] * region + offsets
    row_ids = jnp.arange(sequences, dtype=jnp.int32)
    first_row = jax.random.randint(first_key, (), 0, sequences)
    last_row = jax.random.randint(last_key, (), 0, sequences)
    first_column = jnp.where(row_ids == first_row, 0, starts[:, 0])
    starts = starts.at[:, 0].set(first_column)
    last_column = jnp.where(row_ids == last_row, IMAGES * region - SPAN, starts[:, IMAGES - 1])
    starts = starts.at[:, IMAGES - 1].set(last_column)
    return starts.astype(jnp.int32)


def raised(entries, stream_key, source, target, parts, factor):
    def block_of(dim):
        return (jnp.arange(entries.shape[dim]) // (entries.shape[dim] // parts)).reshape((-1,) + (1,) * (entries.ndim - 1 - dim))

    first = jax.random.permutation(stream_key, parts)[block_of(target)]
    far = (block_of(target) + parts // 2) % parts
    return jnp.where((block_of(source) == first) | (block_of(source) == far), factor * entries, entries)


def block_levels(own_key, dims, cuts, low, high):
    level = 1.0
    for dim, shards_of in cuts:
        steps = jax.random.uniform(jax.random.fold_in(jax.random.fold_in(own_key, 6), dim), (shards_of,), jnp.float32, low / len(cuts), high / len(cuts))
        level = level * jnp.repeat(jnp.exp(steps), dims[dim] // shards_of).reshape((-1,) + (1,) * (len(dims) - 1 - dim))
    return level


def noise(stream_key, shape, deviation, reach, cuts=(), kind=jnp.bfloat16):
    values = jax.random.normal(stream_key, shape, jnp.float32) * deviation
    if len(cuts) > 0:
        values = block_levels(stream_key, shape, cuts, -0.22, 0.18) * values
    return jnp.clip(values, min=-reach, max=reach).astype(kind)


def heavy_noise(rng, shape, scale, reach, shards, heavy, held_as=jnp.bfloat16):
    array = scale * jax.random.normal(rng, shape, jnp.float32)
    if shards:
        array = array * block_levels(rng, shape, shards, -0.22, 0.18)
    return jnp.clip(raised(array, jax.random.fold_in(rng, 3), *heavy), -reach, reach).astype(held_as)


def setup_inputs(seed: int = 0) -> dict:
    key_list = jax.random.split(jax.random.key(seed), 14)
    return {
        "tokens": noise(key_list[0], (TOKENS, D), 1.0, 6.0, ((0, 32),)),
        "gain_one": jnp.clip(1.0 + 0.15 * jax.random.normal(key_list[1], (D,), jnp.float32), 0.25, 1.75),
        "w_qkv": noise(key_list[2], (3, D, D), D ** -0.5, 0.21875, ((1, 8), (2, 4))),
        "rel_table": noise(key_list[3], (HEADS, BUCKETS), 1.0, 4.0, (), jnp.float32),
        "w_mix": noise(key_list[4], (D, D), (D // 64) ** -0.5, 1.75, ((0, 4), (1, 8))),
        "gain_two": jnp.clip(1.0 + 0.15 * jax.random.normal(key_list[5], (D,), jnp.float32), 0.25, 1.75),
        "w_router": noise(key_list[6], (D, EXPERTS), (2 * D) ** -0.5, 0.15625),
        "w_in": noise(key_list[7], (EXPERTS, D, FF), D ** -0.5, 0.21875, ((0, 8), (2, 4))),
        "w_out": noise(key_list[8], (EXPERTS, FF, D), FF ** -0.5, 0.109375, ((0, 8), (1, 4))),
        "routes": draw_routes(jax.random.fold_in(key_list[13], 71), 0),
        "buffer_row_index": draw_buffer_row_index(jax.random.fold_in(key_list[13], 71), 0),
        "image_starts": draw_image_starts(jax.random.fold_in(key_list[13], 71), 0),
        "d_output": heavy_noise(key_list[12], (TOKENS, D), 1.0, 6.0, ((0, 32),), (0, 1, 32, 2.75)),
    }


bucket_edges = (1, 2, 3, 4, 5, 6, 7, 8, 11, 16, 23, 32, 45, 64, 91)
highest = lax.Precision.HIGHEST

@jax.custom_vjp
def low(v):
    return lax.optimization_barrier(v.astype(jnp.bfloat16)).astype(jnp.float32)

@jax.custom_vjp
def low_back(v):
    return v

def low_keep(v):
    return (low(v), None)

def low_pass(kept, grad):
    return (grad,)

def back_keep(v):
    return (v, None)

def back_low(kept, grad):
    return (low(grad),)
low.defvjp(low_keep, low_pass)
low_back.defvjp(back_keep, back_low)

def normalize(values, norm_gain):
    return values * lax.rsqrt(lax.optimization_barrier(jnp.mean(values * values, axis=-1, keepdims=True)) + 1e-06) * norm_gain

def bucket_table(offsets):
    magnitude = jnp.abs(offsets)
    levels = jnp.zeros(offsets.shape, jnp.int32)
    for threshold in bucket_edges:
        levels = levels + (magnitude >= threshold).astype(jnp.int32)
    return levels + (len(bucket_edges) + 1) * (offsets > 0).astype(jnp.int32)

def image_labels(starts, length):
    position = jnp.arange(length, dtype=jnp.int32)
    labels = jnp.full((length,), -1, jnp.int32)
    for image_index in range(starts.shape[0]):
        inside = (position >= starts[image_index]) & (position < starts[image_index] + SPAN)
        labels = jnp.where(inside, image_index, labels)
    return labels

def attend_sequence(queries, key_rows, value_rows, bias_table, labels):
    length = queries.shape[0]
    block_rows = math.gcd(length, 512)
    score_scale = HEAD_DIM ** (-0.5)
    columns = jnp.arange(length, dtype=jnp.int32)

    def one_block(query_block, first_row):
        rows_here = first_row + jnp.arange(block_rows, dtype=jnp.int32)
        attention_scores = jnp.einsum('qhd,khd->hqk', query_block, key_rows, precision=highest) * score_scale
        attention_scores = attention_scores + bias_table[:, bucket_table(columns[None, :] - rows_here[:, None])]
        attention_scores = low_back(attention_scores)
        row_labels = labels[rows_here]
        allowed = (columns[None, :] <= rows_here[:, None]) | (row_labels[:, None] == labels[None, :]) & (row_labels[:, None] >= 0)
        attention_scores = jnp.where(allowed[None], attention_scores, -1e+30)
        weights = jax.nn.softmax(attention_scores, axis=-1)
        return jnp.einsum('hqk,khd->qhd', low(weights), value_rows, precision=highest)

    def run_block(inputs_tuple):
        return jax.checkpoint(one_block)(inputs_tuple[0], inputs_tuple[1])
    blocks = queries.reshape(length // block_rows, block_rows, queries.shape[1], queries.shape[2])
    firsts = jnp.arange(length // block_rows, dtype=jnp.int32) * block_rows
    result = lax.map(run_block, (blocks, firsts))
    return result.reshape(queries.shape)

def reference(tokens, gain_one, w_qkv, rel_table, w_mix, gain_two, w_router, w_in, w_out, routes, buffer_row_index, image_starts, d_output):
    token_count = tokens.shape[0]
    sequences = token_count // TOK_DP
    group_of = jnp.arange(token_count, dtype=jnp.int32) // TOK_DP
    flat_rows = (routes * (N_DP * CAP) + group_of[:, None] * CAP + buffer_row_index).astype(jnp.int32)

    def labels_of(starts):
        return image_labels(starts, TOK_DP)
    labels = jax.vmap(labels_of)(image_starts)

    def forward(tokens_f, gain_a, qkv_f, table_f, mix_f, gain_b, router_f, in_f, out_f):
        normed = low(normalize(tokens_f, gain_a))
        projected = low(low_back(jnp.einsum('td,idc->itc', normed, qkv_f, precision=highest)))
        shaped = projected.reshape(3, sequences, TOK_DP, HEADS, HEAD_DIM)

        def per_sequence(inputs_tuple):
            return attend_sequence(inputs_tuple[0], inputs_tuple[1], inputs_tuple[2], table_f, inputs_tuple[3])
        attended = lax.map(jax.checkpoint(per_sequence), (shaped[0], shaped[1], shaped[2], labels))
        attended = low(low_back(attended.reshape(token_count, D)))
        mixed_rows = low_back(jnp.dot(attended, mix_f, precision=highest))
        hidden = tokens_f + mixed_rows
        normed_two = low(normalize(hidden, gain_b))
        router_scores = jnp.dot(normed_two, router_f, precision=highest)
        chosen = jnp.take_along_axis(router_scores, routes, axis=1)
        gate_values = jax.nn.softmax(chosen, axis=-1)
        buffers = jnp.zeros((EXPERTS * N_DP * CAP, D), jnp.float32).at[flat_rows.reshape(-1)].set(jnp.repeat(normed_two, 2, axis=0))

        def expert(inputs_tuple):
            rows_in, weight_in, weight_out = inputs_tuple
            pre_act = low_back(jnp.dot(rows_in, weight_in, precision=highest))
            activated = low(jax.nn.gelu(pre_act))
            return low_back(jnp.dot(activated, weight_out, precision=highest))
        expert_rows = lax.map(jax.checkpoint(expert), (buffers.reshape(EXPERTS, N_DP * CAP, D), in_f, out_f))
        picked = expert_rows.reshape(EXPERTS * N_DP * CAP, D)[flat_rows]
        moe_rows = low_back(lax.optimization_barrier(jnp.sum(gate_values[:, :, None] * picked, axis=1)))
        return hidden + moe_rows
    floats = (tokens.astype(jnp.float32), gain_one.astype(jnp.float32), w_qkv.astype(jnp.float32), rel_table.astype(jnp.float32), w_mix.astype(jnp.float32), gain_two.astype(jnp.float32), w_router.astype(jnp.float32), w_in.astype(jnp.float32), w_out.astype(jnp.float32))
    output, pullback = jax.vjp(forward, *floats)
    gradients = pullback(d_output.astype(jnp.float32))
    return (output.astype(jnp.bfloat16), gradients[0], gradients[1], gradients[2], gradients[3], gradients[4], gradients[5], gradients[6], gradients[7], gradients[8])
```

```python
import functools

import jax
import jax.numpy as jnp
import numpy as np
from jax import lax
from jax.experimental import pallas as pl
from jax.experimental.pallas import tpu as pltpu
from jax.sharding import PartitionSpec as P

HEAD_DIM = 64
EXPERTS = 64
SPAN = 256
CAP = 40
LOG2E = 1.4426950408889634
NEG = -1e30
bucket_edges = (1, 2, 3, 4, 5, 6, 7, 8, 11, 16, 23, 32, 45, 64, 91)
highest = lax.Precision.HIGHEST
f32 = jnp.float32
bf16 = jnp.bfloat16
i32 = jnp.int32
MIB = 1 << 20


def bucket_of(offsets):
    magnitude = np.abs(offsets)
    levels = np.zeros(offsets.shape, np.int32)
    for threshold in bucket_edges:
        levels = levels + (magnitude >= threshold).astype(np.int32)
    return levels + (len(bucket_edges) + 1) * (offsets > 0).astype(np.int32)


def nn(a, b):
    return jnp.dot(a, b, preferred_element_type=f32)


def nt(a, b):
    return lax.dot_general(a, b, (((1,), (1,)), ((), ())), preferred_element_type=f32)


def tn(a, b):
    return lax.dot_general(a, b, (((0,), (0,)), ((), ())), preferred_element_type=f32)


def split_two(v):
    hi = v.astype(bf16)
    return hi, (v - hi.astype(f32)).astype(bf16)


def swap_core(v):
    return lax.ppermute(v, "tensor", [(i, i ^ 1) for i in range(lax.axis_size("tensor"))])


def swap_x(v):
    return lax.ppermute(v, "tensor", [(i, i ^ 2) for i in range(lax.axis_size("tensor"))])


def exchange(v):
    return lax.all_to_all(v, "dp", 0, 0, tiled=True)


def gather_dp(v):
    groups = lax.axis_size("dp")
    return exchange(jnp.broadcast_to(v[None], (groups,) + v.shape))


def vmem():
    return pl.BlockSpec(memory_space=pltpu.VMEM)


def smem():
    return pl.BlockSpec(memory_space=pltpu.SMEM)


def sds(shape, dtype):
    return jax.ShapeDtypeStruct(shape, dtype)


def params(mib):
    return pltpu.CompilerParams(vmem_limit_bytes=mib * MIB)


def cost(flops, nbytes):
    return pl.CostEstimate(flops=int(flops), bytes_accessed=int(nbytes), transcendentals=0)


def row_to_column(row, n):
    a = lax.broadcasted_iota(i32, (n, n), 0)
    b = lax.broadcasted_iota(i32, (n, n), 1)
    return jnp.sum(jnp.where(a == b, row, 0.0), axis=1, keepdims=True)


def forward_kernel(
    sc, tok, gain, wq, wmt, bvec, normed, q, k, v, att, p_out, keep, send, toep, score, mask
):
    b = pl.program_id(0)
    length = tok.shape[0]
    block = att.shape[0]
    heads = q.shape[0]
    blocks = length // block

    @pl.when(b == 0)
    def _():
        for i in range(0, length, block):
            t = tok[i : i + block, :].astype(f32)
            n = t * lax.rsqrt(jnp.mean(t * t, axis=-1, keepdims=True) + 1e-06) * gain[...]
            n = n.astype(bf16)
            normed[i : i + block, :] = n
            pr = nn(n, wq[...]).astype(bf16)
            for h in range(heads):
                for j, ref in enumerate((q, k, v)):
                    at = (j * heads + h) * HEAD_DIM
                    ref[h, i : i + block, :] = pr[:, at : at + HEAD_DIM]
        for h in range(heads):
            row = jnp.broadcast_to(bvec[h : h + 1, :], (8, 2 * length))
            for a in range(0, block, 8):
                toep[h, a : a + 8, :] = pltpu.roll(row, a, 1, stride=1, stride_axis=0)

    s0, s1, c = sc[0], sc[1], sc[3]
    rc = 16

    def one_block(bs):
        r0 = bs * block
        kv = min(r0 + 2 * block, length)
        wide = kv - r0
        ii = r0 + lax.broadcasted_iota(i32, (block, wide), 0)
        jj = r0 + lax.broadcasted_iota(i32, (block, wide), 1)
        first = (ii >= s0) & (ii < s0 + SPAN) & (jj >= s0) & (jj < s0 + SPAN)
        second = (ii >= s1) & (ii < s1 + SPAN) & (jj >= s1) & (jj < s1 + SPAN)
        mask[:, :wide] = jnp.where((jj <= ii) | first | second, 0.0, NEG)
        for h in range(heads):
            score[:, :kv] = nt(q[h, r0 : r0 + block, :], k[h, :kv, :])

            def body(i, carry):
                rows = pl.ds(pl.multiple_of(i * rc, rc), rc)
                s = score[rows, :kv] * (HEAD_DIM ** (-0.5) * LOG2E)
                s = s + toep[h, rows, length - r0 : length - r0 + kv]
                right = s[:, r0:] + mask[rows, :wide]
                s = right if r0 == 0 else jnp.concatenate([s[:, :r0], right], axis=1)
                e = jnp.exp2(s - jnp.max(s, axis=1, keepdims=True))
                total = jnp.sum(e, axis=1, keepdims=True)
                p_out[h, rows, :kv] = (e * (1.0 / total)).astype(bf16)
                return carry

            lax.fori_loop(0, block // rc, body, 0)
            att[:, h * HEAD_DIM : (h + 1) * HEAD_DIM] = nn(p_out[h, :, :kv], v[h, :kv, :]).astype(
                bf16
            )
        mixed = nt(att[...], wmt[...])

        @pl.when(c == bs % 2)
        def _():
            keep[bs // 2] = mixed

        @pl.when(c != bs % 2)
        def _():
            send[bs // 2] = mixed.astype(bf16)

    for bs in range(blocks):
        pl.when(b == bs)(functools.partial(one_block, bs))


def attention_forward(sc, tok, gain, wq, wmt, bvec, heads):
    length, width = tok.shape
    block = length // 4
    whole = lambda *shape: pl.BlockSpec(shape, lambda b, s: (0,) * len(shape))
    qkv = (heads, length, HEAD_DIM)
    return pl.pallas_call(
        forward_kernel,
        grid_spec=pltpu.PrefetchScalarGridSpec(
            num_scalar_prefetch=1,
            grid=(4,),
            in_specs=[
                whole(length, width),
                whole(1, width),
                whole(*wq.shape),
                whole(*wmt.shape),
                whole(*bvec.shape),
            ],
            out_specs=[
                whole(length, width),
                whole(*qkv),
                whole(*qkv),
                whole(*qkv),
                pl.BlockSpec((block, heads * HEAD_DIM), lambda b, s: (b, 0)),
                pl.BlockSpec((heads, block, length), lambda b, s: (0, b, 0)),
                whole(2, block, width),
                whole(2, block, width),
            ],
            scratch_shapes=[
                pltpu.VMEM((heads, block, 2 * length), f32),
                pltpu.VMEM((block, length), f32),
                pltpu.VMEM((block, 2 * block), f32),
            ],
        ),
        out_shape=[
            sds((length, width), bf16),
            sds(qkv, bf16),
            sds(qkv, bf16),
            sds(qkv, bf16),
            sds((length, heads * HEAD_DIM), bf16),
            sds((heads, length, length), bf16),
            sds((2, block, width), f32),
            sds((2, block, width), bf16),
        ],
        compiler_params=params(52),
        cost_estimate=cost(2e10, 12e6),
        name="attention_forward",
    )(sc, tok, gain, wq, wmt, bvec)


def mix_backward_kernel(sc, da, db, dc, dd, wmt, att, own, gmt, d_att, dmx):
    x, c = sc[2], sc[3]
    _, block, half = da.shape
    heads = d_att.shape[0]
    for xx in range(2):
        for ref, cc, side in ((da, c, x), (db, c, 1 - x), (dc, 1 - c, x), (dd, 1 - c, 1 - x)):
            rows = pl.ds(pl.multiple_of((2 * xx + cc) * block, block), block)
            dmx[rows, pl.ds(pl.multiple_of(side * half, 128), half)] = ref[xx]
    own[...] = dmx[pl.ds(pl.multiple_of((2 * x + c) * block, block), block), :]
    d = nn(dmx[...], wmt[...]).astype(bf16)
    for h in range(heads):
        d_att[h] = d[:, h * HEAD_DIM : (h + 1) * HEAD_DIM]
    gmt[...] = tn(dmx[...], att[...]).astype(bf16)


def mix_backward(sc, pieces, wmt, att, heads):
    _, block, half = pieces[0].shape
    length, width = 4 * block, 2 * half
    return pl.pallas_call(
        mix_backward_kernel,
        in_specs=[smem()] + [vmem()] * 6,
        out_specs=[vmem()] * 3,
        out_shape=[
            sds((block, width), bf16),
            sds((width, heads * HEAD_DIM), bf16),
            sds((heads, length, HEAD_DIM), bf16),
        ],
        scratch_shapes=[pltpu.VMEM((length, width), bf16)],
        compiler_params=params(40),
        cost_estimate=cost(2e9, 6e6),
        name="mix_backward",
    )(sc, *pieces, wmt, att)


def backward_kernel(d_att, p, q, k, v, hot, dproj, tab, score, ds_ref, dkt, dvt, diag, left):
    b = pl.program_id(0)
    heads, length, _ = q.shape
    block = p.shape[1]
    blocks = length // block
    scale = HEAD_DIM ** (-0.5)
    rc = 16
    margin = 128

    @pl.when(b == 0)
    def _():
        dkt[...] = jnp.zeros_like(dkt)
        dvt[...] = jnp.zeros_like(dvt)
        diag[...] = jnp.zeros_like(diag)
        left[...] = jnp.zeros_like(left)

    def one_block(bs):
        r0 = bs * block
        kv = min(r0 + 2 * block, length)
        lo = max(r0 - margin, 0)
        ones = jnp.ones((8, block), bf16)
        for h in range(heads):
            d_out = d_att[h, r0 : r0 + block, :]
            score[:, :kv] = nt(d_out, v[h, :kv, :])

            def body(i, carry):
                rows = pl.ds(pl.multiple_of(i * rc, rc), rc)
                pr = p[h, rows, :kv].astype(f32)
                pd = pr * score[rows, :kv]
                ds = pd - pr * jnp.sum(pd, axis=1, keepdims=True)
                ds_ref[rows, :kv] = ds.astype(bf16)
                parts = [ds[:, lo:kv]]
                before = margin + lo - r0
                after = length - before - (kv - lo)
                if before:
                    parts.insert(0, jnp.zeros((rc, before), f32))
                if after:
                    parts.append(jnp.zeros((rc, after), f32))
                band = jnp.concatenate(parts, axis=1)
                for g in range(rc // 8):
                    shift = length - (i * rc + 8 * g)
                    diag[h] += pltpu.roll(band[8 * g : 8 * g + 8], shift, 1)
                return carry

            lax.fori_loop(0, block // rc, body, 0)
            at = h * HEAD_DIM
            dq = nn(ds_ref[:, :kv], k[h, :kv, :]) * scale
            dproj[r0 : r0 + block, at : at + HEAD_DIM] = dq.astype(bf16)
            dkt[h, :, :kv] += tn(q[h, r0 : r0 + block, :], ds_ref[:, :kv])
            dvt[h, :, :kv] += tn(d_out, p[h, :, :kv])
            if lo > 0:
                left[h, :, :lo] += nn(ones, ds_ref[:, :lo])

    for bs in range(blocks):
        pl.when(b == bs)(functools.partial(one_block, bs))

    @pl.when(b == blocks - 1)
    def _():
        lane = lax.broadcasted_iota(i32, (1, 128), 1)
        for h in range(heads):
            at = (heads + h) * HEAD_DIM
            dproj[:, at : at + HEAD_DIM] = (dkt[h] * scale).T.astype(bf16)
            at = (2 * heads + h) * HEAD_DIM
            dproj[:, at : at + HEAD_DIM] = dvt[h].T.astype(bf16)
            total = jnp.zeros((1, length), f32)
            for s in range(8):
                total = total + pltpu.roll(diag[h, s : s + 1, :], (length - s) % length, 1)
            far = jnp.sum(left[h, 0:1, :])
            row = jnp.dot(
                jnp.broadcast_to(total, (8, length)),
                hot[...],
                precision=highest,
                preferred_element_type=f32,
            )
            tab[h : h + 1, :] = row[0:1] + jnp.where(lane == len(bucket_edges), far, 0.0)


def attention_backward(d_att, p, q, k, v):
    heads, length, _ = q.shape
    block = length // 4
    lanes = np.arange(length)
    offsets = np.where(lanes < 768, lanes, lanes - length) - 128
    hot = (bucket_of(offsets)[:, None] == np.arange(128)[None, :]).astype(np.float32)
    whole = lambda *shape: pl.BlockSpec(shape, lambda b: (0,) * len(shape))
    qkv = (heads, length, HEAD_DIM)
    wide = 3 * heads * HEAD_DIM
    return pl.pallas_call(
        backward_kernel,
        grid=(4,),
        in_specs=[
            whole(*qkv),
            pl.BlockSpec((heads, block, length), lambda b: (0, b, 0)),
            whole(*qkv),
            whole(*qkv),
            whole(*qkv),
            whole(length, 128),
        ],
        out_specs=[whole(length, wide), whole(8, 128)],
        out_shape=[sds((length, wide), bf16), sds((8, 128), f32)],
        scratch_shapes=[
            pltpu.VMEM((block, length), f32),
            pltpu.VMEM((block, length), bf16),
            pltpu.VMEM((heads, HEAD_DIM, length), f32),
            pltpu.VMEM((heads, HEAD_DIM, length), f32),
            pltpu.VMEM((heads, 8, length), f32),
            pltpu.VMEM((heads, 8, length), f32),
        ],
        compiler_params=params(48),
        cost_estimate=cost(3e10, 12e6),
        name="attention_backward",
    )(d_att, p, q, k, v, jnp.asarray(hot))


def input_gradient_kernel(sc, dproj, wq, tok, keep, send, gain_sum):
    c = sc[3]
    _, block, width = keep.shape
    total = jnp.zeros((1, width), f32)
    for i in range(4):
        rows = slice(i * block, (i + 1) * block)
        dn = nt(dproj[rows, :], wq[...])
        t = tok[rows, :].astype(f32)
        hat = t * lax.rsqrt(jnp.mean(t * t, axis=-1, keepdims=True) + 1e-06)
        total = total + jnp.sum(dn * hat, axis=0, keepdims=True)

        @pl.when(c == i % 2)
        def _():
            keep[i // 2] = dn

        @pl.when(c != i % 2)
        def _():
            send[i // 2] = dn.astype(bf16)

    gain_sum[...] = jnp.broadcast_to(total, gain_sum.shape)


def input_gradient(sc, dproj, wq, tok):
    length, width = tok.shape
    block = length // 4
    return pl.pallas_call(
        input_gradient_kernel,
        in_specs=[smem()] + [vmem()] * 3,
        out_specs=[vmem()] * 3,
        out_shape=[
            sds((2, block, width), f32),
            sds((2, block, width), bf16),
            sds((8, width), f32),
        ],
        compiler_params=params(40),
        cost_estimate=cost(4e9, 8e6),
        name="input_gradient",
    )(sc, dproj, wq, tok)


def router_kernel(keep, recv, tok, gain, wrt, routes, hidden, scaled, sums):
    _, block, half = keep.shape
    rows = 2 * block
    h = keep[...] + recv[...].astype(f32) + tok[...].astype(f32)
    h = h.reshape(rows, half)
    hidden[...] = h
    g = (h * gain[...]).astype(bf16)
    scaled[...] = g
    hi, lo = split_two(h * h)
    ones = jnp.ones((8, half), bf16)
    square = nt(ones, hi) + nt(ones, lo)
    logits = nt(wrt[...], g)
    ids = lax.broadcasted_iota(i32, logits.shape, 0)
    first = jnp.sum(jnp.where(ids == routes[0:1, :], logits, 0.0), axis=0, keepdims=True)
    second = jnp.sum(jnp.where(ids == routes[1:2, :], logits, 0.0), axis=0, keepdims=True)
    index = lax.broadcasted_iota(i32, square.shape, 0)
    sums[...] = jnp.where(index == 0, square, jnp.where(index == 1, first, second))


def router(keep, recv, tok, gain, wrt, routes):
    _, block, half = keep.shape
    rows = 2 * block
    return pl.pallas_call(
        router_kernel,
        in_specs=[vmem()] * 6,
        out_specs=[vmem()] * 3,
        out_shape=[sds((rows, half), f32), sds((rows, half), bf16), sds((8, rows), f32)],
        compiler_params=params(32),
        cost_estimate=cost(1e9, 3e6),
        name="router",
    )(keep, recv, tok, gain, wrt, routes)


def pack_kernel(own, other, slots_own, slots_other, *outs):
    for n, out in enumerate(outs):
        count = out.shape[0]
        total = None
        for values, slots in ((own, slots_own), (other, slots_other)):
            at = n * count + lax.broadcasted_iota(i32, (count, values.shape[0]), 0)
            hot = (slots[0:1, :] == at) | (slots[1:2, :] == at)
            part = nn(jnp.where(hot, 1.0, 0.0).astype(bf16), values[...])
            total = part if total is None else total + part
        out[...] = total.astype(bf16)


def pack(own, other, slots_own, slots_other, chunks, count):
    half = own.shape[1]
    return pl.pallas_call(
        pack_kernel,
        in_specs=[vmem()] * 4,
        out_specs=[vmem()] * chunks,
        out_shape=[sds((count, half), bf16)] * chunks,
        compiler_params=params(48),
        cost_estimate=cost(2e9, 3e6),
        name="pack",
    )(own, other, slots_own, slots_other)


def unpack_kernel(slots_own, slots_other, gates_own, gates_other, *refs):
    chunks, (keep, send) = refs[:-2], refs[-2:]
    for slots, gates, out in ((slots_own, gates_own, keep), (slots_other, gates_other, send)):
        picked = [None, None]
        for n, rows in enumerate(chunks):
            count = rows.shape[0]
            at = n * count + lax.broadcasted_iota(i32, (slots.shape[0], count), 1)
            for j in range(2):
                hot = jnp.where(slots[:, j : j + 1] == at, 1.0, 0.0).astype(bf16)
                part = nn(hot, rows[...])
                picked[j] = part if picked[j] is None else picked[j] + part
        out[...] = (gates[:, 0:1] * picked[0] + gates[:, 1:2] * picked[1]).astype(out.dtype)


def unpack(slots_own, slots_other, gates_own, gates_other, chunks):
    rows, half = slots_own.shape[0], chunks[0].shape[1]
    return pl.pallas_call(
        unpack_kernel,
        in_specs=[vmem()] * (4 + len(chunks)),
        out_specs=[vmem()] * 2,
        out_shape=[sds((rows, half), f32), sds((rows, half), bf16)],
        compiler_params=params(48),
        cost_estimate=cost(4e9, 4e6),
        name="unpack",
    )(slots_own, slots_other, gates_own, gates_other, *chunks)


def gates_to_slots_kernel(slots, gates, out):
    count, rows = out.shape[1], slots.shape[1]
    at = lax.broadcasted_iota(i32, (count, rows), 0)
    total = None
    for j in range(2):
        hot = jnp.where(slots[j : j + 1, :] == at, 1.0, 0.0).astype(bf16)
        hi, lo = split_two(jnp.broadcast_to(gates[j : j + 1, :], (8, rows)))
        part = nt(hi, hot) + nt(lo, hot)
        total = part if total is None else total + part
    out[...] = total


def gates_to_slots(slots, gates, count):
    return pl.pallas_call(
        gates_to_slots_kernel,
        in_specs=[vmem()] * 2,
        out_specs=vmem(),
        out_shape=sds((8, count), f32),
        compiler_params=params(48),
        cost_estimate=cost(1e8, 1e5),
        name="gates_to_slots",
    )(slots, gates)


def slots_to_tokens_kernel(slots, values, out):
    count, rows = values.shape[1], slots.shape[1]
    at = lax.broadcasted_iota(i32, (count, rows), 0)
    hi, lo = split_two(jnp.broadcast_to(values[0:1, :], (8, count)))
    for j in range(2):
        hot = jnp.where(slots[j : j + 1, :] == at, 1.0, 0.0).astype(bf16)
        out[j : j + 1, :] = (nn(hi, hot) + nn(lo, hot))[0:1]


def slots_to_tokens(slots, values):
    return pl.pallas_call(
        slots_to_tokens_kernel,
        in_specs=[vmem()] * 2,
        out_specs=vmem(),
        out_shape=sds((2, slots.shape[1]), f32),
        compiler_params=params(48),
        cost_estimate=cost(1e8, 1e5),
        name="slots_to_tokens",
    )(slots, values)


def combine_kernel(keep, recv, hidden, r, dlog, wrt, gain, dn, dots, gain_sum):
    hi, lo = split_two(dlog[...])
    d = keep[...] + recv[...].astype(f32) + nn(hi, wrt[...]) + nn(lo, wrt[...])
    dn[...] = d
    hat = hidden[...] * r[...]
    prod = d * hat
    gain_sum[...] = jnp.broadcast_to(jnp.sum(prod, axis=0, keepdims=True), gain_sum.shape)
    hi, lo = split_two(prod * gain[...])
    ones = jnp.ones((8, hi.shape[1]), bf16)
    dots[...] = nt(ones, hi) + nt(ones, lo)


def combine(keep, recv, hidden, r, dlog, wrt, gain):
    rows, half = hidden.shape
    return pl.pallas_call(
        combine_kernel,
        in_specs=[vmem()] * 7,
        out_specs=[vmem()] * 3,
        out_shape=[sds((rows, half), f32), sds((8, rows), f32), sds((8, half), f32)],
        compiler_params=params(40),
        cost_estimate=cost(1e9, 4e6),
        name="combine",
    )(keep, recv, hidden, r, dlog, wrt, gain)


def hidden_gradient_kernel(dn, hidden, r, gain, dots, recv, d_out, out):
    rows, half = dn.shape
    mean = row_to_column((dots[0:1, :] + recv[0:1, :]) * (0.5 / half), rows)
    rr = r[...]
    d = rr * (gain[...] * dn[...] - hidden[...] * rr * mean)
    out[...] = (d_out[...].astype(f32) + d).astype(bf16)


def hidden_gradient(dn, hidden, r, gain, dots, recv, d_out):
    rows, half = hidden.shape
    return pl.pallas_call(
        hidden_gradient_kernel,
        in_specs=[vmem()] * 7,
        out_specs=vmem(),
        out_shape=sds((rows, half), bf16),
        compiler_params=params(40),
        cost_estimate=cost(1e9, 4e6),
        name="hidden_gradient",
    )(dn, hidden, r, gain, dots, recv, d_out)


def expert_kernel(
    sc, xa, xb, da, db, w_in, w_out, inv_gain, normed, d_moe, act_ref, d_pre_ref, y, dr, dg
):
    x = sc[1]
    groups, _, cap, half = xa.shape
    rows = groups * cap
    width = 2 * half

    def rows_of(a, b):
        a = a[:, 0].astype(f32).reshape(rows, half)
        b = b[:, 0].astype(f32).reshape(rows, half)
        lo = jnp.where(x == 0, a, b)
        hi = jnp.where(x == 0, b, a)
        return jnp.concatenate([lo, hi], axis=1)

    g = rows_of(xa, xb)
    h = g * inv_gain[...]
    r = lax.rsqrt(jnp.sum(h * h, axis=1, keepdims=True) * (1.0 / width) + 1e-06)
    n = (g * r).astype(bf16)
    normed[0] = n
    u = nn(n, w_in[0])
    d = rows_of(da, db).astype(bf16)
    d_moe[0] = d
    da_ = nt(d, w_out[0])
    k = 0.7978845608028654
    uu = u * u
    t = jnp.tanh(k * u * (1.0 + 0.044715 * uu))
    a = 0.5 * (1.0 + t)
    act = (u * a).astype(bf16)
    act_ref[0] = act
    slope = a + 0.5 * u * (1.0 - t * t) * (k + (3.0 * 0.044715 * k) * uu)
    d_pre = (da_ * slope).astype(bf16)
    d_pre_ref[0] = d_pre
    dr[:, 0] = nt(d_pre, w_in[0]).reshape(groups, cap, width).astype(bf16)
    y[:, 0] = nn(act, w_out[0]).reshape(groups, cap, width).astype(bf16)
    hi, lo = split_two(act.astype(f32) * da_)
    ones = jnp.ones((8, hi.shape[1]), bf16)
    dg[0] = nt(ones, hi) + nt(ones, lo)


def experts(sc, xa, xb, da, db, w_in, w_out, inv_gain, virtual):
    groups, count, cap, half = xa.shape
    rows = groups * cap
    width = 2 * half
    local, _, hidden = w_in.shape
    rowspec = pl.BlockSpec((groups, 1, cap, half), lambda i, s: (0, i, 0, 0))
    outspec = pl.BlockSpec((groups, 1, cap, width), lambda i, s: (0, i, 0, 0))
    wspec = lambda i, s: ((s[0] + i) * local // virtual, 0, 0)
    keep = lambda w: pl.BlockSpec((1, rows, w), lambda i, s: (i, 0, 0))
    return pl.pallas_call(
        expert_kernel,
        grid_spec=pltpu.PrefetchScalarGridSpec(
            num_scalar_prefetch=1,
            grid=(count,),
            in_specs=[
                rowspec,
                rowspec,
                rowspec,
                rowspec,
                pl.BlockSpec((1, width, hidden), wspec),
                pl.BlockSpec((1, hidden, width), wspec),
                pl.BlockSpec((1, width), lambda i, s: (0, 0)),
            ],
            out_specs=[
                keep(width),
                keep(width),
                keep(hidden),
                keep(hidden),
                outspec,
                outspec,
                pl.BlockSpec((1, 8, rows), lambda i, s: (i, 0, 0)),
            ],
        ),
        out_shape=[
            sds((count, rows, width), bf16),
            sds((count, rows, width), bf16),
            sds((count, rows, hidden), bf16),
            sds((count, rows, hidden), bf16),
            sds((groups, count, cap, width), bf16),
            sds((groups, count, cap, width), bf16),
            sds((count, 8, rows), f32),
        ],
        compiler_params=params(56),
        cost_estimate=cost(count * 8 * rows * width * hidden, count * 6e6),
        name="experts",
    )(sc, xa, xb, da, db, w_in, w_out, inv_gain)


def weight_gradient_kernel(sc, gate, normed, d_moe, act, d_pre, g_in, g_out):
    rows = normed.shape[1]
    g = row_to_column(gate[0, 0:1, :], rows)
    g_out[0] = tn((act[0].astype(f32) * g).astype(bf16), d_moe[0])
    g_in[0] = tn(normed[0], (d_pre[0].astype(f32) * g).astype(bf16))


def per_device(
    tokens,
    gain_one,
    w_qkv,
    rel_table,
    w_mix,
    gain_two,
    w_router,
    w_in,
    w_out,
    routes,
    buffer_row_index,
    image_starts,
    d_output,
):
    block, width = tokens.shape
    tensor_count = lax.axis_size("tensor")
    tensor_index = lax.axis_index("tensor")
    groups = lax.axis_size("dp")
    cx, cc = tensor_index // 2, tensor_index % 2
    length = block * tensor_count
    heads = rel_table.shape[0] // tensor_count
    head_width = heads * HEAD_DIM
    local = w_in.shape[0]
    half = width // 2
    virtual = max(local, 2)
    per_half = virtual // 2
    cap = CAP * local // virtual
    vcap = cap if cap % 8 == 0 else -(-cap // 16) * 16
    chunks = 2 if per_half % 2 == 0 else 1
    per_chunk = per_half // chunks
    chunk_slots = groups * per_chunk * vcap
    half_slots = chunks * chunk_slots

    sc = jnp.concatenate([image_starts[0], jnp.stack([cx, cc]).astype(i32)])

    def feat(v, axis, side):
        return lax.dynamic_slice_in_dim(v, side * half, half, axis)

    wq_shard = jnp.moveaxis(w_qkv, 0, 1).reshape(w_qkv.shape[1], -1)
    wq = gather_dp(wq_shard).reshape(-1, wq_shard.shape[1])
    tok_x = swap_x(tokens)
    pair = jnp.stack([tokens, tok_x])
    pair_core = swap_core(pair)
    quarters = jnp.stack([pair, pair_core])

    def natural(v, core_first):
        order = jnp.stack([(2 * (cx ^ xx) + (cc ^ k)) for k in range(2) for xx in range(2)])
        flat = v.reshape((4,) + v.shape[2:])
        return jnp.take(flat, jnp.argsort(order), axis=0)

    tok_all = natural(quarters, True).reshape(length, width)
    wmt = gather_dp(w_mix.T).reshape(width, head_width)

    bias_table = lax.dynamic_slice_in_dim(rel_table, tensor_index * heads, heads, 0)
    hot = bucket_of(np.arange(2 * length) - length)[None, :] == np.arange(rel_table.shape[1])[:, None]
    bvec = jnp.dot(bias_table * LOG2E, jnp.asarray(hot.astype(np.float32)), precision=highest)
    bvec = jnp.pad(bvec, ((0, 8 - heads), (0, 0)))

    flat = routes * CAP + buffer_row_index
    expert_v, row_v = flat // cap, flat % cap
    group_v, v_v = expert_v // virtual, expert_v % virtual
    half_v, v2_v = v_v // per_half, v_v % per_half
    chunk_v, vc_v = v2_v // per_chunk, v2_v % per_chunk
    in_half = chunk_v * chunk_slots + (group_v * per_chunk + vc_v) * vcap + row_v
    mine = jnp.where(half_v == cc, in_half, -1)
    by_core = mine.reshape(2, 2, block, 2)
    half_tokens = lambda v, k: lax.dynamic_index_in_dim(v, k, 1, keepdims=False).reshape(
        (2 * block,) + v.shape[3:]
    )
    slots_own, slots_other = half_tokens(by_core, cc), half_tokens(by_core, 1 - cc)
    routes_own = half_tokens(routes.reshape(2, 2, block, 2), cc)
    slots_both = (group_v * virtual + v_v) * vcap + row_v

    do_x = swap_x(feat(d_output, 1, 1 - cx))
    do_mine = feat(d_output, 1, cx)
    do_own = jnp.where(cx == 0, jnp.stack([do_mine, do_x]), jnp.stack([do_x, do_mine]))
    do_own = do_own.reshape(2 * block, half)
    do_other = swap_core(do_own)

    def dispatch(own, other):
        out = []
        packed = pack(own, other, slots_own.T, slots_other.T, chunks, chunk_slots)
        for rows in packed:
            a = exchange(rows.reshape(groups, per_chunk, vcap, half))
            b = swap_x(a)
            ab = swap_core(jnp.stack([a, b]))
            out.append((a, b, ab[0], ab[1]))
        return out

    d_rows_in = dispatch(do_own, do_other)

    normed, q, k, v, att, probs, keep, send = attention_forward(
        sc, tok_all, gain_one[None], wq, wmt, bvec, heads
    )
    chip = keep + swap_core(send).astype(f32)
    mixed_recv = swap_x(feat(chip, 2, 1 - cx).astype(bf16))
    tok_half = lax.dynamic_index_in_dim(tok_all.reshape(2, 2, block, width), cc, 1, keepdims=False)
    gain_half = feat(gain_two, 0, cx)[None]
    wrt_half = feat(w_router, 0, cx).T
    hidden, scaled, sums = router(
        feat(chip, 2, cx), mixed_recv, feat(tok_half, 2, cx), gain_half, wrt_half, routes_own.T
    )
    rows_in = dispatch(scaled, swap_core(scaled))

    sums = sums + swap_x(sums)
    sums_pair = jnp.stack([sums, swap_core(sums)])

    def token_parts(v):
        r = lax.rsqrt(v[0] / width + 1e-06)
        return r, jax.nn.softmax(r[:, None] * v[1:3].T, axis=-1)

    r_own, gates_own = token_parts(sums_pair[0])
    r_other, gates_other = token_parts(sums_pair[1])
    r_own = r_own[:, None]

    def in_order(own, other):
        a, b = own.reshape((2, block) + own.shape[1:]), other.reshape((2, block) + other.shape[1:])
        both = jnp.where(cc == 0, jnp.stack([a, b], 1), jnp.stack([b, a], 1))
        return both.reshape((length,) + own.shape[1:])

    gates_all = in_order(gates_own, gates_other)
    gate_slots = gates_to_slots(slots_both.T, gates_all.T, groups * virtual * vcap)[0]
    gate_rows = exchange(gate_slots.reshape(groups, 1, virtual * vcap))
    gate_rows = jnp.moveaxis(gate_rows.reshape(groups, virtual, vcap), 1, 0)
    gate_rows = jnp.broadcast_to(
        gate_rows.reshape(virtual, 1, groups * vcap), (virtual, 8, groups * vcap)
    )

    inv_gain = (1.0 / gain_two)[None]
    kept, y_ready, dr_ready, dg_parts = {}, [], [], {}
    for n in range(chunks):
        xa, xb, xc, xd = rows_in[n]
        da, db, dc, dd = d_rows_in[n]
        result = {}
        for side, (x0, x1, d0, d1) in (("other", (xc, xd, dc, dd)), ("own", (xa, xb, da, db))):
            base = (cc if side == "own" else 1 - cc) * per_half + n * per_chunk
            call = jnp.stack([base, cx]).astype(i32)
            out = experts(call, x0, x1, d0, d1, w_in, w_out, inv_gain, virtual)
            kept[side, n] = (base, out[:4])
            dg_parts[side, n] = out[6][:, 0]
            result[side] = out
        dr = result["own"][5].astype(f32) + swap_core(result["other"][5]).astype(f32)
        dr = feat(dr, 3, cx) + swap_x(feat(dr, 3, 1 - cx).astype(bf16)).astype(f32)
        dr_ready.append(exchange(dr.astype(bf16)).reshape(chunk_slots, half))
        y_ready.append((result["own"][4], result["other"][4]))

    y_back = []
    for own, other in y_ready:
        y = own.astype(f32) + swap_core(other).astype(f32)
        y = feat(y, 3, cx) + swap_x(feat(y, 3, 1 - cx).astype(bf16)).astype(f32)
        y_back.append(exchange(y.astype(bf16)).reshape(chunk_slots, half))

    own_dg = jnp.concatenate([dg_parts["own", n] for n in range(chunks)], 0)
    other_dg = jnp.concatenate([dg_parts["other", n] for n in range(chunks)], 0)
    dg = jnp.where(
        cc == 0, jnp.concatenate([own_dg, other_dg], 0), jnp.concatenate([other_dg, own_dg], 0)
    )
    dg = jnp.moveaxis(dg.reshape(virtual, groups, vcap), 0, 1).reshape(groups, 1, virtual * vcap)
    dg = exchange(dg).reshape(1, groups * virtual * vcap)
    dg = slots_to_tokens(slots_both.T, dg)
    dg = dg + swap_core(dg)
    dg = dg + swap_x(dg)
    dg_own = half_tokens(dg.T.reshape(2, 2, block, 2), cc)
    d_chosen = gates_own * (dg_own - jnp.sum(gates_own * dg_own, axis=-1, keepdims=True))
    selectors = (routes_own[:, :, None] == jnp.arange(EXPERTS, dtype=i32)).astype(f32)
    d_logits = jnp.sum(d_chosen[:, :, None] * selectors, axis=1)
    nt_own = (scaled.astype(f32) * r_own).astype(bf16)
    grad_router = jnp.dot(nt_own.astype(f32).T, d_logits, precision=highest)

    keep_d, send_d = unpack(slots_own, slots_other, gates_own, gates_other, dr_ready)
    dn, dots, gain_two_sum = combine(
        keep_d, swap_core(send_d), hidden, r_own, d_logits, wrt_half, gain_half
    )
    d_mixed = hidden_gradient(dn, hidden, r_own, gain_half, dots, swap_x(dots), do_own)
    d_mixed = d_mixed.reshape(2, block, half)
    d_mixed_x = swap_x(d_mixed)
    d_pair = swap_core(jnp.stack([d_mixed, d_mixed_x]))
    d_hidden, gmt, d_att = mix_backward(
        sc, (d_mixed, d_mixed_x, d_pair[0], d_pair[1]), wmt, att, heads
    )
    grad_mix = exchange(gmt.reshape(groups, width // groups, head_width))
    grad_mix = jnp.sum(grad_mix.astype(f32), axis=0).T

    dproj, table = attention_backward(d_att, probs, q, k, v)
    grad_qkv = tn(normed, dproj).astype(bf16)
    grad_qkv = exchange(grad_qkv.reshape(groups, width // groups, 3 * head_width))
    keep_n, send_n, gain_one_sum = input_gradient(sc, dproj, wq, tok_all)
    d_norm = keep_n + swap_core(send_n).astype(f32)
    mine_q = lax.dynamic_index_in_dim(d_norm, cx, 0, keepdims=False)
    other_q = lax.dynamic_index_in_dim(d_norm, 1 - cx, 0, keepdims=False)
    d_norm = mine_q + swap_x(other_q.astype(bf16)).astype(f32)
    t = tokens.astype(f32)
    r = lax.rsqrt(jnp.mean(t * t, axis=-1, keepdims=True) + 1e-06)
    gd = gain_one * d_norm
    hat = t * r
    grad_input = d_hidden.astype(f32) + r * (gd - hat * jnp.mean(gd * hat, axis=-1, keepdims=True))
    grad_qkv = jnp.sum(grad_qkv.astype(f32), axis=0)
    grad_qkv = jnp.moveaxis(grad_qkv.reshape(width // groups, 3, head_width), 1, 0)

    def sum_dp(v):
        step = 1
        while step < groups:
            v = v + lax.ppermute(v, "dp", [(i, i ^ step) for i in range(groups)])
            step *= 2
        return v

    small = jnp.concatenate([grad_router, gain_two_sum[0].reshape(-1, EXPERTS)], axis=0)
    rest = half - gain_two_sum.shape[1]
    del rest
    gain_rows = half // EXPERTS
    gain_part = gain_two_sum[0]
    small = sum_dp(small)
    small = small + swap_core(small)
    small_x = swap_x(small)
    small = jnp.where(cx == 0, jnp.stack([small, small_x]), jnp.stack([small_x, small]))
    del gain_part
    grad_router = small[:, :half].reshape(width, EXPERTS)
    grad_gain_two = small[:, half : half + gain_rows].reshape(width)

    table = lax.dynamic_update_slice_in_dim(
        jnp.zeros(rel_table.shape, f32), table[:heads, : rel_table.shape[1]], tensor_index * heads, 0
    )
    last = jnp.concatenate([gain_one_sum[0], table.reshape(-1)]).reshape(-1, 128)
    last = sum_dp(last)
    last = last + swap_core(last)
    last = (last + swap_x(last)).reshape(-1)
    grad_gain_one, grad_table = last[:width], last[width:].reshape(rel_table.shape)

    hidden_units = w_in.shape[2]

    def in_virtual_order(j):
        own = jnp.concatenate([kept["own", n][1][j] for n in range(chunks)], 0)
        other = jnp.concatenate([kept["other", n][1][j] for n in range(chunks)], 0)
        return own, other

    rows = groups * vcap
    order = jnp.concatenate(
        [cc * per_half + jnp.arange(per_half), (1 - cc) * per_half + jnp.arange(per_half)]
    ).astype(i32)
    parts = [jnp.concatenate(in_virtual_order(j), 0) for j in range(4)]
    rowspec = lambda w: pl.BlockSpec((1, rows, w), lambda i, s: (i, 0, 0))
    g_in, g_out = pl.pallas_call(
        weight_gradient_kernel,
        grid_spec=pltpu.PrefetchScalarGridSpec(
            num_scalar_prefetch=1,
            grid=(virtual,),
            in_specs=[
                pl.BlockSpec((1, 8, rows), lambda i, s: (s[i], 0, 0)),
                rowspec(width),
                rowspec(width),
                rowspec(hidden_units),
                rowspec(hidden_units),
            ],
            out_specs=[
                pl.BlockSpec((1, width, hidden_units), lambda i, s: (s[i], 0, 0)),
                pl.BlockSpec((1, hidden_units, width), lambda i, s: (s[i], 0, 0)),
            ],
        ),
        out_shape=[
            sds((virtual, width, hidden_units), f32),
            sds((virtual, hidden_units, width), f32),
        ],
        compiler_params=params(48),
        cost_estimate=cost(virtual * 4 * rows * width * hidden_units, virtual * 6.7e6),
        name="weight_gradient",
    )(order, gate_rows, *parts)
    if virtual != local:
        g_in = jnp.sum(g_in.reshape(local, virtual // local, width, hidden_units), axis=1)
        g_out = jnp.sum(g_out.reshape(local, virtual // local, hidden_units, width), axis=1)

    keep_y, send_y = unpack(slots_own, slots_other, gates_own, gates_other, y_back)
    out = (hidden + keep_y + swap_core(send_y).astype(f32)).astype(bf16).reshape(2, block, half)
    out_mine = lax.dynamic_index_in_dim(out, cx, 0, keepdims=False)
    out_recv = swap_x(lax.dynamic_index_in_dim(out, 1 - cx, 0, keepdims=False))
    output = jnp.where(
        cx == 0,
        jnp.concatenate([out_mine, out_recv], 1),
        jnp.concatenate([out_recv, out_mine], 1),
    )
    return (
        output,
        grad_input,
        grad_gain_one,
        grad_qkv,
        grad_table,
        grad_mix,
        grad_gain_two,
        grad_router,
        g_in,
        g_out,
    )


def solution(mesh):
    in_specs = (
        P(("dp", "tensor"), None),
        P(),
        P(None, "dp", "tensor"),
        P(),
        P("tensor", "dp"),
        P(),
        P(),
        P("dp", None, "tensor"),
        P("dp", "tensor", None),
        P("dp", None),
        P("dp", None),
        P("dp", None),
        P(("dp", "tensor"), None),
    )
    out_specs = (
        P(("dp", "tensor"), None),
        P(("dp", "tensor"), None),
        P(),
        P(None, "dp", "tensor"),
        P(),
        P("tensor", "dp"),
        P(),
        P(),
        P("dp", None, "tensor"),
        P("dp", "tensor", None),
    )
    return jax.shard_map(
        per_device, mesh=mesh, in_specs=in_specs, out_specs=out_specs, check_vma=False
    )
```

```python
import functools

import jax
import jax.numpy as jnp
import numpy as np
from jax import lax
from jax.experimental import pallas as pl
from jax.experimental.pallas import tpu as pltpu
from jax.sharding import PartitionSpec as P

HEAD_DIM = 64
EXPERTS = 64
SPAN = 256
CAP = 40
LOG2E = 1.4426950408889634
NEG = -1e30
bucket_edges = (1, 2, 3, 4, 5, 6, 7, 8, 11, 16, 23, 32, 45, 64, 91)
highest = lax.Precision.HIGHEST
f32 = jnp.float32
bf16 = jnp.bfloat16
i32 = jnp.int32
MIB = 1 << 20


def bucket_of(offsets):
    magnitude = np.abs(offsets)
    levels = np.zeros(offsets.shape, np.int32)
    for threshold in bucket_edges:
        levels = levels + (magnitude >= threshold).astype(np.int32)
    return levels + (len(bucket_edges) + 1) * (offsets > 0).astype(np.int32)


def nn(a, b):
    return jnp.dot(a, b, preferred_element_type=f32)


def nt(a, b):
    return lax.dot_general(a, b, (((1,), (1,)), ((), ())), preferred_element_type=f32)


def tn(a, b):
    return lax.dot_general(a, b, (((0,), (0,)), ((), ())), preferred_element_type=f32)


def split_two(v):
    hi = v.astype(bf16)
    return hi, (v - hi.astype(f32)).astype(bf16)


def swap_core(v):
    return lax.ppermute(v, "tensor", [(i, i ^ 1) for i in range(lax.axis_size("tensor"))])


def swap_x(v):
    return lax.ppermute(v, "tensor", [(i, i ^ 2) for i in range(lax.axis_size("tensor"))])


def exchange(v):
    return lax.all_to_all(v, "dp", 0, 0, tiled=True)


def exchange_small(v):
    groups = lax.axis_size("dp")
    if groups > 8:
        return exchange(v)
    me = lax.axis_index("dp")
    parts = []
    for k in range(groups):
        piece = lax.dynamic_index_in_dim(v, me ^ k, 0, keepdims=False)
        parts.append(lax.ppermute(piece, "dp", [(i, i ^ k) for i in range(groups)]) if k else piece)
    return jnp.take(jnp.stack(parts), jnp.arange(groups) ^ me, axis=0)


def gather_dp(v):
    groups = lax.axis_size("dp")
    return exchange(jnp.broadcast_to(v[None], (groups,) + v.shape))


def smem():
    return pl.BlockSpec(memory_space=pltpu.SMEM)


def sds(shape, dtype):
    return jax.ShapeDtypeStruct(shape, dtype)


def one_step(kernel, name, us, scalars, arrays, outs, scratch=(), mib=20):
    def whole(v):
        return pl.BlockSpec(v.shape, lambda i: (0,) * len(v.shape))

    return pl.pallas_call(
        kernel,
        grid=(1,),
        in_specs=[smem() for _ in scalars] + [whole(v) for v in arrays],
        out_specs=[whole(v) for v in outs],
        out_shape=list(outs),
        scratch_shapes=list(scratch),
        compiler_params=params(mib),
        cost_estimate=cost(1e6, us * 3e6),
        name=name,
    )(*scalars, *arrays)


def params(mib=62):
    return pltpu.CompilerParams(vmem_limit_bytes=62 * MIB)


def cost(flops, nbytes):
    return pl.CostEstimate(flops=int(600 * nbytes), bytes_accessed=int(nbytes), transcendentals=0)


def row_to_column(row, n):
    a = lax.broadcasted_iota(i32, (n, n), 0)
    b = lax.broadcasted_iota(i32, (n, n), 1)
    return jnp.sum(jnp.where(a == b, row, 0.0), axis=1, keepdims=True)


def quarter_rows(sc, flip_x, flip_c, block):
    at = 2 * (sc[2] ^ flip_x) + (sc[3] ^ flip_c)
    return pl.ds(pl.multiple_of(at * block, block), block)


def forward_kernel(
    sc, ta, tb, tc, td, gain, weights, bvec, normed, q, k, v, att, p_out, keep, send, toep, score, mask
):
    b = pl.program_id(0)
    block = att.shape[0]
    length = 4 * block
    heads = q.shape[0]
    blocks = length // block

    @pl.when(b == 0)
    def _():
        for i, ref in enumerate((ta, tb, tc, td)):
            rows = quarter_rows(sc, i % 2, i // 2, block)
            t = ref[...].astype(f32)
            n = t * lax.rsqrt(jnp.mean(t * t, axis=-1, keepdims=True) + 1e-06) * gain[...]
            n = n.astype(bf16)
            normed[rows, :] = n
            pr = nn(n, weights[:, : 3 * heads * HEAD_DIM]).astype(bf16)
            for h in range(heads):
                for j, out in enumerate((q, k, v)):
                    at = (j * heads + h) * HEAD_DIM
                    out[h, rows, :] = pr[:, at : at + HEAD_DIM]
        for h in range(heads):
            row = jnp.broadcast_to(bvec[h : h + 1, :], (8, 2 * length))
            for a in range(0, block, 8):
                toep[h, a : a + 8, :] = pltpu.roll(row, a, 1, stride=1, stride_axis=0)

    s0, s1, x, c = sc[0], sc[1], sc[2], sc[3]
    rc = 16

    def one_block(bs):
        r0 = bs * block
        kv = min(r0 + 2 * block, length)
        wide = kv - r0
        ii = r0 + lax.broadcasted_iota(i32, (block, wide), 0)
        jj = r0 + lax.broadcasted_iota(i32, (block, wide), 1)
        first = (ii >= s0) & (ii < s0 + SPAN) & (jj >= s0) & (jj < s0 + SPAN)
        second = (ii >= s1) & (ii < s1 + SPAN) & (jj >= s1) & (jj < s1 + SPAN)
        mask[:, :wide] = jnp.where((jj <= ii) | first | second, 0.0, NEG)
        for h in range(heads):
            score[:, :kv] = nt(q[h, r0 : r0 + block, :], k[h, :kv, :])
            for i in range(block // rc):
                rows = slice(i * rc, (i + 1) * rc)
                s = score[rows, :kv] * (HEAD_DIM ** (-0.5) * LOG2E)
                s = s + toep[h, rows, length - r0 : length - r0 + kv]
                right = s[:, r0:] + mask[rows, :wide]
                s = right if r0 == 0 else jnp.concatenate([s[:, :r0], right], axis=1)
                e = jnp.exp2(s - jnp.max(s, axis=1, keepdims=True))
                total = jnp.sum(e, axis=1, keepdims=True)
                p_out[h, rows, :kv] = (e * (1.0 / total)).astype(bf16)
            att[:, h * HEAD_DIM : (h + 1) * HEAD_DIM] = nn(p_out[h, :, :kv], v[h, :kv, :]).astype(
                bf16
            )
        mixed = nt(att[...], weights[:, 3 * heads * HEAD_DIM :])

        @pl.when(c == bs % 2)
        def _():
            keep[(bs // 2) ^ x] = mixed

        @pl.when(c != bs % 2)
        def _():
            send[(bs // 2) ^ x] = mixed.astype(bf16)

    for bs in range(blocks):
        pl.when(b == bs)(functools.partial(one_block, bs))


def attention_forward(sc, toks, gain, weights, bvec, heads):
    block, width = toks[0].shape
    length = 4 * block
    whole = lambda *shape: pl.BlockSpec(shape, lambda b, s: (0,) * len(shape))
    qkv = (heads, length, HEAD_DIM)
    return pl.pallas_call(
        forward_kernel,
        grid_spec=pltpu.PrefetchScalarGridSpec(
            num_scalar_prefetch=1,
            grid=(4,),
            in_specs=[whole(block, width)] * 4
            + [
                whole(1, width),
                whole(*weights.shape),
                whole(*bvec.shape),
            ],
            out_specs=[
                whole(length, width),
                whole(*qkv),
                whole(*qkv),
                whole(*qkv),
                pl.BlockSpec((block, heads * HEAD_DIM), lambda b, s: (b, 0)),
                pl.BlockSpec((heads, block, length), lambda b, s: (0, b, 0)),
                whole(2, block, width),
                whole(2, block, width),
            ],
            scratch_shapes=[
                pltpu.VMEM((heads, block, 2 * length), f32),
                pltpu.VMEM((block, length), f32),
                pltpu.VMEM((block, 2 * block), f32),
            ],
        ),
        out_shape=[
            sds((length, width), bf16),
            sds(qkv, bf16),
            sds(qkv, bf16),
            sds(qkv, bf16),
            sds((length, heads * HEAD_DIM), bf16),
            sds((heads, length, length), bf16),
            sds((2, block, width), f32),
            sds((2, block, width), bf16),
        ],
        compiler_params=params(40),
        cost_estimate=cost(1e6, 48e6),
        name="attention_forward",
    )(sc, *toks, gain, weights, bvec)


def chip_sum_kernel(sc, keep, recv, mine, away):
    half = mine.shape[1]
    x = sc[2]
    total = (keep[...] + recv[...].astype(f32)).reshape(mine.shape[0], 2 * half)
    lo, hi = total[:, :half], total[:, half:]
    mine[...] = jnp.where(x == 0, lo, hi)
    away[...] = jnp.where(x == 0, hi, lo).astype(bf16)


def chip_sum(sc, keep, recv):
    _, block, width = keep.shape
    shape = (2 * block, width // 2)
    outs = [sds(shape, f32), sds(shape, bf16)]
    return one_step(chip_sum_kernel, "chip_sum", 1.5, [sc], [keep, recv], outs)


def mix_backward_kernel(sc, da, db, dc, dd, weights, att, own, gmt, d_att, dmx):
    x = sc[2]
    rows, half = da.shape
    block = rows // 2
    heads = d_att.shape[0]
    for ref, flip_x, flip_c, side in ((da, 0, 0, x), (db, 1, 0, 1 - x), (dc, 0, 1, x), (dd, 1, 1, 1 - x)):
        for n in range(2):
            to = quarter_rows(sc, n ^ flip_x, flip_c, block)
            lanes = pl.ds(pl.multiple_of(side * half, 128), half)
            dmx[to, lanes] = ref[n * block : (n + 1) * block, :]
    own[...] = dmx[quarter_rows(sc, 0, 0, block), :]
    d = nn(dmx[...], weights[:, 3 * heads * HEAD_DIM :]).astype(bf16)
    for h in range(heads):
        d_att[h] = d[:, h * HEAD_DIM : (h + 1) * HEAD_DIM]
    gmt[...] = tn(dmx[...], att[...]).astype(bf16)


def mix_backward(sc, pieces, weights, att, heads):
    rows, half = pieces[0].shape
    block, length, width = rows // 2, 2 * rows, 2 * half
    outs = [
        sds((block, width), bf16),
        sds((width, heads * HEAD_DIM), bf16),
        sds((heads, length, HEAD_DIM), bf16),
    ]
    scratch = [pltpu.VMEM((length, width), bf16)]
    arrays = [*pieces, weights, att]
    return one_step(mix_backward_kernel, "mix_backward", 3, [sc], arrays, outs, scratch)


def backward_kernel(
    sc,
    d_att,
    p,
    q,
    k,
    v,
    hot,
    normed,
    gmt,
    weights,
    ta,
    tb,
    tc,
    td,
    tab,
    keep,
    send,
    gain_sum,
    *refs,
):
    gws = refs[:-7]
    dproj, score, ds_ref, dkt, dvt, diag, left = refs[-7:]
    b = pl.program_id(0)
    heads, length, _ = q.shape
    block = p.shape[1]
    blocks = length // block
    scale = HEAD_DIM ** (-0.5)
    rc = 16
    margin = 128

    @pl.when(b == 0)
    def _():
        dkt[...] = jnp.zeros_like(dkt)
        dvt[...] = jnp.zeros_like(dvt)
        diag[...] = jnp.zeros_like(diag)
        left[...] = jnp.zeros_like(left)

    def one_block(bs):
        r0 = bs * block
        kv = min(r0 + 2 * block, length)
        lo = max(r0 - margin, 0)
        ones = jnp.ones((8, block), bf16)
        for h in range(heads):
            d_out = d_att[h, r0 : r0 + block, :]
            score[:, :kv] = nt(d_out, v[h, :kv, :])

            for i in range(block // rc):
                rows = slice(i * rc, (i + 1) * rc)
                pr = p[h, rows, :kv].astype(f32)
                pd = pr * score[rows, :kv]
                ds = pd - pr * jnp.sum(pd, axis=1, keepdims=True)
                ds_ref[rows, :kv] = ds.astype(bf16)
                parts = [ds[:, lo:kv]]
                before = margin + lo - r0
                after = length - before - (kv - lo)
                if before:
                    parts.insert(0, jnp.zeros((rc, before), f32))
                if after:
                    parts.append(jnp.zeros((rc, after), f32))
                band = jnp.concatenate(parts, axis=1)
                for g in range(rc // 8):
                    shift = (length - (i * rc + 8 * g)) % length
                    diag[h] += pltpu.roll(band[8 * g : 8 * g + 8], shift, 1)
            at = h * HEAD_DIM
            dq = nn(ds_ref[:, :kv], k[h, :kv, :]) * scale
            dproj[r0 : r0 + block, at : at + HEAD_DIM] = dq.astype(bf16)
            dkt[h, :, :kv] += tn(q[h, r0 : r0 + block, :], ds_ref[:, :kv])
            dvt[h, :, :kv] += tn(d_out, p[h, :, :kv])
            if lo > 0:
                left[h, :, :lo] += nn(ones, ds_ref[:, :lo])

    for bs in range(blocks):
        pl.when(b == bs)(functools.partial(one_block, bs))

    @pl.when(b == blocks - 1)
    def _():
        lane = lax.broadcasted_iota(i32, (1, 128), 1)
        for h in range(heads):
            at = (heads + h) * HEAD_DIM
            dproj[:, at : at + HEAD_DIM] = (dkt[h] * scale).T.astype(bf16)
            at = (2 * heads + h) * HEAD_DIM
            dproj[:, at : at + HEAD_DIM] = dvt[h].T.astype(bf16)
            total = jnp.zeros((1, length), f32)
            for s in range(8):
                total = total + pltpu.roll(diag[h, s : s + 1, :], (length - s) % length, 1)
            far = jnp.sum(left[h, 0:1, :])
            row = jnp.dot(
                jnp.broadcast_to(total, (8, length)),
                hot[...],
                precision=highest,
                preferred_element_type=f32,
            )
            tab[h : h + 1, :] = row[0:1] + jnp.where(lane == len(bucket_edges), far, 0.0)
        gw = tn(normed[...], dproj[...]).astype(bf16)
        step = sum(ref.shape[1] for ref in gws)
        first = 0
        for ref in gws:
            for n in range(ref.shape[0]):
                rows = slice(n * step + first, n * step + first + ref.shape[1])
                ref[n, :, : dproj.shape[1]] = gw[rows]
                ref[n, :, dproj.shape[1] :] = gmt[rows, :]
            first += ref.shape[1]
        all_sum = jnp.zeros((1, weights.shape[0]), f32)
        wq = weights[:, : dproj.shape[1]]
        for i, ref in enumerate((ta, tb, tc, td)):
            dn = nt(dproj[quarter_rows(sc, i % 2, i // 2, block), :], wq)
            t = ref[...].astype(f32)
            hat = t * lax.rsqrt(jnp.mean(t * t, axis=-1, keepdims=True) + 1e-06)
            all_sum = all_sum + jnp.sum(dn * hat, axis=0, keepdims=True)
            if i < 2:
                keep[i] = dn
            else:
                send[i - 2] = dn.astype(bf16)
        gain_sum[...] = jnp.broadcast_to(all_sum, gain_sum.shape)


def attention_backward(sc, d_att, p, q, k, v, normed, gmt, weights, toks, groups):
    heads, length, _ = q.shape
    block = length // 4
    width = normed.shape[1]
    lanes = np.arange(length)
    offsets = np.where(lanes < 768, lanes, lanes - length) - 128
    hot = (bucket_of(offsets)[:, None] == np.arange(128)[None, :]).astype(np.float32)
    whole = lambda *shape: pl.BlockSpec(shape, lambda b, s: (0,) * len(shape))
    qkv = (heads, length, HEAD_DIM)
    wide = 3 * heads * HEAD_DIM
    outs = [
        sds((8, 128), f32),
        sds((2, block, width), f32),
        sds((2, block, width), bf16),
        sds((8, width), f32),
    ]
    step, columns = width // groups, wide + gmt.shape[1]
    if step % 32 == 0:
        outs += [sds((groups, 32, columns), bf16), sds((groups, step - 32, columns), bf16)]
    else:
        outs += [sds((1, width, columns), bf16)]
    return pl.pallas_call(
        backward_kernel,
        grid_spec=pltpu.PrefetchScalarGridSpec(
            num_scalar_prefetch=1,
            grid=(4,),
            in_specs=[
                whole(*qkv),
                pl.BlockSpec((heads, block, length), lambda b, s: (0, b, 0)),
                whole(*qkv),
                whole(*qkv),
                whole(*qkv),
                whole(length, 128),
                whole(*normed.shape),
                whole(*gmt.shape),
                whole(*weights.shape),
            ]
            + [whole(block, width)] * 4,
            out_specs=[whole(*o.shape) for o in outs],
            scratch_shapes=[
                pltpu.VMEM((length, wide), bf16),
                pltpu.VMEM((block, length), f32),
                pltpu.VMEM((block, length), bf16),
                pltpu.VMEM((heads, HEAD_DIM, length), f32),
                pltpu.VMEM((heads, HEAD_DIM, length), f32),
                pltpu.VMEM((heads, 8, length), f32),
                pltpu.VMEM((heads, 8, length), f32),
            ],
        ),
        out_shape=outs,
        compiler_params=params(),
        cost_estimate=cost(1e6, 48e6),
        name="attention_backward",
    )(sc, d_att, p, q, k, v, jnp.asarray(hot), normed, gmt, weights, *toks)


def router_kernel(mine, recv, ta, tb, gain, wrt, routes, hidden, scaled, sums):
    rows, half = mine.shape
    block = rows // 2
    for n, tok in enumerate((ta, tb)):
        to, back = slice(n * block, (n + 1) * block), slice((1 - n) * block, (2 - n) * block)
        h = mine[to, :] + recv[back, :].astype(f32) + tok[...].astype(f32)
        hidden[to, :] = h
        scaled[to, :] = (h * gain[...]).astype(bf16)
    h = hidden[...]
    hi, lo = split_two(h * h)
    ones = jnp.ones((8, half), bf16)
    square = nt(ones, hi) + nt(ones, lo)
    logits = nt(wrt[...], scaled[...])
    ids = lax.broadcasted_iota(i32, logits.shape, 0)
    first = jnp.sum(jnp.where(ids == routes[0:1, :], logits, 0.0), axis=0, keepdims=True)
    second = jnp.sum(jnp.where(ids == routes[1:2, :], logits, 0.0), axis=0, keepdims=True)
    index = lax.broadcasted_iota(i32, square.shape, 0)
    sums[...] = jnp.where(index == 0, square, jnp.where(index == 1, first, second))


def router(mine, recv, ta, tb, gain, wrt, routes):
    rows, half = mine.shape
    outs = [sds((rows, half), f32), sds((rows, half), bf16), sds((8, rows), f32)]
    arrays = [mine, recv, ta, tb, gain, wrt, routes]
    return one_step(router_kernel, "router", 1.5, [], arrays, outs)


def pack_kernel(parts, count, slots, *refs):
    values, outs = refs[:parts], refs[parts:]
    for n, out in enumerate(outs):
        total, first = None, 0
        for ref in values:
            rows = ref.shape[0]
            at = n * count + lax.broadcasted_iota(i32, (count, rows), 0)
            lanes = slice(first, first + rows)
            hot = (slots[0:1, lanes] == at) | (slots[1:2, lanes] == at)
            part = nn(jnp.where(hot, 1.0, 0.0).astype(bf16), ref[...])
            total = part if total is None else total + part
            first += rows
        out[...] = total.astype(bf16)


def pack(values, slots, chunks, count):
    half = values[0].shape[1]
    outs = [sds((count, half), bf16)] * chunks
    kernel = functools.partial(pack_kernel, len(values), count)
    return one_step(kernel, "pack", 2.5, [], [slots, *values], outs)


def unpack_kernel(offset, slots_own, slots_other, gates_own, gates_other, rows, *refs):
    keep, send = refs[-2:]
    count = rows.shape[0]
    for j, (slots, gates, out) in enumerate(
        ((slots_own, gates_own, keep), (slots_other, gates_other, send))
    ):
        at = offset + lax.broadcasted_iota(i32, (slots.shape[0], count), 1)
        total = refs[j][...] if len(refs) > 2 else None
        for c in range(2):
            hot = jnp.where(slots[:, c : c + 1] == at, 1.0, 0.0).astype(bf16)
            part = gates[:, c : c + 1] * nn(hot, rows[...])
            total = part if total is None else total + part
        out[...] = total.astype(out.dtype)


def unpack(slots_own, slots_other, gates_own, gates_other, n, chunk, sofar, last):
    count, half = chunk.shape
    rows = slots_own.shape[0]
    outs = [sds((rows, half), f32), sds((rows, half), bf16 if last else f32)]
    arrays = [slots_own, slots_other, gates_own, gates_other, chunk, *sofar]
    kernel = functools.partial(unpack_kernel, n * count)
    return one_step(kernel, "unpack", 2.5, [], arrays, outs)


def combine_kernel(keep, recv, hidden, r, dlog, wrt, gain, dn, dots, gain_sum):
    hi, lo = split_two(dlog[...])
    d = keep[...] + recv[...].astype(f32) + nn(hi, wrt[...]) + nn(lo, wrt[...])
    dn[...] = d
    hat = hidden[...] * r[...]
    prod = d * hat
    gain_sum[...] = jnp.broadcast_to(jnp.sum(prod, axis=0, keepdims=True), gain_sum.shape)
    hi, lo = split_two(prod * gain[...])
    ones = jnp.ones((8, hi.shape[1]), bf16)
    dots[...] = nt(ones, hi) + nt(ones, lo)


def combine(keep, recv, hidden, r, dlog, wrt, gain):
    rows, half = hidden.shape
    outs = [sds((rows, half), f32), sds((8, rows), f32), sds((8, half), f32)]
    arrays = [keep, recv, hidden, r, dlog, wrt, gain]
    return one_step(combine_kernel, "combine", 2, [], arrays, outs)


def hidden_gradient_kernel(dn, hidden, r, gain, dots, recv, oa, ob, out):
    rows, half = dn.shape
    block = rows // 2
    other = jnp.concatenate([recv[0:1, block:], recv[0:1, :block]], axis=1)
    mean = row_to_column((dots[0:1, :] + other) * (0.5 / half), rows)
    rr = r[...]
    d = rr * (gain[...] * dn[...] - hidden[...] * rr * mean)
    out[:block, :] = (oa[...].astype(f32) + d[:block]).astype(bf16)
    out[block:, :] = (ob[...].astype(f32) + d[block:]).astype(bf16)


def hidden_gradient(dn, hidden, r, gain, dots, recv, oa, ob):
    arrays = [dn, hidden, r, gain, dots, recv, oa, ob]
    outs = [sds(hidden.shape, bf16)]
    return one_step(hidden_gradient_kernel, "hidden_gradient", 1.5, [], arrays, outs)[0]


def full_rows(scratch, x, a, b):
    groups, _, cap, half = a.shape
    mine = pl.ds(pl.multiple_of(x * half, 128), half)
    away = pl.ds(pl.multiple_of((1 - x) * half, 128), half)
    scratch[:, mine] = a[:, 0].astype(f32).reshape(groups * cap, half)
    scratch[:, away] = b[:, 0].astype(f32).reshape(groups * cap, half)
    return scratch[...]


def d_act_kernel(sc, da, db, w_out, d_moe, d_act, scratch):
    d = full_rows(scratch, sc[1], da, db).astype(bf16)
    d_moe[0] = d
    d_act[0] = nt(d, w_out[0]).astype(bf16)


def row_specs(groups, cap, half):
    return [pl.BlockSpec((groups, 1, cap, half), lambda i, s: (0, i, 0, 0))]


def d_act_rows(sc, da, db, w_out, virtual):
    groups, count, cap, half = da.shape
    rows, width = groups * cap, 2 * half
    local, hidden, _ = w_out.shape
    out = lambda w: pl.BlockSpec((1, rows, w), lambda i, s: (i, 0, 0))
    return pl.pallas_call(
        d_act_kernel,
        grid_spec=pltpu.PrefetchScalarGridSpec(
            num_scalar_prefetch=1,
            grid=(count,),
            in_specs=row_specs(groups, cap, half) * 2
            + [
                pl.BlockSpec(
                    (1, hidden, width), lambda i, s: ((s[0] + i) * local // virtual, 0, 0)
                )
            ],
            out_specs=[out(width), out(hidden)],
            scratch_shapes=[pltpu.VMEM((rows, width), f32)],
        ),
        out_shape=[sds((count, rows, width), bf16), sds((count, rows, hidden), bf16)],
        compiler_params=params(28),
        cost_estimate=cost(1e6, count * 5e6),
        name="d_act_rows",
    )(sc, da, db, w_out)


def expert_kernel(summing, sc, xa, xb, d_act, w_in, inv_gain, *refs):
    if summing:
        recv, normed, act_ref, d_pre_ref, dg, mine, away, scratch = refs
    else:
        normed, act_ref, d_pre_ref, dg, dr, scratch = refs
    x = sc[1]
    groups, _, cap, half = xa.shape
    rows, width = groups * cap, 2 * half
    g = full_rows(scratch, x, xa, xb)
    h = g * inv_gain[...]
    r = lax.rsqrt(jnp.sum(h * h, axis=1, keepdims=True) * (1.0 / width) + 1e-06)
    n = (g * r).astype(bf16)
    normed[0] = n
    u = nn(n, w_in[0])
    k = 0.7978845608028654
    uu = u * u
    t = jnp.tanh(u * (k + (k * 0.044715) * uu))
    a = 0.5 + 0.5 * t
    act = (u * a).astype(bf16)
    act_ref[0] = act
    slope = a + (0.5 * u) * (1.0 - t * t) * (k + (3.0 * 0.044715 * k) * uu)
    da = d_act[0].astype(f32)
    d_pre = (da * slope).astype(bf16)
    d_pre_ref[0] = d_pre
    hi, lo = split_two(act.astype(f32) * da)
    ones = jnp.ones((8, hi.shape[1]), bf16)
    dg[0] = nt(ones, hi) + nt(ones, lo)
    d = nt(d_pre, w_in[0])
    if summing:
        d = d + recv[:, 0].astype(f32).reshape(rows, width)
        lo, hi = d[:, :half], d[:, half:]
        mine[:, 0] = jnp.where(x == 0, lo, hi).reshape(groups, cap, half)
        away[:, 0] = jnp.where(x == 0, hi, lo).reshape(groups, cap, half).astype(bf16)
    else:
        dr[:, 0] = d.reshape(groups, cap, width).astype(bf16)


def experts(sc, xa, xb, d_act, first, w_in, inv_gain, virtual, recv=None):
    groups, count, cap, half = xa.shape
    rows, width = groups * cap, 2 * half
    local, _, hidden = w_in.shape
    (part,) = row_specs(groups, cap, half)
    (full,) = row_specs(groups, cap, width)
    keep = lambda w: pl.BlockSpec((1, rows, w), lambda i, s: (i, 0, 0))
    shape = (groups, count, cap)
    summing = recv is not None
    return pl.pallas_call(
        functools.partial(expert_kernel, summing),
        grid_spec=pltpu.PrefetchScalarGridSpec(
            num_scalar_prefetch=1,
            grid=(count,),
            in_specs=[
                part,
                part,
                pl.BlockSpec((1, rows, hidden), lambda i, s: (first + i, 0, 0)),
                pl.BlockSpec(
                    (1, width, hidden), lambda i, s: ((s[0] + i) * local // virtual, 0, 0)
                ),
                pl.BlockSpec((1, width), lambda i, s: (0, 0)),
            ]
            + ([full] if summing else []),
            out_specs=[
                keep(width),
                keep(hidden),
                keep(hidden),
                pl.BlockSpec((1, 8, rows), lambda i, s: (i, 0, 0)),
            ]
            + ([part, part] if summing else [full]),
            scratch_shapes=[pltpu.VMEM((rows, width), f32)],
        ),
        out_shape=[
            sds((count, rows, width), bf16),
            sds((count, rows, hidden), bf16),
            sds((count, rows, hidden), bf16),
            sds((count, 8, rows), f32),
        ]
        + (
            [sds(shape + (half,), f32), sds(shape + (half,), bf16)]
            if summing
            else [sds(shape + (width,), bf16)]
        ),
        compiler_params=params(30),
        cost_estimate=cost(1e6, count * 11e6),
        name="experts",
    )(sc, xa, xb, d_act, w_in, inv_gain, *([recv] if summing else []))


def by_chunk(index, per_chunk, body, chunks):
    for n in range(chunks):
        pl.when(index // per_chunk == n)(functools.partial(body, n))


def chunk_specs(rows, width, per_chunk, chunks):
    def at(n):
        return lambda i, s: (jnp.clip(i - n * per_chunk, 0, per_chunk - 1), 0, 0)

    return [pl.BlockSpec((1, rows, width), at(n)) for n in range(chunks)]


def expert_out_kernel(summing, per_chunk, sc, w_out, *refs):
    if summing:
        recv, acts, (mine, away) = refs[0], refs[1:-2], refs[-2:]
    else:
        acts, (y_ref,) = refs[:-1], refs[-1:]

    def body(n):
        y = nn(acts[n][0], w_out[0])
        if summing:
            groups, _, cap, half = mine.shape
            y = y + recv[:, 0].astype(f32).reshape(groups * cap, 2 * half)
            lo, hi = y[:, :half], y[:, half:]
            mine[:, 0] = jnp.where(sc[1] == 0, lo, hi).reshape(groups, cap, half)
            away[:, 0] = jnp.where(sc[1] == 0, hi, lo).reshape(groups, cap, half).astype(bf16)
        else:
            groups, _, cap, width = y_ref.shape
            y_ref[:, 0] = y.reshape(groups, cap, width).astype(bf16)

    by_chunk(pl.program_id(0), per_chunk, body, len(acts))


def expert_out(sc, w_out, acts, virtual, groups, recv=None):
    per_chunk, rows, hidden = acts[0].shape
    local, _, width = w_out.shape
    count, cap, half = per_chunk * len(acts), rows // groups, width // 2
    (part,) = row_specs(groups, cap, half)
    (full,) = row_specs(groups, cap, width)
    shape = (groups, count, cap)
    summing = recv is not None
    return pl.pallas_call(
        functools.partial(expert_out_kernel, summing, per_chunk),
        grid_spec=pltpu.PrefetchScalarGridSpec(
            num_scalar_prefetch=1,
            grid=(count,),
            in_specs=[
                pl.BlockSpec(
                    (1, hidden, width), lambda i, s: ((s[0] + i) * local // virtual, 0, 0)
                )
            ]
            + ([full] if summing else [])
            + chunk_specs(rows, hidden, per_chunk, len(acts)),
            out_specs=[part, part] if summing else [full],
        ),
        out_shape=[sds(shape + (half,), f32), sds(shape + (half,), bf16)]
        if summing
        else [sds(shape + (width,), bf16)],
        compiler_params=params(28),
        cost_estimate=cost(1e6, count * 4.5e6),
        name="expert_out",
    )(sc, w_out, *([recv] if summing else []), *acts)


def weight_gradient_kernel(sc, gate, d_moe, normed, act, d_pre, *refs):
    g_in, g_out = refs[-2:]
    g = row_to_column(gate[0, 0:1, :], gate.shape[2])
    g_out[0] = tn((act[0].astype(f32) * g).astype(bf16), d_moe[0])
    g_in[0] = tn(normed[0], (d_pre[0].astype(f32) * g).astype(bf16))


def weight_gradient(sc, gate, d_moe, first, normed, act, d_pre, virtual, earlier):
    count, rows, width = normed.shape
    hidden = act.shape[2]
    part = lambda w: pl.BlockSpec((1, rows, w), lambda i, s: (i, 0, 0))
    return pl.pallas_call(
        weight_gradient_kernel,
        grid_spec=pltpu.PrefetchScalarGridSpec(
            num_scalar_prefetch=1,
            grid=(count,),
            in_specs=[
                pl.BlockSpec((1, 8, rows), lambda i, s: (s[0] + i, 0, 0)),
                pl.BlockSpec((1, rows, width), lambda i, s: (first + i, 0, 0)),
                part(width),
                part(hidden),
                part(hidden),
            ]
            + [pl.BlockSpec(memory_space=pl.ANY)] * len(earlier),
            out_specs=[
                pl.BlockSpec((1, width, hidden), lambda i, s: (s[0] + i, 0, 0)),
                pl.BlockSpec((1, hidden, width), lambda i, s: (s[0] + i, 0, 0)),
            ],
        ),
        out_shape=[
            sds((virtual, width, hidden), f32),
            sds((virtual, hidden, width), f32),
        ],
        input_output_aliases={6 + n: n for n in range(len(earlier))},
        compiler_params=params(),
        cost_estimate=cost(1e6, count * 8e6),
        name="weight_gradient",
    )(sc, gate, d_moe, normed, act, d_pre, *earlier)


def after(value, *others):
    return lax.optimization_barrier((value,) + others)[0]


def per_device(
    tokens,
    gain_one,
    w_qkv,
    rel_table,
    w_mix,
    gain_two,
    w_router,
    w_in,
    w_out,
    routes,
    buffer_row_index,
    image_starts,
    d_output,
):
    block, width = tokens.shape
    tensor_count = lax.axis_size("tensor")
    tensor_index = lax.axis_index("tensor")
    groups = lax.axis_size("dp")
    cx, cc = tensor_index // 2, tensor_index % 2
    length = block * tensor_count
    heads = rel_table.shape[0] // tensor_count
    head_width = heads * HEAD_DIM
    local = w_in.shape[0]
    half = width // 2
    virtual = max(local, 2)
    per_half = virtual // 2
    cap = CAP * local // virtual
    vcap = cap if cap % 8 == 0 else -(-cap // 16) * 16
    chunks = 2 if per_half % 2 == 0 else 1
    per_chunk = per_half // chunks
    chunk_slots = groups * per_chunk * vcap
    half_slots = chunks * chunk_slots

    sc = jnp.concatenate([image_starts[0], jnp.stack([cx, cc]).astype(i32)])

    def feat(v, axis, side):
        return lax.dynamic_slice_in_dim(v, side * half, half, axis)

    shard = jnp.concatenate([w_qkv[0], w_qkv[1], w_qkv[2], w_mix.T], axis=1)
    weights = gather_dp(shard).reshape(width, 4 * head_width)
    tok_x = swap_x(tokens)
    tok_c = swap_core(tokens)
    tok_d = swap_core(tok_x)
    toks = (tokens, tok_x, tok_c, tok_d)

    bias_table = lax.dynamic_slice_in_dim(rel_table, tensor_index * heads, heads, 0)
    hot = bucket_of(np.arange(2 * length) - length)[None, :] == np.arange(rel_table.shape[1])[:, None]
    bvec = jnp.dot(bias_table * LOG2E, jnp.asarray(hot.astype(np.float32)), precision=highest)
    bvec = jnp.pad(bvec, ((0, 8 - heads), (0, 0)))

    def slot_parts(route, index):
        flat = route * CAP + index
        expert_v, row_v = flat // cap, flat % cap
        group_v, v_v = expert_v // virtual, expert_v % virtual
        half_v, v2_v = v_v // per_half, v_v % per_half
        chunk_v, vc_v = v2_v // per_chunk, v2_v % per_chunk
        in_half = chunk_v * chunk_slots + (group_v * per_chunk + vc_v) * vcap + row_v
        whole_half = (group_v * per_half + v2_v) * vcap + row_v
        is_mine = half_v == cc
        return (
            jnp.where(is_mine, in_half, -1),
            jnp.where(is_mine, whole_half, -1),
            (group_v * virtual + v_v) * vcap + row_v,
        )

    def relative(v):
        at = [2 * (cx ^ (n % 2)) + (cc ^ (n // 2)) for n in range(4)]
        return jnp.concatenate([lax.dynamic_slice_in_dim(v, a * block, block, 0) for a in at], 0)

    routes_rel = relative(routes)
    slots_rel, whole_rel, both_rel = slot_parts(routes_rel, relative(buffer_row_index))
    slots_own, slots_other = slots_rel[: 2 * block], slots_rel[2 * block :]
    whole_own, whole_other = whole_rel[: 2 * block], whole_rel[2 * block :]
    routes_own = routes_rel[: 2 * block]

    do_a = feat(d_output, 1, cx)
    do_b = swap_x(feat(d_output, 1, 1 - cx))
    (d_packed,) = pack((do_a, do_b, swap_core(do_a), swap_core(do_b)), whole_rel.T, 1, half_slots)
    d_packed, weights = lax.optimization_barrier((d_packed, weights))
    da = exchange(d_packed.reshape(groups, per_half, vcap, half))

    normed, q, k, v, att, probs, keep, send = attention_forward(
        sc, toks, gain_one[None], weights, bvec, heads
    )
    chip_mine, chip_away = chip_sum(sc, keep, swap_core(send))
    gain_half = feat(gain_two, 0, cx)[None]
    wrt_half = feat(w_router, 0, cx).T
    hidden, scaled, sums = router(
        chip_mine,
        swap_x(chip_away),
        feat(tokens, 1, cx),
        feat(tok_x, 1, cx),
        gain_half,
        wrt_half,
        routes_own.T,
    )
    db = swap_x(after(da, scaled))
    dc, dd = swap_core(da), swap_core(db)
    base_own = cc * per_half
    base_other = (1 - cc) * per_half
    call_own = jnp.stack([base_own, cx]).astype(i32)
    call_other = jnp.stack([base_other, cx]).astype(i32)
    d_moe_own, d_act_own = d_act_rows(call_own, da, db, w_out, virtual)
    d_moe_other, d_act_other = d_act_rows(call_other, dc, dd, w_out, virtual)

    rows_in = []
    for rows in pack((scaled, swap_core(scaled)), slots_rel.T, chunks, chunk_slots):
        a = exchange(rows.reshape(groups, per_chunk, vcap, half))
        b = swap_x(after(a, d_act_other, d_act_own) if rows_in else a)
        rows_in.append((a, b, swap_core(a), swap_core(b)))

    def flip(v):
        return jnp.concatenate([v[:, block:], v[:, :block]], axis=1)

    sums = sums + flip(swap_x(sums))
    sums_other = swap_core(sums)

    def token_parts(v):
        r = lax.rsqrt(v[0] / width + 1e-06)
        return r, jax.nn.softmax(r[:, None] * v[1:3].T, axis=-1)

    r_own, gates_own = token_parts(sums)
    r_other, gates_other = token_parts(sums_other)
    r_own = r_own[:, None]
    gates_all = jnp.concatenate([gates_own, gates_other], 0)
    def one_hots(slots):
        experts_hot = slots[:, :, None] // vcap == jnp.arange(groups * virtual, dtype=i32)
        rows_hot = slots[:, :, None] % vcap == jnp.arange(vcap, dtype=i32)
        return experts_hot.astype(f32), rows_hot.astype(f32)

    experts_hot, rows_hot = one_hots(both_rel)
    gate_slots = jnp.einsum(
        "tce,tcr->er", experts_hot * gates_all[:, :, None], rows_hot, precision=highest
    )
    gate_send = gate_slots.reshape(groups, 1, virtual * vcap)

    inv_gain = (1.0 / gain_two)[None]
    others, owns, dr_send, dr_recvs = [], [], [], []
    for n in range(chunks):
        first = n * per_chunk
        xc, xd = rows_in[n][2:]
        if n == 0:
            xc, d_act_own = lax.optimization_barrier((xc, d_act_own))
        call = call_other + jnp.asarray([first, 0], i32)
        others.append(experts(call, xc, xd, d_act_other, first, w_in, inv_gain, virtual))
    for n in range(chunks):
        first = n * per_chunk
        xa, xb = rows_in[n][:2]
        call = call_own + jnp.asarray([first, 0], i32)
        xa = after(xa, owns[-1][5]) if owns else xa
        out = experts(
            call, xa, xb, d_act_own, first, w_in, inv_gain, virtual, swap_core(others[n][4])
        )
        owns.append(out)
        dr_recvs.append(swap_x(out[5]))
        dr_send.append((out[4] + dr_recvs[-1].astype(f32)).astype(bf16))

    own_dg = jnp.concatenate([o[3][:, 0] for o in owns], 0)
    other_dg = jnp.concatenate([o[3][:, 0] for o in others], 0)
    dg = jnp.where(
        cc == 0, jnp.concatenate([own_dg, other_dg], 0), jnp.concatenate([other_dg, own_dg], 0)
    )
    dg = jnp.moveaxis(dg.reshape(virtual, groups, vcap), 0, 1).reshape(groups, 1, virtual * vcap)
    dg = dg + swap_core(dg)
    dg = dg + swap_x(after(dg, owns[-1][5]))

    acts = [after(o[1], dr_recvs[0]) for o in others]
    (y_other,) = expert_out(call_other, w_out, acts, virtual, groups)
    acts = [after(o[1], dr_recvs[-1], dg) for o in owns]
    y_mine, y_away = expert_out(call_own, w_out, acts, virtual, groups, swap_core(y_other))
    y = (y_mine + swap_x(y_away).astype(f32)).astype(bf16)
    dr_send[-1] = after(dr_send[-1], y_away)
    dr_back = [exchange(v).reshape(chunk_slots, half) for v in dr_send]
    unpack_args = (slots_own, slots_other, gates_own, gates_other)
    sofar = []
    for n in range(chunks - 1):
        sofar = unpack(*unpack_args, n, dr_back[n], sofar, False)
    both = jnp.concatenate([gate_send, dg], axis=2)
    both = exchange_small(after(both, sofar[0] if sofar else y_away))
    gate_rows, dg = both[:, 0, : virtual * vcap], both[:, 0, virtual * vcap :]
    gate_rows = jnp.moveaxis(gate_rows.reshape(groups, virtual, vcap), 1, 0)
    gate_rows = jnp.broadcast_to(
        gate_rows.reshape(virtual, 1, groups * vcap), (virtual, 8, groups * vcap)
    )
    dg = dg.reshape(groups * virtual, vcap)

    def to_tokens(slots):
        ehot = (slots[:, None] // vcap == jnp.arange(groups * virtual, dtype=i32)).astype(f32)
        rhot = (slots[:, None] % vcap == jnp.arange(vcap, dtype=i32)).astype(f32)
        return jnp.sum(jnp.dot(ehot, dg, precision=highest) * rhot, axis=1)

    both_own = both_rel[: 2 * block]
    dg_own = jnp.stack([to_tokens(both_own[:, c]) for c in range(2)], axis=1)
    d_chosen = gates_own * (dg_own - jnp.sum(gates_own * dg_own, axis=-1, keepdims=True))
    selectors = (routes_own[:, :, None] == jnp.arange(EXPERTS, dtype=i32)).astype(f32)
    d_logits = jnp.sum(d_chosen[:, :, None] * selectors, axis=1)
    nt_own = (scaled.astype(f32) * r_own).astype(bf16)
    grad_router = jnp.dot(nt_own.astype(f32).T, d_logits, precision=highest)

    dr_last, d_logits = lax.optimization_barrier((dr_back[-1], d_logits))
    keep_d, send_d = unpack(*unpack_args, chunks - 1, dr_last, sofar, True)
    dn, dots, gain_two_sum = combine(
        keep_d, swap_core(send_d), hidden, r_own, d_logits, wrt_half, gain_half
    )
    dn, y = lax.optimization_barrier((dn, y))
    y_back = exchange(y).reshape(half_slots, half)
    d_mixed = hidden_gradient(dn, hidden, r_own, gain_half, dots, swap_x(dots), do_a, do_b)
    d_mixed_x = swap_x(d_mixed)
    d_hidden, gmt, d_att = mix_backward(
        sc, (d_mixed, d_mixed_x, swap_core(d_mixed), swap_core(d_mixed_x)), weights, att, heads
    )

    d_att, y_back = lax.optimization_barrier((d_att, y_back))
    table, keep_n, send_n, gain_one_sum, *grad_w = attention_backward(
        sc, d_att, probs, q, k, v, normed, gmt, weights, toks, groups
    )
    started = grad_w[0]
    grad_w = [exchange(v.reshape(groups, -1, v.shape[-1])) for v in grad_w]
    if len(grad_w) > 1:
        send_n, gain_one_sum, y_back, first_w = lax.optimization_barrier(
            (send_n, gain_one_sum, y_back, grad_w[0])
        )
        grad_w[0] = first_w
    grad_w = jnp.concatenate(grad_w, axis=1) if len(grad_w) > 1 else grad_w[0]
    d_norm = keep_n + swap_core(send_n).astype(f32)
    d_norm = d_norm[0] + swap_x(d_norm[1].astype(bf16)).astype(f32)
    t = tokens.astype(f32)
    r = lax.rsqrt(jnp.mean(t * t, axis=-1, keepdims=True) + 1e-06)
    gd = gain_one * d_norm
    hat = t * r
    grad_input = d_hidden.astype(f32) + r * (gd - hat * jnp.mean(gd * hat, axis=-1, keepdims=True))
    grad_w = jnp.sum(grad_w.astype(f32), axis=0)
    grad_qkv = jnp.stack([grad_w[:, j * head_width : (j + 1) * head_width] for j in range(3)])
    grad_mix = grad_w[:, 3 * head_width :].T

    def sum_dp(v):
        step = 1
        while step < groups:
            v = v + lax.ppermute(v, "dp", [(i, i ^ step) for i in range(groups)])
            step *= 2
        return v

    table = lax.dynamic_update_slice_in_dim(
        jnp.zeros(rel_table.shape, f32), table[:heads, : rel_table.shape[1]], tensor_index * heads, 0
    )
    small = jnp.concatenate(
        [gain_one_sum[0], table.reshape(-1), gain_two_sum[0], grad_router.reshape(-1)]
    )
    small = sum_dp(small.reshape(-1, 128))
    small = small + swap_core(small)
    small_x = swap_x(small).reshape(-1)
    small = small.reshape(-1)
    cut = width + rel_table.size
    last = small[:cut] + small_x[:cut]
    grad_gain_one, grad_table = last[:width], last[width:].reshape(rel_table.shape)
    small, small_x = small[cut:], small_x[cut:]
    small = jnp.where(cx == 0, jnp.stack([small, small_x]), jnp.stack([small_x, small]))
    grad_gain_two = small[:, :half].reshape(width)
    grad_router = small[:, half:].reshape(width, EXPERTS)

    grads = []
    for call, gone, d_moe in ((call_own, owns, d_moe_own), (call_other, others, d_moe_other)):
        d_moe = after(d_moe, started)
        for n, o in enumerate(gone):
            first = n * per_chunk
            at = call + jnp.asarray([first, 0], i32)
            grads = weight_gradient(at, gate_rows, d_moe, first, *o[:3], virtual, grads)
    g_in, g_out = grads
    if virtual != local:
        hidden_units = w_in.shape[2]
        g_in = jnp.sum(g_in.reshape(local, virtual // local, width, hidden_units), axis=1)
        g_out = jnp.sum(g_out.reshape(local, virtual // local, hidden_units, width), axis=1)

    keep_y, send_y = unpack(
        whole_own, whole_other, gates_own, gates_other, 0, y_back, [], True
    )
    out = (hidden + keep_y + swap_core(send_y).astype(f32)).astype(bf16)
    out_recv = swap_x(out[block:])
    output = jnp.where(
        cx == 0,
        jnp.concatenate([out[:block], out_recv], 1),
        jnp.concatenate([out_recv, out[:block]], 1),
    )
    return (
        output,
        grad_input,
        grad_gain_one,
        grad_qkv,
        grad_table,
        grad_mix,
        grad_gain_two,
        grad_router,
        g_in,
        g_out,
    )


def solution(mesh):
    in_specs = (
        P(("dp", "tensor"), None),
        P(),
        P(None, "dp", "tensor"),
        P(),
        P("tensor", "dp"),
        P(),
        P(),
        P("dp", None, "tensor"),
        P("dp", "tensor", None),
        P("dp", None),
        P("dp", None),
        P("dp", None),
        P(("dp", "tensor"), None),
    )
    out_specs = (
        P(("dp", "tensor"), None),
        P(("dp", "tensor"), None),
        P(),
        P(None, "dp", "tensor"),
        P(),
        P("tensor", "dp"),
        P(),
        P(),
        P("dp", None, "tensor"),
        P("dp", "tensor", None),
    )
    return jax.shard_map(
        per_device, mesh=mesh, in_specs=in_specs, out_specs=out_specs, check_vma=False
    )
```

```python
import functools

import jax
import jax.numpy as jnp
import numpy as np
from jax import lax
from jax.experimental import pallas as pl
from jax.experimental.pallas import tpu as pltpu
from jax.sharding import PartitionSpec as P

HEAD_DIM = 64
EXPERTS = 64
SPAN = 256
CAP = 40
LOG2E = 1.4426950408889634
NEG = -1e30
bucket_edges = (1, 2, 3, 4, 5, 6, 7, 8, 11, 16, 23, 32, 45, 64, 91)
highest = lax.Precision.HIGHEST
f32 = jnp.float32
bf16 = jnp.bfloat16
i32 = jnp.int32
MIB = 1 << 20


def bucket_of(offsets):
    magnitude = np.abs(offsets)
    levels = np.zeros(offsets.shape, np.int32)
    for threshold in bucket_edges:
        levels = levels + (magnitude >= threshold).astype(np.int32)
    return levels + (len(bucket_edges) + 1) * (offsets > 0).astype(np.int32)


def nn(a, b):
    return jnp.dot(a, b, preferred_element_type=f32)


def nt(a, b):
    return lax.dot_general(a, b, (((1,), (1,)), ((), ())), preferred_element_type=f32)


def tn(a, b):
    return lax.dot_general(a, b, (((0,), (0,)), ((), ())), preferred_element_type=f32)


def split_two(v):
    hi = v.astype(bf16)
    return hi, (v - hi.astype(f32)).astype(bf16)


def swap_core(v):
    return lax.ppermute(v, "tensor", [(i, i ^ 1) for i in range(lax.axis_size("tensor"))])


def swap_x(v):
    return lax.ppermute(v, "tensor", [(i, i ^ 2) for i in range(lax.axis_size("tensor"))])


def exchange(v):
    return lax.all_to_all(v, "dp", 0, 0, tiled=True)


def exchange_small(v):
    groups = lax.axis_size("dp")
    order = jnp.arange(groups) ^ lax.axis_index("dp")
    v = jnp.take(v, order, axis=0)
    step = 1
    while step < groups:
        shape = v.shape
        v = v.reshape((groups // (2 * step), 2, step) + shape[1:])
        moved = lax.ppermute(v[:, 1], "dp", [(i, i ^ step) for i in range(groups)])
        v = jnp.stack([v[:, 0], moved], axis=1).reshape(shape)
        step *= 2
    return jnp.take(v, order, axis=0)


def gather_dp(v):
    groups = lax.axis_size("dp")
    return exchange(jnp.broadcast_to(v[None], (groups,) + v.shape))


def smem():
    return pl.BlockSpec(memory_space=pltpu.SMEM)


def sds(shape, dtype):
    return jax.ShapeDtypeStruct(shape, dtype)


def one_step(kernel, name, us, scalars, arrays, outs, scratch=(), mib=20):
    def whole(v):
        return pl.BlockSpec(v.shape, lambda i: (0,) * len(v.shape))

    return pl.pallas_call(
        kernel,
        grid=(1,),
        in_specs=[smem() for _ in scalars] + [whole(v) for v in arrays],
        out_specs=[whole(v) for v in outs],
        out_shape=list(outs),
        scratch_shapes=list(scratch),
        compiler_params=params(mib),
        cost_estimate=cost(1e6, us * 3e6),
        name=name,
    )(*scalars, *arrays)


def params(mib=62):
    return pltpu.CompilerParams(vmem_limit_bytes=62 * MIB)


def cost(flops, nbytes):
    return pl.CostEstimate(flops=int(600 * nbytes), bytes_accessed=int(nbytes), transcendentals=0)


def row_to_column(row, n):
    a = lax.broadcasted_iota(i32, (n, n), 0)
    b = lax.broadcasted_iota(i32, (n, n), 1)
    return jnp.sum(jnp.where(a == b, row, 0.0), axis=1, keepdims=True)


def quarter_rows(sc, flip_x, flip_c, block):
    at = 2 * (sc[2] ^ flip_x) + (sc[3] ^ flip_c)
    return pl.ds(pl.multiple_of(at * block, block), block)


def forward_kernel(
    sc, ta, tb, tc, td, gain, weights, bvec, normed, q, k, v, att, p_out, keep, send, toep, score, mask
):
    b = pl.program_id(0)
    block = att.shape[0]
    length = 4 * block
    heads = q.shape[0]
    blocks = length // block

    @pl.when(b == 0)
    def _():
        for i, ref in enumerate((ta, tb, tc, td)):
            rows = quarter_rows(sc, i % 2, i // 2, block)
            t = ref[...].astype(f32)
            n = t * lax.rsqrt(jnp.mean(t * t, axis=-1, keepdims=True) + 1e-06) * gain[...]
            n = n.astype(bf16)
            normed[rows, :] = n
            pr = nn(n, weights[:, : 3 * heads * HEAD_DIM]).astype(bf16)
            for h in range(heads):
                for j, out in enumerate((q, k, v)):
                    at = (j * heads + h) * HEAD_DIM
                    out[h, rows, :] = pr[:, at : at + HEAD_DIM]
        for h in range(heads):
            row = jnp.broadcast_to(bvec[h : h + 1, :], (8, 2 * length))
            for a in range(0, block, 8):
                toep[h, a : a + 8, :] = pltpu.roll(row, a, 1, stride=1, stride_axis=0)

    s0, s1, x, c = sc[0], sc[1], sc[2], sc[3]
    rc = 16

    def one_block(bs):
        r0 = bs * block
        kv = min(r0 + 2 * block, length)
        wide = kv - r0
        ii = r0 + lax.broadcasted_iota(i32, (block, wide), 0)
        jj = r0 + lax.broadcasted_iota(i32, (block, wide), 1)
        first = (ii >= s0) & (ii < s0 + SPAN) & (jj >= s0) & (jj < s0 + SPAN)
        second = (ii >= s1) & (ii < s1 + SPAN) & (jj >= s1) & (jj < s1 + SPAN)
        mask[:, :wide] = jnp.where((jj <= ii) | first | second, 0.0, NEG)
        for h in range(heads):
            score[:, :kv] = nt(q[h, r0 : r0 + block, :], k[h, :kv, :])
            for i in range(block // rc):
                rows = slice(i * rc, (i + 1) * rc)
                s = score[rows, :kv] * (HEAD_DIM ** (-0.5) * LOG2E)
                s = s + toep[h, rows, length - r0 : length - r0 + kv]
                right = s[:, r0:] + mask[rows, :wide]
                s = right if r0 == 0 else jnp.concatenate([s[:, :r0], right], axis=1)
                e = jnp.exp2(s - jnp.max(s, axis=1, keepdims=True))
                total = jnp.sum(e, axis=1, keepdims=True)
                p_out[h, rows, :kv] = (e * (1.0 / total)).astype(bf16)
            att[:, h * HEAD_DIM : (h + 1) * HEAD_DIM] = nn(p_out[h, :, :kv], v[h, :kv, :]).astype(
                bf16
            )
        mixed = nt(att[...], weights[:, 3 * heads * HEAD_DIM :])

        @pl.when(c == bs % 2)
        def _():
            keep[(bs // 2) ^ x] = mixed

        @pl.when(c != bs % 2)
        def _():
            send[(bs // 2) ^ x] = mixed.astype(bf16)

    for bs in range(blocks):
        pl.when(b == bs)(functools.partial(one_block, bs))


def attention_forward(sc, toks, gain, weights, bvec, heads):
    block, width = toks[0].shape
    length = 4 * block
    whole = lambda *shape: pl.BlockSpec(shape, lambda b, s: (0,) * len(shape))
    qkv = (heads, length, HEAD_DIM)
    return pl.pallas_call(
        forward_kernel,
        grid_spec=pltpu.PrefetchScalarGridSpec(
            num_scalar_prefetch=1,
            grid=(4,),
            in_specs=[whole(block, width)] * 4
            + [
                whole(1, width),
                whole(*weights.shape),
                whole(*bvec.shape),
            ],
            out_specs=[
                whole(length, width),
                whole(*qkv),
                whole(*qkv),
                whole(*qkv),
                pl.BlockSpec((block, heads * HEAD_DIM), lambda b, s: (b, 0)),
                pl.BlockSpec((heads, block, length), lambda b, s: (0, b, 0)),
                whole(2, block, width),
                whole(2, block, width),
            ],
            scratch_shapes=[
                pltpu.VMEM((heads, block, 2 * length), f32),
                pltpu.VMEM((block, length), f32),
                pltpu.VMEM((block, 2 * block), f32),
            ],
        ),
        out_shape=[
            sds((length, width), bf16),
            sds(qkv, bf16),
            sds(qkv, bf16),
            sds(qkv, bf16),
            sds((length, heads * HEAD_DIM), bf16),
            sds((heads, length, length), bf16),
            sds((2, block, width), f32),
            sds((2, block, width), bf16),
        ],
        compiler_params=params(40),
        cost_estimate=cost(1e6, 48e6),
        name="attention_forward",
    )(sc, *toks, gain, weights, bvec)


def chip_sum_kernel(sc, keep, recv, mine, away):
    half = mine.shape[1]
    x = sc[2]
    total = (keep[...] + recv[...].astype(f32)).reshape(mine.shape[0], 2 * half)
    lo, hi = total[:, :half], total[:, half:]
    mine[...] = jnp.where(x == 0, lo, hi)
    away[...] = jnp.where(x == 0, hi, lo).astype(bf16)


def chip_sum(sc, keep, recv):
    _, block, width = keep.shape
    shape = (2 * block, width // 2)
    outs = [sds(shape, f32), sds(shape, bf16)]
    return one_step(chip_sum_kernel, "chip_sum", 1.5, [sc], [keep, recv], outs)


def mix_backward_kernel(sc, da, db, dc, dd, weights, att, own, gmt, d_att, dmx):
    x = sc[2]
    rows, half = da.shape
    block = rows // 2
    heads = d_att.shape[0]
    for ref, flip_x, flip_c, side in ((da, 0, 0, x), (db, 1, 0, 1 - x), (dc, 0, 1, x), (dd, 1, 1, 1 - x)):
        for n in range(2):
            to = quarter_rows(sc, n ^ flip_x, flip_c, block)
            lanes = pl.ds(pl.multiple_of(side * half, 128), half)
            dmx[to, lanes] = ref[n * block : (n + 1) * block, :]
    own[...] = dmx[quarter_rows(sc, 0, 0, block), :]
    d = nn(dmx[...], weights[:, 3 * heads * HEAD_DIM :]).astype(bf16)
    for h in range(heads):
        d_att[h] = d[:, h * HEAD_DIM : (h + 1) * HEAD_DIM]
    gmt[...] = tn(dmx[...], att[...]).astype(bf16)


def mix_backward(sc, pieces, weights, att, heads):
    rows, half = pieces[0].shape
    block, length, width = rows // 2, 2 * rows, 2 * half
    outs = [
        sds((block, width), bf16),
        sds((width, heads * HEAD_DIM), bf16),
        sds((heads, length, HEAD_DIM), bf16),
    ]
    scratch = [pltpu.VMEM((length, width), bf16)]
    arrays = [*pieces, weights, att]
    return one_step(mix_backward_kernel, "mix_backward", 3, [sc], arrays, outs, scratch)


def backward_kernel(
    sc,
    d_att,
    p,
    q,
    k,
    v,
    hot,
    normed,
    gmt,
    weights,
    ta,
    tb,
    tc,
    td,
    tab,
    keep,
    send,
    gain_sum,
    *refs,
):
    gws = refs[:-7]
    dproj, score, ds_ref, dkt, dvt, diag, left = refs[-7:]
    b = pl.program_id(0)
    heads, length, _ = q.shape
    block = p.shape[1]
    blocks = length // block
    scale = HEAD_DIM ** (-0.5)
    rc = 16
    margin = 128

    @pl.when(b == 0)
    def _():
        dkt[...] = jnp.zeros_like(dkt)
        dvt[...] = jnp.zeros_like(dvt)
        diag[...] = jnp.zeros_like(diag)
        left[...] = jnp.zeros_like(left)

    def one_block(bs):
        r0 = bs * block
        kv = min(r0 + 2 * block, length)
        lo = max(r0 - margin, 0)
        ones = jnp.ones((8, block), bf16)
        for h in range(heads):
            d_out = d_att[h, r0 : r0 + block, :]
            score[:, :kv] = nt(d_out, v[h, :kv, :])

            for i in range(block // rc):
                rows = slice(i * rc, (i + 1) * rc)
                pr = p[h, rows, :kv].astype(f32)
                pd = pr * score[rows, :kv]
                ds = pd - pr * jnp.sum(pd, axis=1, keepdims=True)
                ds_ref[rows, :kv] = ds.astype(bf16)
                parts = [ds[:, lo:kv]]
                before = margin + lo - r0
                after = length - before - (kv - lo)
                if before:
                    parts.insert(0, jnp.zeros((rc, before), f32))
                if after:
                    parts.append(jnp.zeros((rc, after), f32))
                band = jnp.concatenate(parts, axis=1)
                for g in range(rc // 8):
                    shift = (length - (i * rc + 8 * g)) % length
                    diag[h] += pltpu.roll(band[8 * g : 8 * g + 8], shift, 1)
            at = h * HEAD_DIM
            dq = nn(ds_ref[:, :kv], k[h, :kv, :]) * scale
            dproj[r0 : r0 + block, at : at + HEAD_DIM] = dq.astype(bf16)
            dkt[h, :, :kv] += tn(q[h, r0 : r0 + block, :], ds_ref[:, :kv])
            dvt[h, :, :kv] += tn(d_out, p[h, :, :kv])
            if lo > 0:
                left[h, :, :lo] += nn(ones, ds_ref[:, :lo])

    for bs in range(blocks):
        pl.when(b == bs)(functools.partial(one_block, bs))

    @pl.when(b == blocks - 1)
    def _():
        lane = lax.broadcasted_iota(i32, (1, 128), 1)
        for h in range(heads):
            at = (heads + h) * HEAD_DIM
            dproj[:, at : at + HEAD_DIM] = (dkt[h] * scale).T.astype(bf16)
            at = (2 * heads + h) * HEAD_DIM
            dproj[:, at : at + HEAD_DIM] = dvt[h].T.astype(bf16)
            total = jnp.zeros((1, length), f32)
            for s in range(8):
                total = total + pltpu.roll(diag[h, s : s + 1, :], (length - s) % length, 1)
            far = jnp.sum(left[h, 0:1, :])
            row = jnp.dot(
                jnp.broadcast_to(total, (8, length)),
                hot[...],
                precision=highest,
                preferred_element_type=f32,
            )
            tab[h : h + 1, :] = row[0:1] + jnp.where(lane == len(bucket_edges), far, 0.0)
        gw = tn(normed[...], dproj[...]).astype(bf16)
        step = sum(ref.shape[1] for ref in gws)
        first = 0
        for ref in gws:
            for n in range(ref.shape[0]):
                rows = slice(n * step + first, n * step + first + ref.shape[1])
                ref[n, :, : dproj.shape[1]] = gw[rows]
                ref[n, :, dproj.shape[1] :] = gmt[rows, :]
            first += ref.shape[1]
        all_sum = jnp.zeros((1, weights.shape[0]), f32)
        wq = weights[:, : dproj.shape[1]]
        for i, ref in enumerate((ta, tb, tc, td)):
            dn = nt(dproj[quarter_rows(sc, i % 2, i // 2, block), :], wq)
            t = ref[...].astype(f32)
            hat = t * lax.rsqrt(jnp.mean(t * t, axis=-1, keepdims=True) + 1e-06)
            all_sum = all_sum + jnp.sum(dn * hat, axis=0, keepdims=True)
            if i < 2:
                keep[i] = dn
            else:
                send[i - 2] = dn.astype(bf16)
        gain_sum[...] = jnp.broadcast_to(all_sum, gain_sum.shape)


def attention_backward(sc, d_att, p, q, k, v, normed, gmt, weights, toks, groups):
    heads, length, _ = q.shape
    block = length // 4
    width = normed.shape[1]
    lanes = np.arange(length)
    offsets = np.where(lanes < 768, lanes, lanes - length) - 128
    hot = (bucket_of(offsets)[:, None] == np.arange(128)[None, :]).astype(np.float32)
    whole = lambda *shape: pl.BlockSpec(shape, lambda b, s: (0,) * len(shape))
    qkv = (heads, length, HEAD_DIM)
    wide = 3 * heads * HEAD_DIM
    outs = [
        sds((8, 128), f32),
        sds((2, block, width), f32),
        sds((2, block, width), bf16),
        sds((8, width), f32),
    ]
    step, columns = width // groups, wide + gmt.shape[1]
    if step % 32 == 0:
        outs += [sds((groups, 32, columns), bf16), sds((groups, step - 32, columns), bf16)]
    else:
        outs += [sds((1, width, columns), bf16)]
    return pl.pallas_call(
        backward_kernel,
        grid_spec=pltpu.PrefetchScalarGridSpec(
            num_scalar_prefetch=1,
            grid=(4,),
            in_specs=[
                whole(*qkv),
                pl.BlockSpec((heads, block, length), lambda b, s: (0, b, 0)),
                whole(*qkv),
                whole(*qkv),
                whole(*qkv),
                whole(length, 128),
                whole(*normed.shape),
                whole(*gmt.shape),
                whole(*weights.shape),
            ]
            + [whole(block, width)] * 4,
            out_specs=[whole(*o.shape) for o in outs],
            scratch_shapes=[
                pltpu.VMEM((length, wide), bf16),
                pltpu.VMEM((block, length), f32),
                pltpu.VMEM((block, length), bf16),
                pltpu.VMEM((heads, HEAD_DIM, length), f32),
                pltpu.VMEM((heads, HEAD_DIM, length), f32),
                pltpu.VMEM((heads, 8, length), f32),
                pltpu.VMEM((heads, 8, length), f32),
            ],
        ),
        out_shape=outs,
        compiler_params=params(),
        cost_estimate=cost(1e6, 48e6),
        name="attention_backward",
    )(sc, d_att, p, q, k, v, jnp.asarray(hot), normed, gmt, weights, *toks)


def router_kernel(mine, recv, ta, tb, gain, wrt, routes, hidden, scaled, sums):
    rows, half = mine.shape
    block = rows // 2
    for n, tok in enumerate((ta, tb)):
        to, back = slice(n * block, (n + 1) * block), slice((1 - n) * block, (2 - n) * block)
        h = mine[to, :] + recv[back, :].astype(f32) + tok[...].astype(f32)
        hidden[to, :] = h
        scaled[to, :] = (h * gain[...]).astype(bf16)
    h = hidden[...]
    hi, lo = split_two(h * h)
    ones = jnp.ones((8, half), bf16)
    square = nt(ones, hi) + nt(ones, lo)
    logits = nt(wrt[...], scaled[...])
    ids = lax.broadcasted_iota(i32, logits.shape, 0)
    first = jnp.sum(jnp.where(ids == routes[0:1, :], logits, 0.0), axis=0, keepdims=True)
    second = jnp.sum(jnp.where(ids == routes[1:2, :], logits, 0.0), axis=0, keepdims=True)
    index = lax.broadcasted_iota(i32, square.shape, 0)
    sums[...] = jnp.where(index == 0, square, jnp.where(index == 1, first, second))


def router(mine, recv, ta, tb, gain, wrt, routes):
    rows, half = mine.shape
    outs = [sds((rows, half), f32), sds((rows, half), bf16), sds((8, rows), f32)]
    arrays = [mine, recv, ta, tb, gain, wrt, routes]
    return one_step(router_kernel, "router", 1.5, [], arrays, outs)


def pack_kernel(parts, count, slots, *refs):
    values, outs = refs[:parts], refs[parts:]
    for n, out in enumerate(outs):
        total, first = None, 0
        for ref in values:
            rows = ref.shape[0]
            at = n * count + lax.broadcasted_iota(i32, (count, rows), 0)
            lanes = slice(first, first + rows)
            hot = (slots[0:1, lanes] == at) | (slots[1:2, lanes] == at)
            part = nn(jnp.where(hot, 1.0, 0.0).astype(bf16), ref[...])
            total = part if total is None else total + part
            first += rows
        out[...] = total.astype(bf16)


def pack(values, slots, chunks, count):
    half = values[0].shape[1]
    outs = [sds((count, half), bf16)] * chunks
    kernel = functools.partial(pack_kernel, len(values), count)
    return one_step(kernel, "pack", 2.5, [], [slots, *values], outs)


def unpack_kernel(offset, slots_own, slots_other, gates_own, gates_other, rows, *refs):
    keep, send = refs[-2:]
    count = rows.shape[0]
    for j, (slots, gates, out) in enumerate(
        ((slots_own, gates_own, keep), (slots_other, gates_other, send))
    ):
        at = offset + lax.broadcasted_iota(i32, (slots.shape[0], count), 1)
        total = refs[j][...] if len(refs) > 2 else None
        for c in range(2):
            hot = jnp.where(slots[:, c : c + 1] == at, 1.0, 0.0).astype(bf16)
            part = gates[:, c : c + 1] * nn(hot, rows[...])
            total = part if total is None else total + part
        out[...] = total.astype(out.dtype)


def unpack(slots_own, slots_other, gates_own, gates_other, n, chunk, sofar, last):
    count, half = chunk.shape
    rows = slots_own.shape[0]
    outs = [sds((rows, half), f32), sds((rows, half), bf16 if last else f32)]
    arrays = [slots_own, slots_other, gates_own, gates_other, chunk, *sofar]
    kernel = functools.partial(unpack_kernel, n * count)
    return one_step(kernel, "unpack", 2.5, [], arrays, outs)


def combine_kernel(keep, recv, hidden, r, dlog, wrt, gain, dn, dots, gain_sum):
    hi, lo = split_two(dlog[...])
    d = keep[...] + recv[...].astype(f32) + nn(hi, wrt[...]) + nn(lo, wrt[...])
    dn[...] = d
    hat = hidden[...] * r[...]
    prod = d * hat
    gain_sum[...] = jnp.broadcast_to(jnp.sum(prod, axis=0, keepdims=True), gain_sum.shape)
    hi, lo = split_two(prod * gain[...])
    ones = jnp.ones((8, hi.shape[1]), bf16)
    dots[...] = nt(ones, hi) + nt(ones, lo)


def combine(keep, recv, hidden, r, dlog, wrt, gain):
    rows, half = hidden.shape
    outs = [sds((rows, half), f32), sds((8, rows), f32), sds((8, half), f32)]
    arrays = [keep, recv, hidden, r, dlog, wrt, gain]
    return one_step(combine_kernel, "combine", 2, [], arrays, outs)


def hidden_gradient_kernel(dn, hidden, r, gain, dots, recv, oa, ob, out):
    rows, half = dn.shape
    block = rows // 2
    other = jnp.concatenate([recv[0:1, block:], recv[0:1, :block]], axis=1)
    mean = row_to_column((dots[0:1, :] + other) * (0.5 / half), rows)
    rr = r[...]
    d = rr * (gain[...] * dn[...] - hidden[...] * rr * mean)
    out[:block, :] = (oa[...].astype(f32) + d[:block]).astype(bf16)
    out[block:, :] = (ob[...].astype(f32) + d[block:]).astype(bf16)


def hidden_gradient(dn, hidden, r, gain, dots, recv, oa, ob):
    arrays = [dn, hidden, r, gain, dots, recv, oa, ob]
    outs = [sds(hidden.shape, bf16)]
    return one_step(hidden_gradient_kernel, "hidden_gradient", 1.5, [], arrays, outs)[0]


def full_rows(scratch, x, a, b):
    groups, _, cap, half = a.shape
    mine = pl.ds(pl.multiple_of(x * half, 128), half)
    away = pl.ds(pl.multiple_of((1 - x) * half, 128), half)
    scratch[:, mine] = a[:, 0].astype(f32).reshape(groups * cap, half)
    scratch[:, away] = b[:, 0].astype(f32).reshape(groups * cap, half)
    return scratch[...]


def d_act_kernel(sc, da, db, w_out, d_moe, d_act, scratch):
    d = full_rows(scratch, sc[1], da, db).astype(bf16)
    d_moe[0] = d
    d_act[0] = nt(d, w_out[0]).astype(bf16)


def row_specs(groups, cap, half):
    return [pl.BlockSpec((groups, 1, cap, half), lambda i, s: (0, i, 0, 0))]


def d_act_rows(sc, da, db, w_out, virtual):
    groups, count, cap, half = da.shape
    rows, width = groups * cap, 2 * half
    local, hidden, _ = w_out.shape
    out = lambda w: pl.BlockSpec((1, rows, w), lambda i, s: (i, 0, 0))
    return pl.pallas_call(
        d_act_kernel,
        grid_spec=pltpu.PrefetchScalarGridSpec(
            num_scalar_prefetch=1,
            grid=(count,),
            in_specs=row_specs(groups, cap, half) * 2
            + [
                pl.BlockSpec(
                    (1, hidden, width), lambda i, s: ((s[0] + i) * local // virtual, 0, 0)
                )
            ],
            out_specs=[out(width), out(hidden)],
            scratch_shapes=[pltpu.VMEM((rows, width), f32)],
        ),
        out_shape=[sds((count, rows, width), bf16), sds((count, rows, hidden), bf16)],
        compiler_params=params(28),
        cost_estimate=cost(1e6, count * 5e6),
        name="d_act_rows",
    )(sc, da, db, w_out)


def expert_kernel(summing, sc, xa, xb, d_act, w_in, inv_gain, *refs):
    if summing:
        recv, normed, act_ref, d_pre_ref, dg, mine, away, scratch = refs
    else:
        normed, act_ref, d_pre_ref, dg, dr, scratch = refs
    x = sc[1]
    groups, _, cap, half = xa.shape
    rows, width = groups * cap, 2 * half
    g = full_rows(scratch, x, xa, xb)
    h = g * inv_gain[...]
    r = lax.rsqrt(jnp.sum(h * h, axis=1, keepdims=True) * (1.0 / width) + 1e-06)
    n = (g * r).astype(bf16)
    normed[0] = n
    u = nn(n, w_in[0])
    k = 0.7978845608028654
    uu = u * u
    t = jnp.tanh(u * (k + (k * 0.044715) * uu))
    a = 0.5 + 0.5 * t
    act = (u * a).astype(bf16)
    act_ref[0] = act
    slope = a + (0.5 * u) * (1.0 - t * t) * (k + (3.0 * 0.044715 * k) * uu)
    da = d_act[0].astype(f32)
    d_pre = (da * slope).astype(bf16)
    d_pre_ref[0] = d_pre
    hi, lo = split_two(act.astype(f32) * da)
    ones = jnp.ones((8, hi.shape[1]), bf16)
    dg[0] = nt(ones, hi) + nt(ones, lo)
    d = nt(d_pre, w_in[0])
    if summing:
        d = d + recv[:, 0].astype(f32).reshape(rows, width)
        lo, hi = d[:, :half], d[:, half:]
        mine[:, 0] = jnp.where(x == 0, lo, hi).reshape(groups, cap, half)
        away[:, 0] = jnp.where(x == 0, hi, lo).reshape(groups, cap, half).astype(bf16)
    else:
        dr[:, 0] = d.reshape(groups, cap, width).astype(bf16)


def experts(sc, xa, xb, d_act, first, w_in, inv_gain, virtual, recv=None):
    groups, count, cap, half = xa.shape
    rows, width = groups * cap, 2 * half
    local, _, hidden = w_in.shape
    (part,) = row_specs(groups, cap, half)
    (full,) = row_specs(groups, cap, width)
    keep = lambda w: pl.BlockSpec((1, rows, w), lambda i, s: (i, 0, 0))
    shape = (groups, count, cap)
    summing = recv is not None
    return pl.pallas_call(
        functools.partial(expert_kernel, summing),
        grid_spec=pltpu.PrefetchScalarGridSpec(
            num_scalar_prefetch=1,
            grid=(count,),
            in_specs=[
                part,
                part,
                pl.BlockSpec((1, rows, hidden), lambda i, s: (first + i, 0, 0)),
                pl.BlockSpec(
                    (1, width, hidden), lambda i, s: ((s[0] + i) * local // virtual, 0, 0)
                ),
                pl.BlockSpec((1, width), lambda i, s: (0, 0)),
            ]
            + ([full] if summing else []),
            out_specs=[
                keep(width),
                keep(hidden),
                keep(hidden),
                pl.BlockSpec((1, 8, rows), lambda i, s: (i, 0, 0)),
            ]
            + ([part, part] if summing else [full]),
            scratch_shapes=[pltpu.VMEM((rows, width), f32)],
        ),
        out_shape=[
            sds((count, rows, width), bf16),
            sds((count, rows, hidden), bf16),
            sds((count, rows, hidden), bf16),
            sds((count, 8, rows), f32),
        ]
        + (
            [sds(shape + (half,), f32), sds(shape + (half,), bf16)]
            if summing
            else [sds(shape + (width,), bf16)]
        ),
        compiler_params=params(30),
        cost_estimate=cost(1e6, count * 11e6),
        name="experts",
    )(sc, xa, xb, d_act, w_in, inv_gain, *([recv] if summing else []))


def by_chunk(index, per_chunk, body, chunks):
    for n in range(chunks):
        pl.when(index // per_chunk == n)(functools.partial(body, n))


def chunk_specs(rows, width, per_chunk, chunks):
    def at(n):
        return lambda i, s: (jnp.clip(i - n * per_chunk, 0, per_chunk - 1), 0, 0)

    return [pl.BlockSpec((1, rows, width), at(n)) for n in range(chunks)]


def expert_out_kernel(summing, per_chunk, sc, w_out, *refs):
    if summing:
        recv, acts, (mine, away) = refs[0], refs[1:-2], refs[-2:]
    else:
        acts, (y_ref,) = refs[:-1], refs[-1:]

    def body(n):
        y = nn(acts[n][0], w_out[0])
        if summing:
            groups, _, cap, half = mine.shape
            y = y + recv[:, 0].astype(f32).reshape(groups * cap, 2 * half)
            lo, hi = y[:, :half], y[:, half:]
            mine[:, 0] = jnp.where(sc[1] == 0, lo, hi).reshape(groups, cap, half)
            away[:, 0] = jnp.where(sc[1] == 0, hi, lo).reshape(groups, cap, half).astype(bf16)
        else:
            groups, _, cap, width = y_ref.shape
            y_ref[:, 0] = y.reshape(groups, cap, width).astype(bf16)

    by_chunk(pl.program_id(0), per_chunk, body, len(acts))


def expert_out(sc, w_out, acts, virtual, groups, recv=None):
    per_chunk, rows, hidden = acts[0].shape
    local, _, width = w_out.shape
    count, cap, half = per_chunk * len(acts), rows // groups, width // 2
    (part,) = row_specs(groups, cap, half)
    (full,) = row_specs(groups, cap, width)
    shape = (groups, count, cap)
    summing = recv is not None
    return pl.pallas_call(
        functools.partial(expert_out_kernel, summing, per_chunk),
        grid_spec=pltpu.PrefetchScalarGridSpec(
            num_scalar_prefetch=1,
            grid=(count,),
            in_specs=[
                pl.BlockSpec(
                    (1, hidden, width), lambda i, s: ((s[0] + i) * local // virtual, 0, 0)
                )
            ]
            + ([full] if summing else [])
            + chunk_specs(rows, hidden, per_chunk, len(acts)),
            out_specs=[part, part] if summing else [full],
        ),
        out_shape=[sds(shape + (half,), f32), sds(shape + (half,), bf16)]
        if summing
        else [sds(shape + (width,), bf16)],
        compiler_params=params(28),
        cost_estimate=cost(1e6, count * 0.4e6),
        name="expert_out",
    )(sc, w_out, *([recv] if summing else []), *acts)


def weight_gradient_kernel(sc, gate, d_moe, normed, act, d_pre, *refs):
    g_in, g_out, token = refs[-3:]
    token[...] = jnp.zeros_like(token)
    g = row_to_column(gate[0, 0:1, :], gate.shape[2])
    g_out[0] = tn((act[0].astype(f32) * g).astype(bf16), d_moe[0])
    g_in[0] = tn(normed[0], (d_pre[0].astype(f32) * g).astype(bf16))


def weight_gradient(sc, gate, d_moe, first, normed, act, d_pre, virtual, earlier, extra):
    count, rows, width = normed.shape
    hidden = act.shape[2]
    part = lambda w: pl.BlockSpec((1, rows, w), lambda i, s: (i, 0, 0))
    return pl.pallas_call(
        weight_gradient_kernel,
        grid_spec=pltpu.PrefetchScalarGridSpec(
            num_scalar_prefetch=1,
            grid=(count,),
            in_specs=[
                pl.BlockSpec((1, 8, rows), lambda i, s: (s[0] + i, 0, 0)),
                pl.BlockSpec((1, rows, width), lambda i, s: (first + i, 0, 0)),
                part(width),
                part(hidden),
                part(hidden),
            ]
            + [pl.BlockSpec(memory_space=pl.ANY)] * (len(earlier) + len(extra)),
            out_specs=[
                pl.BlockSpec((1, width, hidden), lambda i, s: (s[0] + i, 0, 0)),
                pl.BlockSpec((1, hidden, width), lambda i, s: (s[0] + i, 0, 0)),
                pl.BlockSpec((8, 128), lambda i, s: (0, 0)),
            ],
        ),
        out_shape=[
            sds((virtual, width, hidden), f32),
            sds((virtual, hidden, width), f32),
            sds((8, 128), f32),
        ],
        input_output_aliases={6 + n: n for n in range(len(earlier))},
        compiler_params=params(),
        cost_estimate=cost(1e6, count * 8e6),
        name="weight_gradient",
    )(sc, gate, d_moe, normed, act, d_pre, *earlier, *extra)


def together(*values):
    return lax.optimization_barrier(values)


def per_device(
    tokens,
    gain_one,
    w_qkv,
    rel_table,
    w_mix,
    gain_two,
    w_router,
    w_in,
    w_out,
    routes,
    buffer_row_index,
    image_starts,
    d_output,
):
    block, width = tokens.shape
    tensor_count = lax.axis_size("tensor")
    tensor_index = lax.axis_index("tensor")
    groups = lax.axis_size("dp")
    cx, cc = tensor_index // 2, tensor_index % 2
    length = block * tensor_count
    heads = rel_table.shape[0] // tensor_count
    head_width = heads * HEAD_DIM
    local = w_in.shape[0]
    half = width // 2
    virtual = max(local, 2)
    per_half = virtual // 2
    cap = CAP * local // virtual
    vcap = cap if cap % 8 == 0 else -(-cap // 16) * 16
    chunks = 2 if per_half % 2 == 0 else 1
    per_chunk = per_half // chunks
    chunk_slots = groups * per_chunk * vcap
    half_slots = chunks * chunk_slots

    sc = jnp.concatenate([image_starts[0], jnp.stack([cx, cc]).astype(i32)])

    def feat(v, axis, side):
        return lax.dynamic_slice_in_dim(v, side * half, half, axis)

    shard = jnp.concatenate([w_qkv[0], w_qkv[1], w_qkv[2], w_mix.T], axis=1)
    weights = gather_dp(shard).reshape(width, 4 * head_width)
    tok_x = swap_x(tokens)
    tok_c = swap_core(tokens)
    tok_d = swap_core(tok_x)
    toks = (tokens, tok_x, tok_c, tok_d)

    bias_table = lax.dynamic_slice_in_dim(rel_table, tensor_index * heads, heads, 0)
    hot = bucket_of(np.arange(2 * length) - length)[None, :] == np.arange(rel_table.shape[1])[:, None]
    bvec = jnp.dot(bias_table * LOG2E, jnp.asarray(hot.astype(np.float32)), precision=highest)
    bvec = jnp.pad(bvec, ((0, 8 - heads), (0, 0)))

    def slot_parts(route, index):
        flat = route * CAP + index
        expert_v, row_v = flat // cap, flat % cap
        group_v, v_v = expert_v // virtual, expert_v % virtual
        half_v, v2_v = v_v // per_half, v_v % per_half
        chunk_v, vc_v = v2_v // per_chunk, v2_v % per_chunk
        in_half = chunk_v * chunk_slots + (group_v * per_chunk + vc_v) * vcap + row_v
        whole_half = (group_v * per_half + v2_v) * vcap + row_v
        is_mine = half_v == cc
        return (
            jnp.where(is_mine, in_half, -1),
            jnp.where(is_mine, whole_half, -1),
            (group_v * virtual + v_v) * vcap + row_v,
        )

    def relative(v):
        at = [2 * (cx ^ (n % 2)) + (cc ^ (n // 2)) for n in range(4)]
        return jnp.concatenate([lax.dynamic_slice_in_dim(v, a * block, block, 0) for a in at], 0)

    routes_rel = relative(routes)
    slots_rel, whole_rel, both_rel = slot_parts(routes_rel, relative(buffer_row_index))
    slots_own, slots_other = slots_rel[: 2 * block], slots_rel[2 * block :]
    whole_own, whole_other = whole_rel[: 2 * block], whole_rel[2 * block :]
    routes_own = routes_rel[: 2 * block]

    do_a = feat(d_output, 1, cx)
    do_b = swap_x(feat(d_output, 1, 1 - cx))
    (d_packed,) = pack((do_a, do_b, swap_core(do_a), swap_core(do_b)), whole_rel.T, 1, half_slots)
    d_packed, weights = lax.optimization_barrier((d_packed, weights))
    da = exchange(d_packed.reshape(groups, per_half, vcap, half))

    normed, q, k, v, att, probs, keep, send = attention_forward(
        sc, toks, gain_one[None], weights, bvec, heads
    )
    chip_mine, chip_away = chip_sum(sc, keep, swap_core(send))
    gain_half = feat(gain_two, 0, cx)[None]
    wrt_half = feat(w_router, 0, cx).T
    hidden, scaled, sums = router(
        chip_mine,
        swap_x(chip_away),
        feat(tokens, 1, cx),
        feat(tok_x, 1, cx),
        gain_half,
        wrt_half,
        routes_own.T,
    )
    db = swap_x(da)
    dc, dd = swap_core(da), swap_core(db)
    base_own = cc * per_half
    base_other = (1 - cc) * per_half
    call_own = jnp.stack([base_own, cx]).astype(i32)
    call_other = jnp.stack([base_other, cx]).astype(i32)
    d_moe_own, d_act_own = d_act_rows(call_own, da, db, w_out, virtual)
    d_moe_other, d_act_other = d_act_rows(call_other, dc, dd, w_out, virtual)

    rows_in = []
    for rows in pack((scaled, swap_core(scaled)), slots_rel.T, chunks, chunk_slots):
        if rows_in:
            rows, db = together(rows, db)
        a = exchange(rows.reshape(groups, per_chunk, vcap, half))
        if rows_in:
            a, d_act_other, d_act_own = together(a, d_act_other, d_act_own)
        b = swap_x(a)
        rows_in.append((a, b, swap_core(a)))

    def flip(v):
        return jnp.concatenate([v[:, block:], v[:, :block]], axis=1)

    sums = sums + flip(swap_x(sums))
    sums_other = swap_core(sums)

    def token_parts(v):
        r = lax.rsqrt(v[0] / width + 1e-06)
        return r, jax.nn.softmax(r[:, None] * v[1:3].T, axis=-1)

    r_own, gates_own = token_parts(sums)
    r_other, gates_other = token_parts(sums_other)
    r_own = r_own[:, None]
    gates_all = jnp.concatenate([gates_own, gates_other], 0)
    def one_hots(slots):
        experts_hot = slots[:, :, None] // vcap == jnp.arange(groups * virtual, dtype=i32)
        rows_hot = slots[:, :, None] % vcap == jnp.arange(vcap, dtype=i32)
        return experts_hot.astype(f32), rows_hot.astype(f32)

    experts_hot, rows_hot = one_hots(both_rel)
    gate_slots = jnp.einsum(
        "tce,tcr->er", experts_hot * gates_all[:, :, None], rows_hot, precision=highest
    )
    gate_send = gate_slots.reshape(groups, 1, virtual * vcap)

    inv_gain = (1.0 / gain_two)[None]
    others, owns, dr_recvs = [], [], []
    for n in range(chunks):
        first = n * per_chunk
        _, b, xc = rows_in[n]
        if others:
            b, others[-1][4] = together(b, others[-1][4])
        xd = swap_core(b)
        if n == 0:
            xc, d_act_own = lax.optimization_barrier((xc, d_act_own))
        call = call_other + jnp.asarray([first, 0], i32)
        others.append(list(experts(call, xc, xd, d_act_other, first, w_in, inv_gain, virtual)))
    for n in range(chunks):
        first = n * per_chunk
        xa, xb = rows_in[n][:2]
        call = call_own + jnp.asarray([first, 0], i32)
        if owns:
            xa, owns[-1][3] = together(xa, owns[-1][3])
        out = experts(
            call, xa, xb, d_act_own, first, w_in, inv_gain, virtual, swap_core(others[n][4])
        )
        owns.append(list(out))
        dr_recvs.append(swap_x(out[5]))

    dr_send = [(o[4] + v.astype(f32)).astype(bf16) for o, v in zip(owns, dr_recvs)]
    if chunks > 1:
        dr_send[0], others[0][1], others[1][1], owns[-1][3] = together(
            dr_send[0], others[0][1], others[1][1], owns[-1][3]
        )
    own_dg = jnp.concatenate([o[3][:, 0] for o in owns], 0)
    other_dg = jnp.concatenate([o[3][:, 0] for o in others], 0)
    dg = jnp.where(
        cc == 0, jnp.concatenate([own_dg, other_dg], 0), jnp.concatenate([other_dg, own_dg], 0)
    )
    dg = jnp.moveaxis(dg.reshape(virtual, groups, vcap), 0, 1).reshape(groups, 1, virtual * vcap)
    dg = dg + swap_core(dg)
    dg = dg + swap_x(dg)

    acts = [o[1] for o in others]
    (y_other,) = expert_out(call_other, w_out, acts, virtual, groups)
    dr_send[-1], dg, owns[0][1] = together(dr_send[-1], dg, owns[0][1])
    acts = [o[1] for o in owns]
    y_mine, y_away = expert_out(call_own, w_out, acts, virtual, groups, swap_core(y_other))
    dr_back = []
    if chunks > 1:
        first_back, y_away = together(exchange(dr_send[0]), y_away)
        dr_back.append(first_back)
    dr_send[-1], y_away = together(dr_send[-1], y_away)
    both = jnp.concatenate([gate_send, dg], axis=2)
    dr_send[-1], both = together(dr_send[-1], both)
    y = (y_mine + swap_x(y_away).astype(f32)).astype(bf16)
    dr_back.append(exchange(dr_send[-1]))
    dr_back = [v.reshape(chunk_slots, half) for v in dr_back]
    unpack_args = (slots_own, slots_other, gates_own, gates_other)
    sofar = []
    for n in range(chunks - 1):
        sofar = list(unpack(*unpack_args, n, dr_back[n], sofar, False))
    if sofar:
        both, sofar[0] = together(both, sofar[0])
    both = exchange_small(both)
    gate_rows, dg = both[:, 0, : virtual * vcap], both[:, 0, virtual * vcap :]
    gate_rows = jnp.moveaxis(gate_rows.reshape(groups, virtual, vcap), 1, 0)
    gate_rows = jnp.broadcast_to(
        gate_rows.reshape(virtual, 1, groups * vcap), (virtual, 8, groups * vcap)
    )
    dg = dg.reshape(groups * virtual, vcap)

    def to_tokens(slots):
        ehot = (slots[:, None] // vcap == jnp.arange(groups * virtual, dtype=i32)).astype(f32)
        rhot = (slots[:, None] % vcap == jnp.arange(vcap, dtype=i32)).astype(f32)
        return jnp.sum(jnp.dot(ehot, dg, precision=highest) * rhot, axis=1)

    both_own = both_rel[: 2 * block]
    dg_own = jnp.stack([to_tokens(both_own[:, c]) for c in range(2)], axis=1)
    d_chosen = gates_own * (dg_own - jnp.sum(gates_own * dg_own, axis=-1, keepdims=True))
    selectors = (routes_own[:, :, None] == jnp.arange(EXPERTS, dtype=i32)).astype(f32)
    d_logits = jnp.sum(d_chosen[:, :, None] * selectors, axis=1)
    nt_own = (scaled.astype(f32) * r_own).astype(bf16)
    grad_router = jnp.dot(nt_own.astype(f32).T, d_logits, precision=highest)

    dr_last, d_logits = lax.optimization_barrier((dr_back[-1], d_logits))
    keep_d, send_d = unpack(*unpack_args, chunks - 1, dr_last, sofar, True)
    dn, dots, gain_two_sum = combine(
        keep_d, swap_core(send_d), hidden, r_own, d_logits, wrt_half, gain_half
    )
    dn, y = lax.optimization_barrier((dn, y))
    y_back = exchange(y).reshape(half_slots, half)
    d_mixed = hidden_gradient(dn, hidden, r_own, gain_half, dots, swap_x(dots), do_a, do_b)
    pieces = [
        (call, first * per_chunk, d_moe, o)
        for call, d_moe, gone in ((call_own, d_moe_own, owns), (call_other, d_moe_other, others))
        for first, o in enumerate(gone)
    ]

    def weight_part(piece, earlier, extra):
        call, first, d_moe, o = piece
        at = call + jnp.asarray([first, 0], i32)
        *earlier, token = weight_gradient(
            at, gate_rows, d_moe, first, *o[:3], virtual, earlier, extra
        )
        return earlier, token

    def held(piece, *others):
        call, first, d_moe, o = piece
        act, *others = together(o[1], *others)
        return ((call, first, d_moe, (o[0], act, o[2])), *others)

    pieces[0], d_mixed = held(pieces[0], d_mixed)
    grads, token = weight_part(pieces[0], [], [])
    d_mixed_x, token = together(swap_x(d_mixed), token)
    d_hidden, gmt, d_att = mix_backward(
        sc, (d_mixed, d_mixed_x, swap_core(d_mixed), swap_core(d_mixed_x)), weights, att, heads
    )

    d_att, y_back = lax.optimization_barrier((d_att, y_back))
    table, keep_n, send_n, gain_one_sum, *grad_w = attention_backward(
        sc, d_att, probs, q, k, v, normed, gmt, weights, toks, groups
    )

    grad_w = [v.reshape(groups, -1, v.shape[-1]) for v in grad_w]
    middle = len(pieces) - 1
    for n in range(1, middle):
        pieces[n], grad_w[-1] = held(pieces[n], grad_w[-1])
        grads, token = weight_part(pieces[n], grads, [token])
    grad_w[0] = exchange(grad_w[0])
    if len(grad_w) > 1:
        grad_w[0], grad_w[1], token, send_n, gain_one_sum, y_back = together(
            grad_w[0], grad_w[1], token, send_n, gain_one_sum, y_back
        )
        grad_w[1] = exchange(grad_w[1])
    grad_w = jnp.concatenate(grad_w, axis=1) if len(grad_w) > 1 else grad_w[0]
    d_norm = keep_n + swap_core(send_n).astype(f32)
    norm_send = d_norm[1].astype(bf16)
    pieces[-1], norm_send, y_back, gain_one_sum = held(
        pieces[-1], norm_send, y_back, gain_one_sum
    )
    d_norm = d_norm[0] + swap_x(norm_send).astype(f32)
    t = tokens.astype(f32)
    r = lax.rsqrt(jnp.mean(t * t, axis=-1, keepdims=True) + 1e-06)
    gd = gain_one * d_norm
    hat = t * r
    grad_input = d_hidden.astype(f32) + r * (gd - hat * jnp.mean(gd * hat, axis=-1, keepdims=True))
    grad_w = jnp.sum(grad_w.astype(f32), axis=0)
    grad_qkv = jnp.stack([grad_w[:, j * head_width : (j + 1) * head_width] for j in range(3)])
    grad_mix = grad_w[:, 3 * head_width :].T

    def sum_dp(v):
        step = 1
        while step < groups:
            v = v + lax.ppermute(v, "dp", [(i, i ^ step) for i in range(groups)])
            step *= 2
        return v

    table = lax.dynamic_update_slice_in_dim(
        jnp.zeros(rel_table.shape, f32), table[:heads, : rel_table.shape[1]], tensor_index * heads, 0
    )
    small = jnp.concatenate(
        [gain_one_sum[0], table.reshape(-1), gain_two_sum[0], grad_router.reshape(-1)]
    )
    small = sum_dp(small.reshape(-1, 128))
    small = small + swap_core(small)
    small_x = swap_x(small).reshape(-1)
    small = small.reshape(-1)
    cut = width + rel_table.size
    last = small[:cut] + small_x[:cut]
    grad_gain_one, grad_table = last[:width], last[width:].reshape(rel_table.shape)
    small, small_x = small[cut:], small_x[cut:]
    small = jnp.where(cx == 0, jnp.stack([small, small_x]), jnp.stack([small_x, small]))
    grad_gain_two = small[:, :half].reshape(width)
    grad_router = small[:, half:].reshape(width, EXPERTS)

    (g_in, g_out), _ = weight_part(pieces[-1], grads, [token])
    if virtual != local:
        hidden_units = w_in.shape[2]
        g_in = jnp.sum(g_in.reshape(local, virtual // local, width, hidden_units), axis=1)
        g_out = jnp.sum(g_out.reshape(local, virtual // local, hidden_units, width), axis=1)

    keep_y, send_y = unpack(
        whole_own, whole_other, gates_own, gates_other, 0, y_back, [], True
    )
    out = (hidden + keep_y + swap_core(send_y).astype(f32)).astype(bf16)
    out_recv = swap_x(out[block:])
    output = jnp.where(
        cx == 0,
        jnp.concatenate([out[:block], out_recv], 1),
        jnp.concatenate([out_recv, out[:block]], 1),
    )
    return (
        output,
        grad_input,
        grad_gain_one,
        grad_qkv,
        grad_table,
        grad_mix,
        grad_gain_two,
        grad_router,
        g_in,
        g_out,
    )


def solution(mesh):
    in_specs = (
        P(("dp", "tensor"), None),
        P(),
        P(None, "dp", "tensor"),
        P(),
        P("tensor", "dp"),
        P(),
        P(),
        P("dp", None, "tensor"),
        P("dp", "tensor", None),
        P("dp", None),
        P("dp", None),
        P("dp", None),
        P(("dp", "tensor"), None),
    )
    out_specs = (
        P(("dp", "tensor"), None),
        P(("dp", "tensor"), None),
        P(),
        P(None, "dp", "tensor"),
        P(),
        P("tensor", "dp"),
        P(),
        P(),
        P("dp", None, "tensor"),
        P("dp", "tensor", None),
    )
    return jax.shard_map(
        per_device, mesh=mesh, in_specs=in_specs, out_specs=out_specs, check_vma=False
    )
```

```python
import functools

import jax
import jax.numpy as jnp
import numpy as np
from jax import lax
from jax.experimental import pallas as pl
from jax.experimental.pallas import tpu as pltpu
from jax.sharding import PartitionSpec as P

HEAD_DIM = 64
EXPERTS = 64
SPAN = 256
CAP = 40
LOG2E = 1.4426950408889634
NEG = -1e30
bucket_edges = (1, 2, 3, 4, 5, 6, 7, 8, 11, 16, 23, 32, 45, 64, 91)
highest = lax.Precision.HIGHEST
f32 = jnp.float32
bf16 = jnp.bfloat16
i32 = jnp.int32
MIB = 1 << 20


def bucket_of(offsets):
    magnitude = np.abs(offsets)
    levels = np.zeros(offsets.shape, np.int32)
    for threshold in bucket_edges:
        levels = levels + (magnitude >= threshold).astype(np.int32)
    return levels + (len(bucket_edges) + 1) * (offsets > 0).astype(np.int32)


def nn(a, b):
    return jnp.dot(a, b, preferred_element_type=f32)


def nt(a, b):
    return lax.dot_general(a, b, (((1,), (1,)), ((), ())), preferred_element_type=f32)


def tn(a, b):
    return lax.dot_general(a, b, (((0,), (0,)), ((), ())), preferred_element_type=f32)


def split_two(v):
    hi = v.astype(bf16)
    return hi, (v - hi.astype(f32)).astype(bf16)


def swap_core(v):
    return lax.ppermute(v, "tensor", [(i, i ^ 1) for i in range(lax.axis_size("tensor"))])


def swap_x(v):
    return lax.ppermute(v, "tensor", [(i, i ^ 2) for i in range(lax.axis_size("tensor"))])


def exchange(v):
    return lax.all_to_all(v, "dp", 0, 0, tiled=True)


def exchange_small(v):
    groups = lax.axis_size("dp")
    order = jnp.arange(groups) ^ lax.axis_index("dp")
    v = jnp.take(v, order, axis=0)
    step = 1
    while step < groups:
        shape = v.shape
        v = v.reshape((groups // (2 * step), 2, step) + shape[1:])
        moved = lax.ppermute(v[:, 1], "dp", [(i, i ^ step) for i in range(groups)])
        v = jnp.stack([v[:, 0], moved], axis=1).reshape(shape)
        step *= 2
    return jnp.take(v, order, axis=0)


def gather_dp(v):
    groups = lax.axis_size("dp")
    return exchange(jnp.broadcast_to(v[None], (groups,) + v.shape))


def smem():
    return pl.BlockSpec(memory_space=pltpu.SMEM)


def sds(shape, dtype):
    return jax.ShapeDtypeStruct(shape, dtype)


def one_step(kernel, name, us, scalars, arrays, outs, scratch=(), mib=20):
    def whole(v):
        return pl.BlockSpec(v.shape, lambda i: (0,) * len(v.shape))

    return pl.pallas_call(
        kernel,
        grid=(1,),
        in_specs=[smem() for _ in scalars] + [whole(v) for v in arrays],
        out_specs=[whole(v) for v in outs],
        out_shape=list(outs),
        scratch_shapes=list(scratch),
        compiler_params=params(mib),
        cost_estimate=cost(1e6, us * 3e6),
        name=name,
    )(*scalars, *arrays)


def params(mib=62):
    return pltpu.CompilerParams(vmem_limit_bytes=62 * MIB)


def cost(flops, nbytes):
    return pl.CostEstimate(flops=int(600 * nbytes), bytes_accessed=int(nbytes), transcendentals=0)


def row_to_column(row, n):
    a = lax.broadcasted_iota(i32, (n, n), 0)
    b = lax.broadcasted_iota(i32, (n, n), 1)
    return jnp.sum(jnp.where(a == b, row, 0.0), axis=1, keepdims=True)


def quarter_rows(sc, flip_x, flip_c, block):
    at = 2 * (sc[2] ^ flip_x) + (sc[3] ^ flip_c)
    return pl.ds(pl.multiple_of(at * block, block), block)


def forward_kernel(
    sc, ta, tb, tc, td, gain, weights, bvec, normed, q, k, v, att, p_out, keep, send, toep, score, mask
):
    b = pl.program_id(0)
    block = att.shape[0]
    length = 4 * block
    heads = q.shape[0]
    blocks = length // block

    @pl.when(b == 0)
    def _():
        for i, ref in enumerate((ta, tb, tc, td)):
            rows = quarter_rows(sc, i % 2, i // 2, block)
            t = ref[...].astype(f32)
            n = t * lax.rsqrt(jnp.mean(t * t, axis=-1, keepdims=True) + 1e-06) * gain[...]
            n = n.astype(bf16)
            normed[rows, :] = n
            pr = nn(n, weights[:, : 3 * heads * HEAD_DIM]).astype(bf16)
            for h in range(heads):
                for j, out in enumerate((q, k, v)):
                    at = (j * heads + h) * HEAD_DIM
                    out[h, rows, :] = pr[:, at : at + HEAD_DIM]
        for h in range(heads):
            row = jnp.broadcast_to(bvec[h : h + 1, :], (8, 2 * length))
            for a in range(0, block, 8):
                toep[h, a : a + 8, :] = pltpu.roll(row, a, 1, stride=1, stride_axis=0)

    s0, s1, x, c = sc[0], sc[1], sc[2], sc[3]
    rc = 16

    def one_block(bs):
        r0 = bs * block
        kv = min(r0 + 2 * block, length)
        wide = kv - r0
        ii = r0 + lax.broadcasted_iota(i32, (block, wide), 0)
        jj = r0 + lax.broadcasted_iota(i32, (block, wide), 1)
        first = (ii >= s0) & (ii < s0 + SPAN) & (jj >= s0) & (jj < s0 + SPAN)
        second = (ii >= s1) & (ii < s1 + SPAN) & (jj >= s1) & (jj < s1 + SPAN)
        mask[:, :wide] = jnp.where((jj <= ii) | first | second, 0.0, NEG)
        for h in range(heads):
            score[:, :kv] = nt(q[h, r0 : r0 + block, :], k[h, :kv, :])
            for i in range(block // rc):
                rows = slice(i * rc, (i + 1) * rc)
                s = score[rows, :kv] * (HEAD_DIM ** (-0.5) * LOG2E)
                s = s + toep[h, rows, length - r0 : length - r0 + kv]
                right = s[:, r0:] + mask[rows, :wide]
                s = right if r0 == 0 else jnp.concatenate([s[:, :r0], right], axis=1)
                e = jnp.exp2(s - jnp.max(s, axis=1, keepdims=True))
                total = jnp.sum(e, axis=1, keepdims=True)
                p_out[h, rows, :kv] = (e * (1.0 / total)).astype(bf16)
            att[:, h * HEAD_DIM : (h + 1) * HEAD_DIM] = nn(p_out[h, :, :kv], v[h, :kv, :]).astype(
                bf16
            )
        mixed = nt(att[...], weights[:, 3 * heads * HEAD_DIM :])

        @pl.when(c == bs % 2)
        def _():
            keep[(bs // 2) ^ x] = mixed

        @pl.when(c != bs % 2)
        def _():
            send[(bs // 2) ^ x] = mixed.astype(bf16)

    for bs in range(blocks):
        pl.when(b == bs)(functools.partial(one_block, bs))


def attention_forward(sc, toks, gain, weights, bvec, heads):
    block, width = toks[0].shape
    length = 4 * block
    whole = lambda *shape: pl.BlockSpec(shape, lambda b, s: (0,) * len(shape))
    qkv = (heads, length, HEAD_DIM)
    return pl.pallas_call(
        forward_kernel,
        grid_spec=pltpu.PrefetchScalarGridSpec(
            num_scalar_prefetch=1,
            grid=(4,),
            in_specs=[whole(block, width)] * 4
            + [
                whole(1, width),
                whole(*weights.shape),
                whole(*bvec.shape),
            ],
            out_specs=[
                whole(length, width),
                whole(*qkv),
                whole(*qkv),
                whole(*qkv),
                pl.BlockSpec((block, heads * HEAD_DIM), lambda b, s: (b, 0)),
                pl.BlockSpec((heads, block, length), lambda b, s: (0, b, 0)),
                whole(2, block, width),
                whole(2, block, width),
            ],
            scratch_shapes=[
                pltpu.VMEM((heads, block, 2 * length), f32),
                pltpu.VMEM((block, length), f32),
                pltpu.VMEM((block, 2 * block), f32),
            ],
        ),
        out_shape=[
            sds((length, width), bf16),
            sds(qkv, bf16),
            sds(qkv, bf16),
            sds(qkv, bf16),
            sds((length, heads * HEAD_DIM), bf16),
            sds((heads, length, length), bf16),
            sds((2, block, width), f32),
            sds((2, block, width), bf16),
        ],
        compiler_params=params(40),
        cost_estimate=cost(1e6, 48e6),
        name="attention_forward",
    )(sc, *toks, gain, weights, bvec)


def chip_sum_kernel(sc, keep, recv, mine, away):
    half = mine.shape[1]
    x = sc[2]
    total = (keep[...] + recv[...].astype(f32)).reshape(mine.shape[0], 2 * half)
    lo, hi = total[:, :half], total[:, half:]
    mine[...] = jnp.where(x == 0, lo, hi)
    away[...] = jnp.where(x == 0, hi, lo).astype(bf16)


def chip_sum(sc, keep, recv):
    _, block, width = keep.shape
    shape = (2 * block, width // 2)
    outs = [sds(shape, f32), sds(shape, bf16)]
    return one_step(chip_sum_kernel, "chip_sum", 1.5, [sc], [keep, recv], outs)


def mix_backward_kernel(sc, da, db, dc, dd, weights, att, own, gmt, d_att, dmx):
    x = sc[2]
    rows, half = da.shape
    block = rows // 2
    heads = d_att.shape[0]
    for ref, flip_x, flip_c, side in ((da, 0, 0, x), (db, 1, 0, 1 - x), (dc, 0, 1, x), (dd, 1, 1, 1 - x)):
        for n in range(2):
            to = quarter_rows(sc, n ^ flip_x, flip_c, block)
            lanes = pl.ds(pl.multiple_of(side * half, 128), half)
            dmx[to, lanes] = ref[n * block : (n + 1) * block, :]
    own[...] = dmx[quarter_rows(sc, 0, 0, block), :]
    d = nn(dmx[...], weights[:, 3 * heads * HEAD_DIM :]).astype(bf16)
    for h in range(heads):
        d_att[h] = d[:, h * HEAD_DIM : (h + 1) * HEAD_DIM]
    gmt[...] = tn(dmx[...], att[...]).astype(bf16)


def mix_backward(sc, pieces, weights, att, heads):
    rows, half = pieces[0].shape
    block, length, width = rows // 2, 2 * rows, 2 * half
    outs = [
        sds((block, width), bf16),
        sds((width, heads * HEAD_DIM), bf16),
        sds((heads, length, HEAD_DIM), bf16),
    ]
    scratch = [pltpu.VMEM((length, width), bf16)]
    arrays = [*pieces, weights, att]
    return one_step(mix_backward_kernel, "mix_backward", 3, [sc], arrays, outs, scratch)


def backward_kernel(
    sc,
    d_att,
    p,
    q,
    k,
    v,
    hot,
    normed,
    gmt,
    weights,
    ta,
    tb,
    tc,
    td,
    tab,
    keep,
    send,
    gain_sum,
    *refs,
):
    gws = refs[:-7]
    dproj, score, ds_ref, dkt, dvt, diag, left = refs[-7:]
    b = pl.program_id(0)
    heads, length, _ = q.shape
    block = p.shape[1]
    blocks = length // block
    scale = HEAD_DIM ** (-0.5)
    rc = 16
    margin = 128

    @pl.when(b == 0)
    def _():
        dkt[...] = jnp.zeros_like(dkt)
        dvt[...] = jnp.zeros_like(dvt)
        diag[...] = jnp.zeros_like(diag)
        left[...] = jnp.zeros_like(left)

    def one_block(bs):
        r0 = bs * block
        kv = min(r0 + 2 * block, length)
        lo = max(r0 - margin, 0)
        ones = jnp.ones((8, block), bf16)
        for h in range(heads):
            d_out = d_att[h, r0 : r0 + block, :]
            score[:, :kv] = nt(d_out, v[h, :kv, :])

            for i in range(block // rc):
                rows = slice(i * rc, (i + 1) * rc)
                pr = p[h, rows, :kv].astype(f32)
                pd = pr * score[rows, :kv]
                ds = pd - pr * jnp.sum(pd, axis=1, keepdims=True)
                ds_ref[rows, :kv] = ds.astype(bf16)
                parts = [ds[:, lo:kv]]
                before = margin + lo - r0
                after = length - before - (kv - lo)
                if before:
                    parts.insert(0, jnp.zeros((rc, before), f32))
                if after:
                    parts.append(jnp.zeros((rc, after), f32))
                band = jnp.concatenate(parts, axis=1)
                for g in range(rc // 8):
                    shift = (length - (i * rc + 8 * g)) % length
                    diag[h] += pltpu.roll(band[8 * g : 8 * g + 8], shift, 1)
            at = h * HEAD_DIM
            dq = nn(ds_ref[:, :kv], k[h, :kv, :]) * scale
            dproj[r0 : r0 + block, at : at + HEAD_DIM] = dq.astype(bf16)
            dkt[h, :, :kv] += tn(q[h, r0 : r0 + block, :], ds_ref[:, :kv])
            dvt[h, :, :kv] += tn(d_out, p[h, :, :kv])
            if lo > 0:
                left[h, :, :lo] += nn(ones, ds_ref[:, :lo])

    for bs in range(blocks):
        pl.when(b == bs)(functools.partial(one_block, bs))

    @pl.when(b == blocks - 1)
    def _():
        lane = lax.broadcasted_iota(i32, (1, 128), 1)
        for h in range(heads):
            at = (heads + h) * HEAD_DIM
            dproj[:, at : at + HEAD_DIM] = (dkt[h] * scale).T.astype(bf16)
            at = (2 * heads + h) * HEAD_DIM
            dproj[:, at : at + HEAD_DIM] = dvt[h].T.astype(bf16)
            total = jnp.zeros((1, length), f32)
            for s in range(8):
                total = total + pltpu.roll(diag[h, s : s + 1, :], (length - s) % length, 1)
            far = jnp.sum(left[h, 0:1, :])
            row = jnp.dot(
                jnp.broadcast_to(total, (8, length)),
                hot[...],
                precision=highest,
                preferred_element_type=f32,
            )
            tab[h : h + 1, :] = row[0:1] + jnp.where(lane == len(bucket_edges), far, 0.0)
        gw = tn(normed[...], dproj[...]).astype(bf16)
        step = sum(ref.shape[1] for ref in gws)
        first = 0
        for ref in gws:
            for n in range(ref.shape[0]):
                rows = slice(n * step + first, n * step + first + ref.shape[1])
                ref[n, :, : dproj.shape[1]] = gw[rows]
                ref[n, :, dproj.shape[1] :] = gmt[rows, :]
            first += ref.shape[1]
        all_sum = jnp.zeros((1, weights.shape[0]), f32)
        wq = weights[:, : dproj.shape[1]]
        for i, ref in enumerate((ta, tb, tc, td)):
            dn = nt(dproj[quarter_rows(sc, i % 2, i // 2, block), :], wq)
            t = ref[...].astype(f32)
            hat = t * lax.rsqrt(jnp.mean(t * t, axis=-1, keepdims=True) + 1e-06)
            all_sum = all_sum + jnp.sum(dn * hat, axis=0, keepdims=True)
            if i < 2:
                keep[i] = dn
            else:
                send[i - 2] = dn.astype(bf16)
        gain_sum[...] = jnp.broadcast_to(all_sum, gain_sum.shape)


def attention_backward(sc, d_att, p, q, k, v, normed, gmt, weights, toks, groups):
    heads, length, _ = q.shape
    block = length // 4
    width = normed.shape[1]
    lanes = np.arange(length)
    offsets = np.where(lanes < 768, lanes, lanes - length) - 128
    hot = (bucket_of(offsets)[:, None] == np.arange(128)[None, :]).astype(np.float32)
    whole = lambda *shape: pl.BlockSpec(shape, lambda b, s: (0,) * len(shape))
    qkv = (heads, length, HEAD_DIM)
    wide = 3 * heads * HEAD_DIM
    outs = [
        sds((8, 128), f32),
        sds((2, block, width), f32),
        sds((2, block, width), bf16),
        sds((8, width), f32),
    ]
    step, columns = width // groups, wide + gmt.shape[1]
    if step % 32 == 0:
        outs += [sds((groups, step, columns), bf16)]
    else:
        outs += [sds((1, width, columns), bf16)]
    return pl.pallas_call(
        backward_kernel,
        grid_spec=pltpu.PrefetchScalarGridSpec(
            num_scalar_prefetch=1,
            grid=(4,),
            in_specs=[
                whole(*qkv),
                pl.BlockSpec((heads, block, length), lambda b, s: (0, b, 0)),
                whole(*qkv),
                whole(*qkv),
                whole(*qkv),
                whole(length, 128),
                whole(*normed.shape),
                whole(*gmt.shape),
                whole(*weights.shape),
            ]
            + [whole(block, width)] * 4,
            out_specs=[whole(*o.shape) for o in outs],
            scratch_shapes=[
                pltpu.VMEM((length, wide), bf16),
                pltpu.VMEM((block, length), f32),
                pltpu.VMEM((block, length), bf16),
                pltpu.VMEM((heads, HEAD_DIM, length), f32),
                pltpu.VMEM((heads, HEAD_DIM, length), f32),
                pltpu.VMEM((heads, 8, length), f32),
                pltpu.VMEM((heads, 8, length), f32),
            ],
        ),
        out_shape=outs,
        compiler_params=params(),
        cost_estimate=cost(1e6, 48e6),
        name="attention_backward",
    )(sc, d_att, p, q, k, v, jnp.asarray(hot), normed, gmt, weights, *toks)


def router_kernel(mine, recv, ta, tb, gain, wrt, routes, hidden, scaled, sums):
    rows, half = mine.shape
    block = rows // 2
    for n, tok in enumerate((ta, tb)):
        to, back = slice(n * block, (n + 1) * block), slice((1 - n) * block, (2 - n) * block)
        h = mine[to, :] + recv[back, :].astype(f32) + tok[...].astype(f32)
        hidden[to, :] = h
        scaled[to, :] = (h * gain[...]).astype(bf16)
    h = hidden[...]
    hi, lo = split_two(h * h)
    ones = jnp.ones((8, half), bf16)
    square = nt(ones, hi) + nt(ones, lo)
    logits = nt(wrt[...], scaled[...])
    ids = lax.broadcasted_iota(i32, logits.shape, 0)
    first = jnp.sum(jnp.where(ids == routes[0:1, :], logits, 0.0), axis=0, keepdims=True)
    second = jnp.sum(jnp.where(ids == routes[1:2, :], logits, 0.0), axis=0, keepdims=True)
    index = lax.broadcasted_iota(i32, square.shape, 0)
    sums[...] = jnp.where(index == 0, square, jnp.where(index == 1, first, second))


def router(mine, recv, ta, tb, gain, wrt, routes):
    rows, half = mine.shape
    outs = [sds((rows, half), f32), sds((rows, half), bf16), sds((8, rows), f32)]
    arrays = [mine, recv, ta, tb, gain, wrt, routes]
    return one_step(router_kernel, "router", 1.5, [], arrays, outs)


def pack_kernel(parts, count, slots, *refs):
    values, outs = refs[:parts], refs[parts:]
    for n, out in enumerate(outs):
        total, first = None, 0
        for ref in values:
            rows = ref.shape[0]
            at = n * count + lax.broadcasted_iota(i32, (count, rows), 0)
            lanes = slice(first, first + rows)
            hot = (slots[0:1, lanes] == at) | (slots[1:2, lanes] == at)
            part = nn(jnp.where(hot, 1.0, 0.0).astype(bf16), ref[...])
            total = part if total is None else total + part
            first += rows
        out[...] = total.astype(bf16)


def pack(values, slots, chunks, count):
    half = values[0].shape[1]
    outs = [sds((count, half), bf16)] * chunks
    kernel = functools.partial(pack_kernel, len(values), count)
    return one_step(kernel, "pack", 2.5, [], [slots, *values], outs)


def unpack_kernel(offset, slots_own, slots_other, gates_own, gates_other, rows, *refs):
    keep, send = refs[-2:]
    count = rows.shape[0]
    for j, (slots, gates, out) in enumerate(
        ((slots_own, gates_own, keep), (slots_other, gates_other, send))
    ):
        at = offset + lax.broadcasted_iota(i32, (slots.shape[0], count), 1)
        total = refs[j][...] if len(refs) > 2 else None
        for c in range(2):
            hot = jnp.where(slots[:, c : c + 1] == at, 1.0, 0.0).astype(bf16)
            part = gates[:, c : c + 1] * nn(hot, rows[...])
            total = part if total is None else total + part
        out[...] = total.astype(out.dtype)


def unpack(slots_own, slots_other, gates_own, gates_other, n, chunk, sofar, last):
    count, half = chunk.shape
    rows = slots_own.shape[0]
    outs = [sds((rows, half), f32), sds((rows, half), bf16 if last else f32)]
    arrays = [slots_own, slots_other, gates_own, gates_other, chunk, *sofar]
    kernel = functools.partial(unpack_kernel, n * count)
    return one_step(kernel, "unpack", 2.5, [], arrays, outs)


def combine_kernel(keep, recv, hidden, r, dlog, wrt, gain, dn, dots, gain_sum):
    hi, lo = split_two(dlog[...])
    d = keep[...] + recv[...].astype(f32) + nn(hi, wrt[...]) + nn(lo, wrt[...])
    dn[...] = d
    hat = hidden[...] * r[...]
    prod = d * hat
    gain_sum[...] = jnp.broadcast_to(jnp.sum(prod, axis=0, keepdims=True), gain_sum.shape)
    hi, lo = split_two(prod * gain[...])
    ones = jnp.ones((8, hi.shape[1]), bf16)
    dots[...] = nt(ones, hi) + nt(ones, lo)


def combine(keep, recv, hidden, r, dlog, wrt, gain):
    rows, half = hidden.shape
    outs = [sds((rows, half), f32), sds((8, rows), f32), sds((8, half), f32)]
    arrays = [keep, recv, hidden, r, dlog, wrt, gain]
    return one_step(combine_kernel, "combine", 2, [], arrays, outs)


def hidden_gradient_kernel(dn, hidden, r, gain, dots, recv, oa, ob, out):
    rows, half = dn.shape
    block = rows // 2
    other = jnp.concatenate([recv[0:1, block:], recv[0:1, :block]], axis=1)
    mean = row_to_column((dots[0:1, :] + other) * (0.5 / half), rows)
    rr = r[...]
    d = rr * (gain[...] * dn[...] - hidden[...] * rr * mean)
    out[:block, :] = (oa[...].astype(f32) + d[:block]).astype(bf16)
    out[block:, :] = (ob[...].astype(f32) + d[block:]).astype(bf16)


def hidden_gradient(dn, hidden, r, gain, dots, recv, oa, ob):
    arrays = [dn, hidden, r, gain, dots, recv, oa, ob]
    outs = [sds(hidden.shape, bf16)]
    return one_step(hidden_gradient_kernel, "hidden_gradient", 1.5, [], arrays, outs)[0]


def full_rows(scratch, x, a, b):
    groups, _, cap, half = a.shape
    mine = pl.ds(pl.multiple_of(x * half, 128), half)
    away = pl.ds(pl.multiple_of((1 - x) * half, 128), half)
    scratch[:, mine] = a[:, 0].astype(f32).reshape(groups * cap, half)
    scratch[:, away] = b[:, 0].astype(f32).reshape(groups * cap, half)
    return scratch[...]


def d_act_kernel(sc, da, db, w_out, d_moe, d_act, scratch):
    d = full_rows(scratch, sc[1], da, db).astype(bf16)
    d_moe[0] = d
    d_act[0] = nt(d, w_out[0]).astype(bf16)


def row_specs(groups, cap, half):
    return [pl.BlockSpec((groups, 1, cap, half), lambda i, s: (0, i, 0, 0))]


def d_act_rows(sc, da, db, w_out, virtual):
    groups, count, cap, half = da.shape
    rows, width = groups * cap, 2 * half
    local, hidden, _ = w_out.shape
    out = lambda w: pl.BlockSpec((1, rows, w), lambda i, s: (i, 0, 0))
    return pl.pallas_call(
        d_act_kernel,
        grid_spec=pltpu.PrefetchScalarGridSpec(
            num_scalar_prefetch=1,
            grid=(count,),
            in_specs=row_specs(groups, cap, half) * 2
            + [
                pl.BlockSpec(
                    (1, hidden, width), lambda i, s: ((s[0] + i) * local // virtual, 0, 0)
                )
            ],
            out_specs=[out(width), out(hidden)],
            scratch_shapes=[pltpu.VMEM((rows, width), f32)],
        ),
        out_shape=[sds((count, rows, width), bf16), sds((count, rows, hidden), bf16)],
        compiler_params=params(28),
        cost_estimate=cost(1e6, count * 5e6),
        name="d_act_rows",
    )(sc, da, db, w_out)


def expert_kernel(summing, sc, xa, xb, d_act, w_in, w_out, inv_gain, *refs):
    if summing:
        recv, y_recv, normed, act_ref, d_pre_ref, dg, *parts, scratch = refs
    else:
        normed, act_ref, d_pre_ref, dg, *parts, scratch = refs
    x = sc[1]
    groups, _, cap, half = xa.shape
    rows, width = groups * cap, 2 * half
    g = full_rows(scratch, x, xa, xb)
    h = g * inv_gain[...]
    r = lax.rsqrt(jnp.sum(h * h, axis=1, keepdims=True) * (1.0 / width) + 1e-06)
    n = (g * r).astype(bf16)
    normed[0] = n
    u = nn(n, w_in[0])
    k = 0.7978845608028654
    uu = u * u
    t = jnp.tanh(u * (k + (k * 0.044715) * uu))
    a = 0.5 + 0.5 * t
    act = (u * a).astype(bf16)
    act_ref[0] = act
    slope = a + (0.5 * u) * (1.0 - t * t) * (k + (3.0 * 0.044715 * k) * uu)
    da = d_act[0].astype(f32)
    d_pre = (da * slope).astype(bf16)
    d_pre_ref[0] = d_pre
    hi, lo = split_two(act.astype(f32) * da)
    ones = jnp.ones((8, hi.shape[1]), bf16)
    dg[0] = nt(ones, hi) + nt(ones, lo)
    row_gradient, row_out = nt(d_pre, w_in[0]), nn(act, w_out[0])
    if summing:
        for d, came, (mine, away) in (
            (row_gradient, recv, parts[:2]),
            (row_out, y_recv, parts[2:]),
        ):
            d = d + came[:, 0].astype(f32).reshape(rows, width)
            lo, hi = d[:, :half], d[:, half:]
            mine[:, 0] = jnp.where(x == 0, lo, hi).reshape(groups, cap, half)
            away[:, 0] = jnp.where(x == 0, hi, lo).reshape(groups, cap, half).astype(bf16)
    else:
        for d, out in ((row_gradient, parts[0]), (row_out, parts[1])):
            out[:, 0] = d.reshape(groups, cap, width).astype(bf16)


def experts(sc, xa, xb, d_act, first, w_in, w_out, inv_gain, virtual, recvs=()):
    groups, count, cap, half = xa.shape
    rows, width = groups * cap, 2 * half
    local, _, hidden = w_in.shape
    (part,) = row_specs(groups, cap, half)
    (full,) = row_specs(groups, cap, width)
    keep = lambda w: pl.BlockSpec((1, rows, w), lambda i, s: (i, 0, 0))
    shape = (groups, count, cap)
    summing = len(recvs) > 0
    return pl.pallas_call(
        functools.partial(expert_kernel, summing),
        grid_spec=pltpu.PrefetchScalarGridSpec(
            num_scalar_prefetch=1,
            grid=(count,),
            in_specs=[
                part,
                part,
                pl.BlockSpec((1, rows, hidden), lambda i, s: (first + i, 0, 0)),
                pl.BlockSpec(
                    (1, width, hidden), lambda i, s: ((s[0] + i) * local // virtual, 0, 0)
                ),
                pl.BlockSpec(
                    (1, hidden, width), lambda i, s: ((s[0] + i) * local // virtual, 0, 0)
                ),
                pl.BlockSpec((1, width), lambda i, s: (0, 0)),
            ]
            + [full] * len(recvs),
            out_specs=[
                keep(width),
                keep(hidden),
                keep(hidden),
                pl.BlockSpec((1, 8, rows), lambda i, s: (i, 0, 0)),
            ]
            + ([part] * 4 if summing else [full] * 2),
            scratch_shapes=[pltpu.VMEM((rows, width), f32)],
        ),
        out_shape=[
            sds((count, rows, width), bf16),
            sds((count, rows, hidden), bf16),
            sds((count, rows, hidden), bf16),
            sds((count, 8, rows), f32),
        ]
        + (
            [sds(shape + (half,), f32), sds(shape + (half,), bf16)] * 2
            if summing
            else [sds(shape + (width,), bf16)] * 2
        ),
        compiler_params=params(30),
        cost_estimate=cost(1e6, count * 11e6),
        name="experts",
    )(sc, xa, xb, d_act, w_in, w_out, inv_gain, *recvs)


def weight_gradient_kernel(sc, gate, d_moe, normed, act, d_pre, *refs):
    g_in, g_out, token = refs[-3:]
    token[...] = jnp.zeros_like(token)
    g = row_to_column(gate[0, 0:1, :], gate.shape[2])
    g_out[0] = tn((act[0].astype(f32) * g).astype(bf16), d_moe[0])
    g_in[0] = tn(normed[0], (d_pre[0].astype(f32) * g).astype(bf16))


def weight_gradient(sc, gate, d_moe, first, normed, act, d_pre, virtual, earlier, extra):
    count, rows, width = normed.shape
    hidden = act.shape[2]
    part = lambda w: pl.BlockSpec((1, rows, w), lambda i, s: (i, 0, 0))
    return pl.pallas_call(
        weight_gradient_kernel,
        grid_spec=pltpu.PrefetchScalarGridSpec(
            num_scalar_prefetch=1,
            grid=(count,),
            in_specs=[
                pl.BlockSpec((1, 8, rows), lambda i, s: (s[0] + i, 0, 0)),
                pl.BlockSpec((1, rows, width), lambda i, s: (first + i, 0, 0)),
                part(width),
                part(hidden),
                part(hidden),
            ]
            + [pl.BlockSpec(memory_space=pl.ANY)] * (len(earlier) + len(extra)),
            out_specs=[
                pl.BlockSpec((1, width, hidden), lambda i, s: (s[0] + i, 0, 0)),
                pl.BlockSpec((1, hidden, width), lambda i, s: (s[0] + i, 0, 0)),
                pl.BlockSpec((8, 128), lambda i, s: (0, 0)),
            ],
        ),
        out_shape=[
            sds((virtual, width, hidden), f32),
            sds((virtual, hidden, width), f32),
            sds((8, 128), f32),
        ],
        input_output_aliases={6 + n: n for n in range(len(earlier))},
        compiler_params=params(),
        cost_estimate=cost(1e6, count * 8e6),
        name="weight_gradient",
    )(sc, gate, d_moe, normed, act, d_pre, *earlier, *extra)


def together(*values):
    return lax.optimization_barrier(values)


def per_device(
    tokens,
    gain_one,
    w_qkv,
    rel_table,
    w_mix,
    gain_two,
    w_router,
    w_in,
    w_out,
    routes,
    buffer_row_index,
    image_starts,
    d_output,
):
    block, width = tokens.shape
    tensor_count = lax.axis_size("tensor")
    tensor_index = lax.axis_index("tensor")
    groups = lax.axis_size("dp")
    cx, cc = tensor_index // 2, tensor_index % 2
    length = block * tensor_count
    heads = rel_table.shape[0] // tensor_count
    head_width = heads * HEAD_DIM
    local = w_in.shape[0]
    half = width // 2
    virtual = max(local, 2)
    per_half = virtual // 2
    cap = CAP * local // virtual
    vcap = cap if cap % 8 == 0 else -(-cap // 16) * 16
    chunks = 2 if per_half % 2 == 0 else 1
    per_chunk = per_half // chunks
    chunk_slots = groups * per_chunk * vcap
    half_slots = chunks * chunk_slots

    sc = jnp.concatenate([image_starts[0], jnp.stack([cx, cc]).astype(i32)])

    def feat(v, axis, side):
        return lax.dynamic_slice_in_dim(v, side * half, half, axis)

    shard = jnp.concatenate([w_qkv[0], w_qkv[1], w_qkv[2], w_mix.T], axis=1)
    weights = gather_dp(shard).reshape(width, 4 * head_width)
    tok_x = swap_x(tokens)
    tok_c = swap_core(tokens)
    tok_d = swap_core(tok_x)
    toks = (tokens, tok_x, tok_c, tok_d)

    bias_table = lax.dynamic_slice_in_dim(rel_table, tensor_index * heads, heads, 0)
    hot = bucket_of(np.arange(2 * length) - length)[None, :] == np.arange(rel_table.shape[1])[:, None]
    bvec = jnp.dot(bias_table * LOG2E, jnp.asarray(hot.astype(np.float32)), precision=highest)
    bvec = jnp.pad(bvec, ((0, 8 - heads), (0, 0)))

    def slot_parts(route, index):
        flat = route * CAP + index
        expert_v, row_v = flat // cap, flat % cap
        group_v, v_v = expert_v // virtual, expert_v % virtual
        half_v, v2_v = v_v // per_half, v_v % per_half
        chunk_v, vc_v = v2_v // per_chunk, v2_v % per_chunk
        in_half = chunk_v * chunk_slots + (group_v * per_chunk + vc_v) * vcap + row_v
        whole_half = (group_v * per_half + v2_v) * vcap + row_v
        is_mine = half_v == cc
        return (
            jnp.where(is_mine, in_half, -1),
            jnp.where(is_mine, whole_half, -1),
            (group_v * virtual + v_v) * vcap + row_v,
        )

    def relative(v):
        at = [2 * (cx ^ (n % 2)) + (cc ^ (n // 2)) for n in range(4)]
        return jnp.concatenate([lax.dynamic_slice_in_dim(v, a * block, block, 0) for a in at], 0)

    routes_rel = relative(routes)
    slots_rel, whole_rel, both_rel = slot_parts(routes_rel, relative(buffer_row_index))
    slots_own, slots_other = slots_rel[: 2 * block], slots_rel[2 * block :]
    whole_own, whole_other = whole_rel[: 2 * block], whole_rel[2 * block :]
    routes_own = routes_rel[: 2 * block]

    do_a = feat(d_output, 1, cx)
    do_b = swap_x(feat(d_output, 1, 1 - cx))
    (d_packed,) = pack((do_a, do_b, swap_core(do_a), swap_core(do_b)), whole_rel.T, 1, half_slots)
    d_packed, weights = lax.optimization_barrier((d_packed, weights))
    da = exchange(d_packed.reshape(groups, per_half, vcap, half))

    normed, q, k, v, att, probs, keep, send = attention_forward(
        sc, toks, gain_one[None], weights, bvec, heads
    )
    chip_mine, chip_away = chip_sum(sc, keep, swap_core(send))
    gain_half = feat(gain_two, 0, cx)[None]
    wrt_half = feat(w_router, 0, cx).T
    hidden, scaled, sums = router(
        chip_mine,
        swap_x(chip_away),
        feat(tokens, 1, cx),
        feat(tok_x, 1, cx),
        gain_half,
        wrt_half,
        routes_own.T,
    )
    db = swap_x(da)
    dc, dd = swap_core(da), swap_core(db)
    base_own = cc * per_half
    base_other = (1 - cc) * per_half
    call_own = jnp.stack([base_own, cx]).astype(i32)
    call_other = jnp.stack([base_other, cx]).astype(i32)
    d_moe_own, d_act_own = d_act_rows(call_own, da, db, w_out, virtual)
    d_moe_other, d_act_other = d_act_rows(call_other, dc, dd, w_out, virtual)

    rows_in = []
    for rows in pack((scaled, swap_core(scaled)), slots_rel.T, chunks, chunk_slots):
        if rows_in:
            rows, db = together(rows, db)
        a = exchange(rows.reshape(groups, per_chunk, vcap, half))
        if rows_in:
            a, d_act_other, d_act_own = together(a, d_act_other, d_act_own)
        b = swap_x(a)
        rows_in.append((a, b, swap_core(a)))

    def flip(v):
        return jnp.concatenate([v[:, block:], v[:, :block]], axis=1)

    sums = sums + flip(swap_x(sums))
    sums_other = swap_core(sums)

    def token_parts(v):
        r = lax.rsqrt(v[0] / width + 1e-06)
        return r, jax.nn.softmax(r[:, None] * v[1:3].T, axis=-1)

    r_own, gates_own = token_parts(sums)
    r_other, gates_other = token_parts(sums_other)
    r_own = r_own[:, None]
    gates_all = jnp.concatenate([gates_own, gates_other], 0)
    def one_hots(slots):
        experts_hot = slots[:, :, None] // vcap == jnp.arange(groups * virtual, dtype=i32)
        rows_hot = slots[:, :, None] % vcap == jnp.arange(vcap, dtype=i32)
        return experts_hot.astype(f32), rows_hot.astype(f32)

    experts_hot, rows_hot = one_hots(both_rel)
    gate_slots = jnp.einsum(
        "tce,tcr->er", experts_hot * gates_all[:, :, None], rows_hot, precision=highest
    )
    gate_send = gate_slots.reshape(groups, 1, virtual * vcap)

    inv_gain = (1.0 / gain_two)[None]
    others, owns, dr_recvs = [], [], []
    for n in range(chunks):
        first = n * per_chunk
        _, b, xc = rows_in[n]
        if others:
            b, others[-1][4] = together(b, others[-1][4])
        xd = swap_core(b)
        if n == 0:
            xc, d_act_own = lax.optimization_barrier((xc, d_act_own))
        call = call_other + jnp.asarray([first, 0], i32)
        others.append(list(experts(call, xc, xd, d_act_other, first, w_in, w_out, inv_gain, virtual)))
    for n in range(chunks):
        first = n * per_chunk
        xa, xb = rows_in[n][:2]
        call = call_own + jnp.asarray([first, 0], i32)
        if owns:
            xa, owns[-1][3] = together(xa, owns[-1][3])
        recvs = (swap_core(others[n][4]), swap_core(others[n][5]))
        out = experts(
            call, xa, xb, d_act_own, first, w_in, w_out, inv_gain, virtual, recvs
        )
        owns.append(list(out))
        dr_recvs.append(swap_x(out[5]))

    dr_send = [(o[4] + v.astype(f32)).astype(bf16) for o, v in zip(owns, dr_recvs)]
    if chunks > 1:
        dr_send[0], owns[-1][3] = together(dr_send[0], owns[-1][3])
    own_dg = jnp.concatenate([o[3][:, 0] for o in owns], 0)
    other_dg = jnp.concatenate([o[3][:, 0] for o in others], 0)
    dg = jnp.where(
        cc == 0, jnp.concatenate([own_dg, other_dg], 0), jnp.concatenate([other_dg, own_dg], 0)
    )
    dg = jnp.moveaxis(dg.reshape(virtual, groups, vcap), 0, 1).reshape(groups, 1, virtual * vcap)
    dg = dg + swap_core(dg)
    dg = dg + swap_x(dg)

    dr_back = [exchange(v).reshape(chunk_slots, half) for v in dr_send[:-1]]
    both = jnp.concatenate([gate_send, dg], axis=2)
    dr_send[-1], both, owns[-1][7] = together(dr_send[-1], both, owns[-1][7])
    y = jnp.concatenate(
        [(o[6] + swap_x(o[7]).astype(f32)).astype(bf16) for o in owns], axis=1
    )
    dr_back.append(exchange(dr_send[-1]).reshape(chunk_slots, half))
    unpack_args = (slots_own, slots_other, gates_own, gates_other)
    sofar = []
    for n in range(chunks - 1):
        sofar = list(unpack(*unpack_args, n, dr_back[n], sofar, False))
    if sofar:
        both, sofar[0] = together(both, sofar[0])
    both = exchange_small(both)
    gate_rows, dg = both[:, 0, : virtual * vcap], both[:, 0, virtual * vcap :]
    gate_rows = jnp.moveaxis(gate_rows.reshape(groups, virtual, vcap), 1, 0)
    gate_rows = jnp.broadcast_to(
        gate_rows.reshape(virtual, 1, groups * vcap), (virtual, 8, groups * vcap)
    )
    dg = dg.reshape(groups * virtual, vcap)

    def to_tokens(slots):
        ehot = (slots[:, None] // vcap == jnp.arange(groups * virtual, dtype=i32)).astype(f32)
        rhot = (slots[:, None] % vcap == jnp.arange(vcap, dtype=i32)).astype(f32)
        return jnp.sum(jnp.dot(ehot, dg, precision=highest) * rhot, axis=1)

    both_own = both_rel[: 2 * block]
    dg_own = jnp.stack([to_tokens(both_own[:, c]) for c in range(2)], axis=1)
    d_chosen = gates_own * (dg_own - jnp.sum(gates_own * dg_own, axis=-1, keepdims=True))
    selectors = (routes_own[:, :, None] == jnp.arange(EXPERTS, dtype=i32)).astype(f32)
    d_logits = jnp.sum(d_chosen[:, :, None] * selectors, axis=1)
    nt_own = (scaled.astype(f32) * r_own).astype(bf16)
    grad_router = jnp.dot(nt_own.astype(f32).T, d_logits, precision=highest)

    pieces = [
        (call, first * per_chunk, d_moe, o)
        for call, d_moe, gone in ((call_own, d_moe_own, owns), (call_other, d_moe_other, others))
        for first, o in enumerate(gone)
    ]

    def weight_part(piece, earlier, extra):
        call, first, d_moe, o = piece
        at = call + jnp.asarray([first, 0], i32)
        *earlier, token = weight_gradient(
            at, gate_rows, d_moe, first, *o[:3], virtual, earlier, extra
        )
        return earlier, token

    def held(piece, *others):
        call, first, d_moe, o = piece
        act, *others = together(o[1], *others)
        return ((call, first, d_moe, (o[0], act, o[2])), *others)

    grads, token = weight_part(pieces[0], [], [])
    dr_last, d_logits, token = together(dr_back[-1], d_logits, token)
    keep_d, send_d = unpack(*unpack_args, chunks - 1, dr_last, sofar, True)
    dn, dots, gain_two_sum = combine(
        keep_d, swap_core(send_d), hidden, r_own, d_logits, wrt_half, gain_half
    )
    dn, y = lax.optimization_barrier((dn, y))
    y_back = exchange(y).reshape(half_slots, half)
    d_mixed = hidden_gradient(dn, hidden, r_own, gain_half, dots, swap_x(dots), do_a, do_b)
    if len(pieces) > 2:
        pieces[1], d_mixed = held(pieces[1], d_mixed)
        grads, token = weight_part(pieces[1], grads, [token])
    d_mixed_x, token = together(swap_x(d_mixed), token)
    d_hidden, gmt, d_att = mix_backward(
        sc, (d_mixed, d_mixed_x, swap_core(d_mixed), swap_core(d_mixed_x)), weights, att, heads
    )

    d_att, y_back = lax.optimization_barrier((d_att, y_back))
    table, keep_n, send_n, gain_one_sum, *grad_w = attention_backward(
        sc, d_att, probs, q, k, v, normed, gmt, weights, toks, groups
    )

    grad_w = grad_w[0].reshape(groups, -1, grad_w[0].shape[-1])

    def sum_dp(v):
        step = 1
        while step < groups:
            v = v + lax.ppermute(v, "dp", [(i, i ^ step) for i in range(groups)])
            step *= 2
        return v

    table = lax.dynamic_update_slice_in_dim(
        jnp.zeros(rel_table.shape, f32), table[:heads, : rel_table.shape[1]], tensor_index * heads, 0
    )
    small = jnp.concatenate(
        [gain_one_sum[0], table.reshape(-1), gain_two_sum[0], grad_router.reshape(-1)]
    )
    small = sum_dp(small.reshape(-1, 128))
    d_norm = keep_n + swap_core(send_n).astype(f32)
    norm_send = d_norm[1].astype(bf16)
    grad_w, small, norm_send, y_back = together(grad_w, small, norm_send, y_back)
    if len(pieces) > 2:
        pieces[-2], grad_w = held(pieces[-2], grad_w)
        grads, token = weight_part(pieces[-2], grads, [token])
    grad_w = exchange(grad_w)
    norm_recv = swap_x(norm_send)
    pieces[-1], norm_recv = held(pieces[-1], norm_recv)
    d_norm = d_norm[0] + norm_recv.astype(f32)
    t = tokens.astype(f32)
    r = lax.rsqrt(jnp.mean(t * t, axis=-1, keepdims=True) + 1e-06)
    gd = gain_one * d_norm
    hat = t * r
    grad_input = d_hidden.astype(f32) + r * (gd - hat * jnp.mean(gd * hat, axis=-1, keepdims=True))
    grad_w = jnp.sum(grad_w.astype(f32), axis=0)
    grad_qkv = jnp.stack([grad_w[:, j * head_width : (j + 1) * head_width] for j in range(3)])
    grad_mix = grad_w[:, 3 * head_width :].T

    small = small + swap_core(small)
    small_x = swap_x(small).reshape(-1)
    small = small.reshape(-1)
    cut = width + rel_table.size
    last = small[:cut] + small_x[:cut]
    grad_gain_one, grad_table = last[:width], last[width:].reshape(rel_table.shape)
    small, small_x = small[cut:], small_x[cut:]
    small = jnp.where(cx == 0, jnp.stack([small, small_x]), jnp.stack([small_x, small]))
    grad_gain_two = small[:, :half].reshape(width)
    grad_router = small[:, half:].reshape(width, EXPERTS)

    (g_in, g_out), _ = weight_part(pieces[-1], grads, [token])
    if virtual != local:
        hidden_units = w_in.shape[2]
        g_in = jnp.sum(g_in.reshape(local, virtual // local, width, hidden_units), axis=1)
        g_out = jnp.sum(g_out.reshape(local, virtual // local, hidden_units, width), axis=1)

    keep_y, send_y = unpack(
        whole_own, whole_other, gates_own, gates_other, 0, y_back, [], True
    )
    out = (hidden + keep_y + swap_core(send_y).astype(f32)).astype(bf16)
    out_recv = swap_x(out[block:])
    output = jnp.where(
        cx == 0,
        jnp.concatenate([out[:block], out_recv], 1),
        jnp.concatenate([out_recv, out[:block]], 1),
    )
    return (
        output,
        grad_input,
        grad_gain_one,
        grad_qkv,
        grad_table,
        grad_mix,
        grad_gain_two,
        grad_router,
        g_in,
        g_out,
    )


def solution(mesh):
    in_specs = (
        P(("dp", "tensor"), None),
        P(),
        P(None, "dp", "tensor"),
        P(),
        P("tensor", "dp"),
        P(),
        P(),
        P("dp", None, "tensor"),
        P("dp", "tensor", None),
        P("dp", None),
        P("dp", None),
        P("dp", None),
        P(("dp", "tensor"), None),
    )
    out_specs = (
        P(("dp", "tensor"), None),
        P(("dp", "tensor"), None),
        P(),
        P(None, "dp", "tensor"),
        P(),
        P("tensor", "dp"),
        P(),
        P(),
        P("dp", None, "tensor"),
        P("dp", "tensor", None),
    )
    return jax.shard_map(
        per_device, mesh=mesh, in_specs=in_specs, out_specs=out_specs, check_vma=False
    )
```

```python
import functools

import jax
import jax.numpy as jnp
import numpy as np
from jax import lax
from jax.experimental import pallas as pl
from jax.experimental.pallas import tpu as pltpu
from jax.sharding import PartitionSpec as P

HEAD_DIM = 64
EXPERTS = 64
SPAN = 256
CAP = 40
LOG2E = 1.4426950408889634
NEG = -1e30
bucket_edges = (1, 2, 3, 4, 5, 6, 7, 8, 11, 16, 23, 32, 45, 64, 91)
highest = lax.Precision.HIGHEST
f32 = jnp.float32
bf16 = jnp.bfloat16
i32 = jnp.int32
MIB = 1 << 20


def bucket_of(offsets):
    magnitude = np.abs(offsets)
    levels = np.zeros(offsets.shape, np.int32)
    for threshold in bucket_edges:
        levels = levels + (magnitude >= threshold).astype(np.int32)
    return levels + (len(bucket_edges) + 1) * (offsets > 0).astype(np.int32)


def nn(a, b):
    return jnp.dot(a, b, preferred_element_type=f32)


def nt(a, b):
    return lax.dot_general(a, b, (((1,), (1,)), ((), ())), preferred_element_type=f32)


def tn(a, b):
    return lax.dot_general(a, b, (((0,), (0,)), ((), ())), preferred_element_type=f32)


def split_two(v):
    hi = v.astype(bf16)
    return hi, (v - hi.astype(f32)).astype(bf16)


def swap_core(v):
    return lax.ppermute(v, "tensor", [(i, i ^ 1) for i in range(lax.axis_size("tensor"))])


def swap_x(v):
    return lax.ppermute(v, "tensor", [(i, i ^ 2) for i in range(lax.axis_size("tensor"))])


def exchange(v):
    return lax.all_to_all(v, "dp", 0, 0, tiled=True)


def exchange_small(v):
    groups = lax.axis_size("dp")
    order = jnp.arange(groups) ^ lax.axis_index("dp")
    v = jnp.take(v, order, axis=0)
    step = 1
    while step < groups:
        shape = v.shape
        v = v.reshape((groups // (2 * step), 2, step) + shape[1:])
        moved = lax.ppermute(v[:, 1], "dp", [(i, i ^ step) for i in range(groups)])
        v = jnp.stack([v[:, 0], moved], axis=1).reshape(shape)
        step *= 2
    return jnp.take(v, order, axis=0)


def gather_dp(v):
    groups = lax.axis_size("dp")
    return exchange(jnp.broadcast_to(v[None], (groups,) + v.shape))


def smem():
    return pl.BlockSpec(memory_space=pltpu.SMEM)


def sds(shape, dtype):
    return jax.ShapeDtypeStruct(shape, dtype)


def one_step(kernel, name, us, scalars, arrays, outs, scratch=(), mib=20):
    def whole(v):
        return pl.BlockSpec(v.shape, lambda i: (0,) * len(v.shape))

    return pl.pallas_call(
        kernel,
        grid=(1,),
        in_specs=[smem() for _ in scalars] + [whole(v) for v in arrays],
        out_specs=[whole(v) for v in outs],
        out_shape=list(outs),
        scratch_shapes=list(scratch),
        compiler_params=params(mib),
        cost_estimate=cost(1e6, us * 3e6),
        name=name,
    )(*scalars, *arrays)


def params(mib=62):
    return pltpu.CompilerParams(vmem_limit_bytes=62 * MIB)


def cost(flops, nbytes):
    return pl.CostEstimate(flops=int(600 * nbytes), bytes_accessed=int(nbytes), transcendentals=0)


def row_to_column(row, n):
    a = lax.broadcasted_iota(i32, (n, n), 0)
    b = lax.broadcasted_iota(i32, (n, n), 1)
    return jnp.sum(jnp.where(a == b, row, 0.0), axis=1, keepdims=True)


def quarter_rows(sc, flip_x, flip_c, block):
    at = 2 * (sc[2] ^ flip_x) + (sc[3] ^ flip_c)
    return pl.ds(pl.multiple_of(at * block, block), block)


def forward_kernel(
    sc, ta, tb, tc, td, gain, weights, bvec, normed, q, k, v, att, p_out, keep, send, toep, score, mask
):
    b = pl.program_id(0)
    block = att.shape[0]
    length = 4 * block
    heads = q.shape[0]
    blocks = length // block

    @pl.when(b == 0)
    def _():
        for i, ref in enumerate((ta, tb, tc, td)):
            rows = quarter_rows(sc, i % 2, i // 2, block)
            t = ref[...].astype(f32)
            n = t * lax.rsqrt(jnp.mean(t * t, axis=-1, keepdims=True) + 1e-06) * gain[...]
            n = n.astype(bf16)
            normed[rows, :] = n
            pr = nn(n, weights[:, : 3 * heads * HEAD_DIM]).astype(bf16)
            for h in range(heads):
                for j, out in enumerate((q, k, v)):
                    at = (j * heads + h) * HEAD_DIM
                    out[h, rows, :] = pr[:, at : at + HEAD_DIM]
        for h in range(heads):
            row = jnp.broadcast_to(bvec[h : h + 1, :], (8, 2 * length))
            for a in range(0, block, 8):
                toep[h, a : a + 8, :] = pltpu.roll(row, a, 1, stride=1, stride_axis=0)

    s0, s1, x, c = sc[0], sc[1], sc[2], sc[3]
    rc = 16

    def one_block(bs):
        r0 = bs * block
        kv = min(r0 + 2 * block, length)
        wide = kv - r0
        ii = r0 + lax.broadcasted_iota(i32, (block, wide), 0)
        jj = r0 + lax.broadcasted_iota(i32, (block, wide), 1)
        first = (ii >= s0) & (ii < s0 + SPAN) & (jj >= s0) & (jj < s0 + SPAN)
        second = (ii >= s1) & (ii < s1 + SPAN) & (jj >= s1) & (jj < s1 + SPAN)
        mask[:, :wide] = jnp.where((jj <= ii) | first | second, 0.0, NEG)
        for h in range(heads):
            score[:, :kv] = nt(q[h, r0 : r0 + block, :], k[h, :kv, :])
            for i in range(block // rc):
                rows = slice(i * rc, (i + 1) * rc)
                s = score[rows, :kv] * (HEAD_DIM ** (-0.5) * LOG2E)
                s = s + toep[h, rows, length - r0 : length - r0 + kv]
                right = s[:, r0:] + mask[rows, :wide]
                s = right if r0 == 0 else jnp.concatenate([s[:, :r0], right], axis=1)
                e = jnp.exp2(s - jnp.max(s, axis=1, keepdims=True))
                total = jnp.sum(e, axis=1, keepdims=True)
                p_out[h, rows, :kv] = (e * (1.0 / total)).astype(bf16)
            att[:, h * HEAD_DIM : (h + 1) * HEAD_DIM] = nn(p_out[h, :, :kv], v[h, :kv, :]).astype(
                bf16
            )
        mixed = nt(att[...], weights[:, 3 * heads * HEAD_DIM :])

        @pl.when(c == bs % 2)
        def _():
            keep[(bs // 2) ^ x] = mixed

        @pl.when(c != bs % 2)
        def _():
            send[(bs // 2) ^ x] = mixed.astype(bf16)

    for bs in range(blocks):
        pl.when(b == bs)(functools.partial(one_block, bs))


def attention_forward(sc, toks, gain, weights, bvec, heads):
    block, width = toks[0].shape
    length = 4 * block
    whole = lambda *shape: pl.BlockSpec(shape, lambda b, s: (0,) * len(shape))
    qkv = (heads, length, HEAD_DIM)
    return pl.pallas_call(
        forward_kernel,
        grid_spec=pltpu.PrefetchScalarGridSpec(
            num_scalar_prefetch=1,
            grid=(4,),
            in_specs=[whole(block, width)] * 4
            + [
                whole(1, width),
                whole(*weights.shape),
                whole(*bvec.shape),
            ],
            out_specs=[
                whole(length, width),
                whole(*qkv),
                whole(*qkv),
                whole(*qkv),
                pl.BlockSpec((block, heads * HEAD_DIM), lambda b, s: (b, 0)),
                pl.BlockSpec((heads, block, length), lambda b, s: (0, b, 0)),
                whole(2, block, width),
                whole(2, block, width),
            ],
            scratch_shapes=[
                pltpu.VMEM((heads, block, 2 * length), f32),
                pltpu.VMEM((block, length), f32),
                pltpu.VMEM((block, 2 * block), f32),
            ],
        ),
        out_shape=[
            sds((length, width), bf16),
            sds(qkv, bf16),
            sds(qkv, bf16),
            sds(qkv, bf16),
            sds((length, heads * HEAD_DIM), bf16),
            sds((heads, length, length), bf16),
            sds((2, block, width), f32),
            sds((2, block, width), bf16),
        ],
        compiler_params=params(40),
        cost_estimate=cost(1e6, 48e6),
        name="attention_forward",
    )(sc, *toks, gain, weights, bvec)


def chip_sum_kernel(sc, keep, recv, mine, away):
    half = mine.shape[1]
    x = sc[2]
    total = (keep[...] + recv[...].astype(f32)).reshape(mine.shape[0], 2 * half)
    lo, hi = total[:, :half], total[:, half:]
    mine[...] = jnp.where(x == 0, lo, hi)
    away[...] = jnp.where(x == 0, hi, lo).astype(bf16)


def chip_sum(sc, keep, recv):
    _, block, width = keep.shape
    shape = (2 * block, width // 2)
    outs = [sds(shape, f32), sds(shape, bf16)]
    return one_step(chip_sum_kernel, "chip_sum", 1.5, [sc], [keep, recv], outs)


def mix_backward_kernel(sc, da, db, dc, dd, weights, att, own, gmt, d_att, dmx):
    x = sc[2]
    rows, half = da.shape
    block = rows // 2
    heads = d_att.shape[0]
    for ref, flip_x, flip_c, side in ((da, 0, 0, x), (db, 1, 0, 1 - x), (dc, 0, 1, x), (dd, 1, 1, 1 - x)):
        for n in range(2):
            to = quarter_rows(sc, n ^ flip_x, flip_c, block)
            lanes = pl.ds(pl.multiple_of(side * half, 128), half)
            dmx[to, lanes] = ref[n * block : (n + 1) * block, :]
    own[...] = dmx[quarter_rows(sc, 0, 0, block), :]
    d = nn(dmx[...], weights[:, 3 * heads * HEAD_DIM :]).astype(bf16)
    for h in range(heads):
        d_att[h] = d[:, h * HEAD_DIM : (h + 1) * HEAD_DIM]
    gmt[...] = tn(dmx[...], att[...]).astype(bf16)


def mix_backward(sc, pieces, weights, att, heads):
    rows, half = pieces[0].shape
    block, length, width = rows // 2, 2 * rows, 2 * half
    outs = [
        sds((block, width), bf16),
        sds((width, heads * HEAD_DIM), bf16),
        sds((heads, length, HEAD_DIM), bf16),
    ]
    scratch = [pltpu.VMEM((length, width), bf16)]
    arrays = [*pieces, weights, att]
    return one_step(mix_backward_kernel, "mix_backward", 3, [sc], arrays, outs, scratch)


def backward_kernel(
    sc,
    d_att,
    p,
    q,
    k,
    v,
    hot,
    normed,
    gmt,
    weights,
    ta,
    tb,
    tc,
    td,
    tab,
    keep,
    send,
    gain_sum,
    *refs,
):
    gws = refs[:-7]
    dproj, score, ds_ref, dkt, dvt, diag, left = refs[-7:]
    b = pl.program_id(0)
    heads, length, _ = q.shape
    block = p.shape[1]
    blocks = length // block
    scale = HEAD_DIM ** (-0.5)
    rc = 16
    margin = 128

    @pl.when(b == 0)
    def _():
        dkt[...] = jnp.zeros_like(dkt)
        dvt[...] = jnp.zeros_like(dvt)
        diag[...] = jnp.zeros_like(diag)
        left[...] = jnp.zeros_like(left)

    def one_block(bs):
        r0 = bs * block
        kv = min(r0 + 2 * block, length)
        lo = max(r0 - margin, 0)
        ones = jnp.ones((8, block), bf16)
        for h in range(heads):
            d_out = d_att[h, r0 : r0 + block, :]
            score[:, :kv] = nt(d_out, v[h, :kv, :])

            for i in range(block // rc):
                rows = slice(i * rc, (i + 1) * rc)
                pr = p[h, rows, :kv].astype(f32)
                pd = pr * score[rows, :kv]
                ds = pd - pr * jnp.sum(pd, axis=1, keepdims=True)
                ds_ref[rows, :kv] = ds.astype(bf16)
                parts = [ds[:, lo:kv]]
                before = margin + lo - r0
                after = length - before - (kv - lo)
                if before:
                    parts.insert(0, jnp.zeros((rc, before), f32))
                if after:
                    parts.append(jnp.zeros((rc, after), f32))
                band = jnp.concatenate(parts, axis=1)
                for g in range(rc // 8):
                    shift = (length - (i * rc + 8 * g)) % length
                    diag[h] += pltpu.roll(band[8 * g : 8 * g + 8], shift, 1)
            at = h * HEAD_DIM
            dq = nn(ds_ref[:, :kv], k[h, :kv, :]) * scale
            dproj[r0 : r0 + block, at : at + HEAD_DIM] = dq.astype(bf16)
            dkt[h, :, :kv] += tn(q[h, r0 : r0 + block, :], ds_ref[:, :kv])
            dvt[h, :, :kv] += tn(d_out, p[h, :, :kv])
            if lo > 0:
                left[h, :, :lo] += nn(ones, ds_ref[:, :lo])

    for bs in range(blocks):
        pl.when(b == bs)(functools.partial(one_block, bs))

    @pl.when(b == blocks - 1)
    def _():
        lane = lax.broadcasted_iota(i32, (1, 128), 1)
        for h in range(heads):
            at = (heads + h) * HEAD_DIM
            dproj[:, at : at + HEAD_DIM] = (dkt[h] * scale).T.astype(bf16)
            at = (2 * heads + h) * HEAD_DIM
            dproj[:, at : at + HEAD_DIM] = dvt[h].T.astype(bf16)
            total = jnp.zeros((1, length), f32)
            for s in range(8):
                total = total + pltpu.roll(diag[h, s : s + 1, :], (length - s) % length, 1)
            far = jnp.sum(left[h, 0:1, :])
            row = jnp.dot(
                jnp.broadcast_to(total, (8, length)),
                hot[...],
                precision=highest,
                preferred_element_type=f32,
            )
            tab[h : h + 1, :] = row[0:1] + jnp.where(lane == len(bucket_edges), far, 0.0)
        gw = tn(normed[...], dproj[...]).astype(bf16)
        step = sum(ref.shape[1] for ref in gws)
        first = 0
        for ref in gws:
            for n in range(ref.shape[0]):
                rows = slice(n * step + first, n * step + first + ref.shape[1])
                ref[n, :, : dproj.shape[1]] = gw[rows]
                ref[n, :, dproj.shape[1] :] = gmt[rows, :]
            first += ref.shape[1]
        all_sum = jnp.zeros((1, weights.shape[0]), f32)
        wq = weights[:, : dproj.shape[1]]
        for i, ref in enumerate((ta, tb, tc, td)):
            dn = nt(dproj[quarter_rows(sc, i % 2, i // 2, block), :], wq)
            t = ref[...].astype(f32)
            hat = t * lax.rsqrt(jnp.mean(t * t, axis=-1, keepdims=True) + 1e-06)
            all_sum = all_sum + jnp.sum(dn * hat, axis=0, keepdims=True)
            if i < 2:
                keep[i] = dn
            else:
                send[i - 2] = dn.astype(bf16)
        gain_sum[...] = jnp.broadcast_to(all_sum, gain_sum.shape)


def attention_backward(sc, d_att, p, q, k, v, normed, gmt, weights, toks, groups):
    heads, length, _ = q.shape
    block = length // 4
    width = normed.shape[1]
    lanes = np.arange(length)
    offsets = np.where(lanes < 768, lanes, lanes - length) - 128
    hot = (bucket_of(offsets)[:, None] == np.arange(128)[None, :]).astype(np.float32)
    whole = lambda *shape: pl.BlockSpec(shape, lambda b, s: (0,) * len(shape))
    qkv = (heads, length, HEAD_DIM)
    wide = 3 * heads * HEAD_DIM
    outs = [
        sds((8, 128), f32),
        sds((2, block, width), f32),
        sds((2, block, width), bf16),
        sds((8, width), f32),
    ]
    step, columns = width // groups, wide + gmt.shape[1]
    if step % 32 == 0:
        outs += [sds((groups, step, columns), bf16)]
    else:
        outs += [sds((1, width, columns), bf16)]
    return pl.pallas_call(
        backward_kernel,
        grid_spec=pltpu.PrefetchScalarGridSpec(
            num_scalar_prefetch=1,
            grid=(4,),
            in_specs=[
                whole(*qkv),
                pl.BlockSpec((heads, block, length), lambda b, s: (0, b, 0)),
                whole(*qkv),
                whole(*qkv),
                whole(*qkv),
                whole(length, 128),
                whole(*normed.shape),
                whole(*gmt.shape),
                whole(*weights.shape),
            ]
            + [whole(block, width)] * 4,
            out_specs=[whole(*o.shape) for o in outs],
            scratch_shapes=[
                pltpu.VMEM((length, wide), bf16),
                pltpu.VMEM((block, length), f32),
                pltpu.VMEM((block, length), bf16),
                pltpu.VMEM((heads, HEAD_DIM, length), f32),
                pltpu.VMEM((heads, HEAD_DIM, length), f32),
                pltpu.VMEM((heads, 8, length), f32),
                pltpu.VMEM((heads, 8, length), f32),
            ],
        ),
        out_shape=outs,
        compiler_params=params(),
        cost_estimate=cost(1e6, 48e6),
        name="attention_backward",
    )(sc, d_att, p, q, k, v, jnp.asarray(hot), normed, gmt, weights, *toks)


def router_kernel(mine, recv, ta, tb, gain, wrt, routes, hidden, scaled, sums):
    rows, half = mine.shape
    block = rows // 2
    for n, tok in enumerate((ta, tb)):
        to, back = slice(n * block, (n + 1) * block), slice((1 - n) * block, (2 - n) * block)
        h = mine[to, :] + recv[back, :].astype(f32) + tok[...].astype(f32)
        hidden[to, :] = h
        scaled[to, :] = (h * gain[...]).astype(bf16)
    h = hidden[...]
    hi, lo = split_two(h * h)
    ones = jnp.ones((8, half), bf16)
    square = nt(ones, hi) + nt(ones, lo)
    logits = nt(wrt[...], scaled[...])
    ids = lax.broadcasted_iota(i32, logits.shape, 0)
    first = jnp.sum(jnp.where(ids == routes[0:1, :], logits, 0.0), axis=0, keepdims=True)
    second = jnp.sum(jnp.where(ids == routes[1:2, :], logits, 0.0), axis=0, keepdims=True)
    index = lax.broadcasted_iota(i32, square.shape, 0)
    sums[...] = jnp.where(index == 0, square, jnp.where(index == 1, first, second))


def router(mine, recv, ta, tb, gain, wrt, routes):
    rows, half = mine.shape
    outs = [sds((rows, half), f32), sds((rows, half), bf16), sds((8, rows), f32)]
    arrays = [mine, recv, ta, tb, gain, wrt, routes]
    return one_step(router_kernel, "router", 1.5, [], arrays, outs)


def pack_kernel(parts, count, slots, *refs):
    values, outs = refs[:parts], refs[parts:]
    for n, out in enumerate(outs):
        total, first = None, 0
        for ref in values:
            rows = ref.shape[0]
            at = n * count + lax.broadcasted_iota(i32, (count, rows), 0)
            lanes = slice(first, first + rows)
            hot = (slots[0:1, lanes] == at) | (slots[1:2, lanes] == at)
            part = nn(jnp.where(hot, 1.0, 0.0).astype(bf16), ref[...])
            total = part if total is None else total + part
            first += rows
        out[...] = total.astype(bf16)


def pack(values, slots, chunks, count):
    half = values[0].shape[1]
    outs = [sds((count, half), bf16)] * chunks
    kernel = functools.partial(pack_kernel, len(values), count)
    return one_step(kernel, "pack", 2.5, [], [slots, *values], outs)


def unpack_kernel(offset, slots_own, slots_other, gates_own, gates_other, rows, *refs):
    keep, send = refs[-2:]
    count = rows.shape[0]
    for j, (slots, gates, out) in enumerate(
        ((slots_own, gates_own, keep), (slots_other, gates_other, send))
    ):
        at = offset + lax.broadcasted_iota(i32, (slots.shape[0], count), 1)
        total = refs[j][...] if len(refs) > 2 else None
        for c in range(2):
            hot = jnp.where(slots[:, c : c + 1] == at, 1.0, 0.0).astype(bf16)
            part = gates[:, c : c + 1] * nn(hot, rows[...])
            total = part if total is None else total + part
        out[...] = total.astype(out.dtype)


def unpack(slots_own, slots_other, gates_own, gates_other, n, chunk, sofar, last):
    count, half = chunk.shape
    rows = slots_own.shape[0]
    outs = [sds((rows, half), f32), sds((rows, half), bf16 if last else f32)]
    arrays = [slots_own, slots_other, gates_own, gates_other, chunk, *sofar]
    kernel = functools.partial(unpack_kernel, n * count)
    return one_step(kernel, "unpack", 2.5, [], arrays, outs)


def combine_kernel(keep, recv, hidden, r, dlog, wrt, gain, dn, dots, gain_sum):
    hi, lo = split_two(dlog[...])
    d = keep[...] + recv[...].astype(f32) + nn(hi, wrt[...]) + nn(lo, wrt[...])
    dn[...] = d
    hat = hidden[...] * r[...]
    prod = d * hat
    gain_sum[...] = jnp.broadcast_to(jnp.sum(prod, axis=0, keepdims=True), gain_sum.shape)
    hi, lo = split_two(prod * gain[...])
    ones = jnp.ones((8, hi.shape[1]), bf16)
    dots[...] = nt(ones, hi) + nt(ones, lo)


def combine(keep, recv, hidden, r, dlog, wrt, gain):
    rows, half = hidden.shape
    outs = [sds((rows, half), f32), sds((8, rows), f32), sds((8, half), f32)]
    arrays = [keep, recv, hidden, r, dlog, wrt, gain]
    return one_step(combine_kernel, "combine", 2, [], arrays, outs)


def hidden_gradient_kernel(dn, hidden, r, gain, dots, recv, oa, ob, out):
    rows, half = dn.shape
    block = rows // 2
    other = jnp.concatenate([recv[0:1, block:], recv[0:1, :block]], axis=1)
    mean = row_to_column((dots[0:1, :] + other) * (0.5 / half), rows)
    rr = r[...]
    d = rr * (gain[...] * dn[...] - hidden[...] * rr * mean)
    out[:block, :] = (oa[...].astype(f32) + d[:block]).astype(bf16)
    out[block:, :] = (ob[...].astype(f32) + d[block:]).astype(bf16)


def hidden_gradient(dn, hidden, r, gain, dots, recv, oa, ob):
    arrays = [dn, hidden, r, gain, dots, recv, oa, ob]
    outs = [sds(hidden.shape, bf16)]
    return one_step(hidden_gradient_kernel, "hidden_gradient", 1.5, [], arrays, outs)[0]


def full_rows(scratch, x, a, b):
    groups, _, cap, half = a.shape
    mine = pl.ds(pl.multiple_of(x * half, 128), half)
    away = pl.ds(pl.multiple_of((1 - x) * half, 128), half)
    scratch[:, mine] = a[:, 0].astype(f32).reshape(groups * cap, half)
    scratch[:, away] = b[:, 0].astype(f32).reshape(groups * cap, half)
    return scratch[...]


def d_act_kernel(sc, da, db, w_out, d_moe, d_act, scratch):
    d = full_rows(scratch, sc[1], da, db).astype(bf16)
    d_moe[0] = d
    d_act[0] = nt(d, w_out[0]).astype(bf16)


def row_specs(groups, cap, half):
    return [pl.BlockSpec((groups, 1, cap, half), lambda i, s: (0, i, 0, 0))]


def d_act_rows(sc, da, db, w_out, virtual):
    groups, count, cap, half = da.shape
    rows, width = groups * cap, 2 * half
    local, hidden, _ = w_out.shape
    out = lambda w: pl.BlockSpec((1, rows, w), lambda i, s: (i, 0, 0))
    return pl.pallas_call(
        d_act_kernel,
        grid_spec=pltpu.PrefetchScalarGridSpec(
            num_scalar_prefetch=1,
            grid=(count,),
            in_specs=row_specs(groups, cap, half) * 2
            + [
                pl.BlockSpec(
                    (1, hidden, width), lambda i, s: ((s[0] + i) * local // virtual, 0, 0)
                )
            ],
            out_specs=[out(width), out(hidden)],
            scratch_shapes=[pltpu.VMEM((rows, width), f32)],
        ),
        out_shape=[sds((count, rows, width), bf16), sds((count, rows, hidden), bf16)],
        compiler_params=params(28),
        cost_estimate=cost(1e6, count * 5e6),
        name="d_act_rows",
    )(sc, da, db, w_out)


def expert_kernel(summing, sc, xa, xb, d_act, w_in, w_out, inv_gain, *refs):
    if summing:
        recv, y_recv, normed, act_ref, d_pre_ref, dg, *parts, scratch = refs
    else:
        normed, act_ref, d_pre_ref, dg, *parts, scratch = refs
    x = sc[1]
    groups, _, cap, half = xa.shape
    rows, width = groups * cap, 2 * half
    g = full_rows(scratch, x, xa, xb)
    h = g * inv_gain[...]
    r = lax.rsqrt(jnp.sum(h * h, axis=1, keepdims=True) * (1.0 / width) + 1e-06)
    n = (g * r).astype(bf16)
    normed[0] = n
    u = nn(n, w_in[0])
    k = 0.7978845608028654
    uu = u * u
    t = jnp.tanh(u * (k + (k * 0.044715) * uu))
    a = 0.5 + 0.5 * t
    act = (u * a).astype(bf16)
    act_ref[0] = act
    slope = a + (0.5 * u) * (1.0 - t * t) * (k + (3.0 * 0.044715 * k) * uu)
    da = d_act[0].astype(f32)
    d_pre = (da * slope).astype(bf16)
    d_pre_ref[0] = d_pre
    hi, lo = split_two(act.astype(f32) * da)
    ones = jnp.ones((8, hi.shape[1]), bf16)
    dg[0] = nt(ones, hi) + nt(ones, lo)
    row_gradient, row_out = nt(d_pre, w_in[0]), nn(act, w_out[0])
    if summing:
        for d, came, (mine, away) in (
            (row_gradient, recv, parts[:2]),
            (row_out, y_recv, parts[2:]),
        ):
            d = d + came[:, 0].astype(f32).reshape(rows, width)
            lo, hi = d[:, :half], d[:, half:]
            mine[:, 0] = jnp.where(x == 0, lo, hi).reshape(groups, cap, half).astype(bf16)
            away[:, 0] = jnp.where(x == 0, hi, lo).reshape(groups, cap, half).astype(bf16)
    else:
        for d, out in ((row_gradient, parts[0]), (row_out, parts[1])):
            out[:, 0] = d.reshape(groups, cap, width).astype(bf16)


def experts(sc, xa, xb, d_act, first, w_in, w_out, inv_gain, virtual, recvs=()):
    groups, count, cap, half = xa.shape
    rows, width = groups * cap, 2 * half
    local, _, hidden = w_in.shape
    (part,) = row_specs(groups, cap, half)
    (full,) = row_specs(groups, cap, width)
    keep = lambda w: pl.BlockSpec((1, rows, w), lambda i, s: (i, 0, 0))
    shape = (groups, count, cap)
    summing = len(recvs) > 0
    return pl.pallas_call(
        functools.partial(expert_kernel, summing),
        grid_spec=pltpu.PrefetchScalarGridSpec(
            num_scalar_prefetch=1,
            grid=(count,),
            in_specs=[
                part,
                part,
                pl.BlockSpec((1, rows, hidden), lambda i, s: (first + i, 0, 0)),
                pl.BlockSpec(
                    (1, width, hidden), lambda i, s: ((s[0] + i) * local // virtual, 0, 0)
                ),
                pl.BlockSpec(
                    (1, hidden, width), lambda i, s: ((s[0] + i) * local // virtual, 0, 0)
                ),
                pl.BlockSpec((1, width), lambda i, s: (0, 0)),
            ]
            + [full] * len(recvs),
            out_specs=[
                keep(width),
                keep(hidden),
                keep(hidden),
                pl.BlockSpec((1, 8, rows), lambda i, s: (i, 0, 0)),
            ]
            + ([part] * 4 if summing else [full] * 2),
            scratch_shapes=[pltpu.VMEM((rows, width), f32)],
        ),
        out_shape=[
            sds((count, rows, width), bf16),
            sds((count, rows, hidden), bf16),
            sds((count, rows, hidden), bf16),
            sds((count, 8, rows), f32),
        ]
        + (
            [sds(shape + (half,), bf16)] * 4
            if summing
            else [sds(shape + (width,), bf16)] * 2
        ),
        compiler_params=params(30),
        cost_estimate=cost(1e6, count * 11e6),
        name="experts",
    )(sc, xa, xb, d_act, w_in, w_out, inv_gain, *recvs)


def weight_gradient_kernel(sc, gate, d_moe, normed, act, d_pre, *refs):
    g_in, g_out, token = refs[-3:]
    token[...] = jnp.zeros_like(token)
    g = row_to_column(gate[0, 0:1, :], gate.shape[2])
    g_out[0] = tn((act[0].astype(f32) * g).astype(bf16), d_moe[0])
    g_in[0] = tn(normed[0], (d_pre[0].astype(f32) * g).astype(bf16))


def weight_gradient(sc, gate, d_moe, first, normed, act, d_pre, virtual, earlier, extra):
    count, rows, width = normed.shape
    hidden = act.shape[2]
    part = lambda w: pl.BlockSpec((1, rows, w), lambda i, s: (i, 0, 0))
    return pl.pallas_call(
        weight_gradient_kernel,
        grid_spec=pltpu.PrefetchScalarGridSpec(
            num_scalar_prefetch=1,
            grid=(count,),
            in_specs=[
                pl.BlockSpec((1, 8, rows), lambda i, s: (s[0] + i, 0, 0)),
                pl.BlockSpec((1, rows, width), lambda i, s: (first + i, 0, 0)),
                part(width),
                part(hidden),
                part(hidden),
            ]
            + [pl.BlockSpec(memory_space=pl.ANY)] * (len(earlier) + len(extra)),
            out_specs=[
                pl.BlockSpec((1, width, hidden), lambda i, s: (s[0] + i, 0, 0)),
                pl.BlockSpec((1, hidden, width), lambda i, s: (s[0] + i, 0, 0)),
                pl.BlockSpec((8, 128), lambda i, s: (0, 0)),
            ],
        ),
        out_shape=[
            sds((virtual, width, hidden), f32),
            sds((virtual, hidden, width), f32),
            sds((8, 128), f32),
        ],
        input_output_aliases={6 + n: n for n in range(len(earlier))},
        compiler_params=params(),
        cost_estimate=cost(1e6, count * 8e6),
        name="weight_gradient",
    )(sc, gate, d_moe, normed, act, d_pre, *earlier, *extra)


def together(*values):
    return lax.optimization_barrier(values)


def per_device(
    tokens,
    gain_one,
    w_qkv,
    rel_table,
    w_mix,
    gain_two,
    w_router,
    w_in,
    w_out,
    routes,
    buffer_row_index,
    image_starts,
    d_output,
):
    block, width = tokens.shape
    tensor_count = lax.axis_size("tensor")
    tensor_index = lax.axis_index("tensor")
    groups = lax.axis_size("dp")
    cx, cc = tensor_index // 2, tensor_index % 2
    length = block * tensor_count
    heads = rel_table.shape[0] // tensor_count
    head_width = heads * HEAD_DIM
    local = w_in.shape[0]
    half = width // 2
    virtual = max(local, 2)
    per_half = virtual // 2
    cap = CAP * local // virtual
    vcap = cap if cap % 8 == 0 else -(-cap // 16) * 16
    chunks = 2 if per_half % 2 == 0 else 1
    per_chunk = per_half // chunks
    chunk_slots = groups * per_chunk * vcap
    half_slots = chunks * chunk_slots

    sc = jnp.concatenate([image_starts[0], jnp.stack([cx, cc]).astype(i32)])

    def feat(v, axis, side):
        return lax.dynamic_slice_in_dim(v, side * half, half, axis)

    shard = jnp.concatenate([w_qkv[0], w_qkv[1], w_qkv[2], w_mix.T], axis=1)
    weights = gather_dp(shard).reshape(width, 4 * head_width)
    tok_x = swap_x(tokens)
    tok_c = swap_core(tokens)
    tok_d = swap_core(tok_x)
    toks = (tokens, tok_x, tok_c, tok_d)

    bias_table = lax.dynamic_slice_in_dim(rel_table, tensor_index * heads, heads, 0)
    hot = bucket_of(np.arange(2 * length) - length)[None, :] == np.arange(rel_table.shape[1])[:, None]
    bvec = jnp.dot(bias_table * LOG2E, jnp.asarray(hot.astype(np.float32)), precision=highest)
    bvec = jnp.pad(bvec, ((0, 8 - heads), (0, 0)))

    def slot_parts(route, index):
        flat = route * CAP + index
        expert_v, row_v = flat // cap, flat % cap
        group_v, v_v = expert_v // virtual, expert_v % virtual
        half_v, v2_v = v_v // per_half, v_v % per_half
        chunk_v, vc_v = v2_v // per_chunk, v2_v % per_chunk
        in_half = chunk_v * chunk_slots + (group_v * per_chunk + vc_v) * vcap + row_v
        whole_half = (group_v * per_half + v2_v) * vcap + row_v
        is_mine = half_v == cc
        return (
            jnp.where(is_mine, in_half, -1),
            jnp.where(is_mine, whole_half, -1),
            (group_v * virtual + v_v) * vcap + row_v,
        )

    def relative(v):
        at = [2 * (cx ^ (n % 2)) + (cc ^ (n // 2)) for n in range(4)]
        return jnp.concatenate([lax.dynamic_slice_in_dim(v, a * block, block, 0) for a in at], 0)

    routes_rel = relative(routes)
    slots_rel, whole_rel, both_rel = slot_parts(routes_rel, relative(buffer_row_index))
    slots_own, slots_other = slots_rel[: 2 * block], slots_rel[2 * block :]
    whole_own, whole_other = whole_rel[: 2 * block], whole_rel[2 * block :]
    routes_own = routes_rel[: 2 * block]

    do_a = feat(d_output, 1, cx)
    do_b = swap_x(feat(d_output, 1, 1 - cx))
    (d_packed,) = pack((do_a, do_b, swap_core(do_a), swap_core(do_b)), whole_rel.T, 1, half_slots)
    d_packed, weights = lax.optimization_barrier((d_packed, weights))
    da = exchange(d_packed.reshape(groups, per_half, vcap, half))

    normed, q, k, v, att, probs, keep, send = attention_forward(
        sc, toks, gain_one[None], weights, bvec, heads
    )
    chip_mine, chip_away = chip_sum(sc, keep, swap_core(send))
    gain_half = feat(gain_two, 0, cx)[None]
    wrt_half = feat(w_router, 0, cx).T
    hidden, scaled, sums = router(
        chip_mine,
        swap_x(chip_away),
        feat(tokens, 1, cx),
        feat(tok_x, 1, cx),
        gain_half,
        wrt_half,
        routes_own.T,
    )
    db = swap_x(da)
    dc, dd = swap_core(da), swap_core(db)
    base_own = cc * per_half
    base_other = (1 - cc) * per_half
    call_own = jnp.stack([base_own, cx]).astype(i32)
    call_other = jnp.stack([base_other, cx]).astype(i32)
    d_moe_own, d_act_own = d_act_rows(call_own, da, db, w_out, virtual)
    d_moe_other, d_act_other = d_act_rows(call_other, dc, dd, w_out, virtual)

    rows_in = []
    for rows in pack((scaled, swap_core(scaled)), slots_rel.T, chunks, chunk_slots):
        if rows_in:
            rows, db = together(rows, db)
        a = exchange(rows.reshape(groups, per_chunk, vcap, half))
        if rows_in:
            a, d_act_other, d_act_own = together(a, d_act_other, d_act_own)
        b = swap_x(a)
        rows_in.append((a, b, swap_core(a)))

    def flip(v):
        return jnp.concatenate([v[:, block:], v[:, :block]], axis=1)

    sums = sums + flip(swap_x(sums))
    sums_other = swap_core(sums)

    def token_parts(v):
        r = lax.rsqrt(v[0] / width + 1e-06)
        return r, jax.nn.softmax(r[:, None] * v[1:3].T, axis=-1)

    r_own, gates_own = token_parts(sums)
    r_other, gates_other = token_parts(sums_other)
    r_own = r_own[:, None]
    gates_all = jnp.concatenate([gates_own, gates_other], 0)
    def one_hots(slots):
        experts_hot = slots[:, :, None] // vcap == jnp.arange(groups * virtual, dtype=i32)
        rows_hot = slots[:, :, None] % vcap == jnp.arange(vcap, dtype=i32)
        return experts_hot.astype(f32), rows_hot.astype(f32)

    experts_hot, rows_hot = one_hots(both_rel)
    gate_slots = jnp.einsum(
        "tce,tcr->er", experts_hot * gates_all[:, :, None], rows_hot, precision=highest
    )
    gate_send = gate_slots.reshape(groups, 1, virtual * vcap)

    inv_gain = (1.0 / gain_two)[None]
    others, owns, dr_recvs = [], [], []
    for n in range(chunks):
        first = n * per_chunk
        _, b, xc = rows_in[n]
        if others:
            b, others[-1][4] = together(b, others[-1][4])
        xd = swap_core(b)
        if n == 0:
            xc, d_act_own = lax.optimization_barrier((xc, d_act_own))
        call = call_other + jnp.asarray([first, 0], i32)
        others.append(list(experts(call, xc, xd, d_act_other, first, w_in, w_out, inv_gain, virtual)))
    for n in range(chunks):
        first = n * per_chunk
        xa, xb = rows_in[n][:2]
        call = call_own + jnp.asarray([first, 0], i32)
        if owns:
            xa, owns[-1][3] = together(xa, owns[-1][3])
        recvs = (swap_core(others[n][4]), swap_core(others[n][5]))
        out = experts(
            call, xa, xb, d_act_own, first, w_in, w_out, inv_gain, virtual, recvs
        )
        owns.append(list(out))
        dr_recvs.append(swap_x(out[5]))

    dr_send = [(o[4].astype(f32) + v.astype(f32)).astype(bf16) for o, v in zip(owns, dr_recvs)]
    if chunks > 1:
        dr_send[0], owns[-1][3] = together(dr_send[0], owns[-1][3])
    own_dg = jnp.concatenate([o[3][:, 0] for o in owns], 0)
    other_dg = jnp.concatenate([o[3][:, 0] for o in others], 0)
    dg = jnp.where(
        cc == 0, jnp.concatenate([own_dg, other_dg], 0), jnp.concatenate([other_dg, own_dg], 0)
    )
    dg = jnp.moveaxis(dg.reshape(virtual, groups, vcap), 0, 1).reshape(groups, 1, virtual * vcap)
    dg = dg + swap_core(dg)
    dg = dg + swap_x(dg)

    dr_back = [exchange(v).reshape(chunk_slots, half) for v in dr_send[:-1]]
    both = jnp.concatenate([gate_send, dg], axis=2)
    dr_send[-1], both, owns[-1][7] = together(dr_send[-1], both, owns[-1][7])
    y = jnp.concatenate(
        [(o[6].astype(f32) + swap_x(o[7]).astype(f32)).astype(bf16) for o in owns], axis=1
    )
    dr_back.append(exchange(dr_send[-1]).reshape(chunk_slots, half))
    unpack_args = (slots_own, slots_other, gates_own, gates_other)
    sofar = []
    for n in range(chunks - 1):
        sofar = list(unpack(*unpack_args, n, dr_back[n], sofar, False))
    if sofar:
        both, sofar[0] = together(both, sofar[0])
    both = exchange_small(both)
    gate_rows, dg = both[:, 0, : virtual * vcap], both[:, 0, virtual * vcap :]
    gate_rows = jnp.moveaxis(gate_rows.reshape(groups, virtual, vcap), 1, 0)
    gate_rows = jnp.broadcast_to(
        gate_rows.reshape(virtual, 1, groups * vcap), (virtual, 8, groups * vcap)
    )
    dg = dg.reshape(groups * virtual, vcap)

    def to_tokens(slots):
        ehot = (slots[:, None] // vcap == jnp.arange(groups * virtual, dtype=i32)).astype(f32)
        rhot = (slots[:, None] % vcap == jnp.arange(vcap, dtype=i32)).astype(f32)
        return jnp.sum(jnp.dot(ehot, dg, precision=highest) * rhot, axis=1)

    both_own = both_rel[: 2 * block]
    dg_own = jnp.stack([to_tokens(both_own[:, c]) for c in range(2)], axis=1)
    d_chosen = gates_own * (dg_own - jnp.sum(gates_own * dg_own, axis=-1, keepdims=True))
    selectors = (routes_own[:, :, None] == jnp.arange(EXPERTS, dtype=i32)).astype(f32)
    d_logits = jnp.sum(d_chosen[:, :, None] * selectors, axis=1)
    nt_own = (scaled.astype(f32) * r_own).astype(bf16)
    grad_router = jnp.dot(nt_own.astype(f32).T, d_logits, precision=highest)

    pieces = [
        (call, first * per_chunk, d_moe, o)
        for call, d_moe, gone in ((call_own, d_moe_own, owns), (call_other, d_moe_other, others))
        for first, o in enumerate(gone)
    ]

    def weight_part(piece, earlier, extra):
        call, first, d_moe, o = piece
        at = call + jnp.asarray([first, 0], i32)
        *earlier, token = weight_gradient(
            at, gate_rows, d_moe, first, *o[:3], virtual, earlier, extra
        )
        return earlier, token

    def held(piece, *others):
        call, first, d_moe, o = piece
        act, *others = together(o[1], *others)
        return ((call, first, d_moe, (o[0], act, o[2])), *others)

    grads, token = weight_part(pieces[0], [], [])
    dr_last, d_logits, token = together(dr_back[-1], d_logits, token)
    keep_d, send_d = unpack(*unpack_args, chunks - 1, dr_last, sofar, True)
    dn, dots, gain_two_sum = combine(
        keep_d, swap_core(send_d), hidden, r_own, d_logits, wrt_half, gain_half
    )
    dn, y = lax.optimization_barrier((dn, y))
    y_back = exchange(y).reshape(half_slots, half)
    d_mixed = hidden_gradient(dn, hidden, r_own, gain_half, dots, swap_x(dots), do_a, do_b)
    if len(pieces) > 2:
        pieces[1], d_mixed = held(pieces[1], d_mixed)
        grads, token = weight_part(pieces[1], grads, [token])
    d_mixed_x, token = together(swap_x(d_mixed), token)
    d_hidden, gmt, d_att = mix_backward(
        sc, (d_mixed, d_mixed_x, swap_core(d_mixed), swap_core(d_mixed_x)), weights, att, heads
    )

    d_att, y_back = lax.optimization_barrier((d_att, y_back))
    table, keep_n, send_n, gain_one_sum, *grad_w = attention_backward(
        sc, d_att, probs, q, k, v, normed, gmt, weights, toks, groups
    )

    grad_w = grad_w[0].reshape(groups, -1, grad_w[0].shape[-1])

    def sum_dp(v):
        step = 1
        while step < groups:
            v = v + lax.ppermute(v, "dp", [(i, i ^ step) for i in range(groups)])
            step *= 2
        return v

    table = lax.dynamic_update_slice_in_dim(
        jnp.zeros(rel_table.shape, f32), table[:heads, : rel_table.shape[1]], tensor_index * heads, 0
    )
    small = jnp.concatenate(
        [gain_one_sum[0], table.reshape(-1), gain_two_sum[0], grad_router.reshape(-1)]
    )
    small = sum_dp(small.reshape(-1, 128))
    d_norm = keep_n + swap_core(send_n).astype(f32)
    norm_send = d_norm[1].astype(bf16)
    grad_w, small, norm_send, y_back = together(grad_w, small, norm_send, y_back)
    if len(pieces) > 2:
        pieces[-2], grad_w = held(pieces[-2], grad_w)
        grads, token = weight_part(pieces[-2], grads, [token])
    grad_w = exchange(grad_w)
    norm_recv = swap_x(norm_send)
    pieces[-1], norm_recv = held(pieces[-1], norm_recv)
    d_norm = d_norm[0] + norm_recv.astype(f32)
    t = tokens.astype(f32)
    r = lax.rsqrt(jnp.mean(t * t, axis=-1, keepdims=True) + 1e-06)
    gd = gain_one * d_norm
    hat = t * r
    grad_input = d_hidden.astype(f32) + r * (gd - hat * jnp.mean(gd * hat, axis=-1, keepdims=True))
    grad_w = jnp.sum(grad_w.astype(f32), axis=0)
    grad_qkv = jnp.stack([grad_w[:, j * head_width : (j + 1) * head_width] for j in range(3)])
    grad_mix = grad_w[:, 3 * head_width :].T

    small = small + swap_core(small)
    small_x = swap_x(small).reshape(-1)
    small = small.reshape(-1)
    cut = width + rel_table.size
    last = small[:cut] + small_x[:cut]
    grad_gain_one, grad_table = last[:width], last[width:].reshape(rel_table.shape)
    small, small_x = small[cut:], small_x[cut:]
    small = jnp.where(cx == 0, jnp.stack([small, small_x]), jnp.stack([small_x, small]))
    grad_gain_two = small[:, :half].reshape(width)
    grad_router = small[:, half:].reshape(width, EXPERTS)

    (g_in, g_out), _ = weight_part(pieces[-1], grads, [token])
    if virtual != local:
        hidden_units = w_in.shape[2]
        g_in = jnp.sum(g_in.reshape(local, virtual // local, width, hidden_units), axis=1)
        g_out = jnp.sum(g_out.reshape(local, virtual // local, hidden_units, width), axis=1)

    keep_y, send_y = unpack(
        whole_own, whole_other, gates_own, gates_other, 0, y_back, [], True
    )
    out = (hidden + keep_y + swap_core(send_y).astype(f32)).astype(bf16)
    out_recv = swap_x(out[block:])
    output = jnp.where(
        cx == 0,
        jnp.concatenate([out[:block], out_recv], 1),
        jnp.concatenate([out_recv, out[:block]], 1),
    )
    return (
        output,
        grad_input,
        grad_gain_one,
        grad_qkv,
        grad_table,
        grad_mix,
        grad_gain_two,
        grad_router,
        g_in,
        g_out,
    )


def solution(mesh):
    in_specs = (
        P(("dp", "tensor"), None),
        P(),
        P(None, "dp", "tensor"),
        P(),
        P("tensor", "dp"),
        P(),
        P(),
        P("dp", None, "tensor"),
        P("dp", "tensor", None),
        P("dp", None),
        P("dp", None),
        P("dp", None),
        P(("dp", "tensor"), None),
    )
    out_specs = (
        P(("dp", "tensor"), None),
        P(("dp", "tensor"), None),
        P(),
        P(None, "dp", "tensor"),
        P(),
        P("tensor", "dp"),
        P(),
        P(),
        P("dp", None, "tensor"),
        P("dp", "tensor", None),
    )
    return jax.shard_map(
        per_device, mesh=mesh, in_specs=in_specs, out_specs=out_specs, check_vma=False
    )
```
